32 devices in a mesh: groups: 2 (over y), ctx: 4 (over z), heads: 2 (over x), rep: 2 (over core).
Axes of the slice: x: 2, y: 2, z: 4, core: 2. Of those that a mesh axis runs over, the one named last changes fastest.
Arguments:
- queries: bfloat16 [24576, 32, 128], P(('groups', 'ctx'), ('heads', 'rep')), parts along dimension 0, may hold values from -14 to 14
- keys: bfloat16 [24576, 8, 128], P(('groups', 'ctx'), 'heads'), parts along dimension 0, may hold values from -14 to 14
- values: bfloat16 [24576, 8, 128], P(('groups', 'ctx'), 'heads'), parts along dimension 0, may hold values from -6 to 6
- chosen: int32 [8, 192, 8], P('heads', ('groups', 'ctx')), parts along dimension 1, may hold values from 0 to 95, as said below
Outputs:
- attended: bfloat16 [24576, 32, 128], P(('groups', 'ctx'), ('heads', 'rep')), parts along dimension 0
The draws below stay inside these ranges and needn't reach their ends.
There are 2 independent parts, one for each index of `groups`. The reference program is written for one: setup_inputs(seed, part) draws one part's arguments, and reference() takes and returns one part's arrays. A program takes and returns all parts, laid end to end along the dimension named above; each array names one. Nothing has to cross between parts.
Inputs may be any that keep to these rules, and one draw needn't show every extreme that they name: chosen[h, b, 0] = b. The other entries of a list are at most b and differ from each other, except that b itself may be repeated. For one key-value head, the 24 query blocks of one sequence shard list at most 2 distinct blocks of any other shard.
All inputs are finite; a program needn't handle non-finite values.
Results may differ from the reference program's by a relative error of at most 0.0046.
Values may be sent and summed in bfloat16 or wider, within the bound.
No kernel may reach another device: no remote copies, remote signals or barrier semaphores. Data moves between devices by JAX's collectives and lax.ppermute only.
A program may use at most 128 MiB of HBM per device.

```python
import jax
import jax.numpy as jnp
from jax import lax

QUERY_HEADS = 32
KEY_VALUE_HEADS = 8
HEAD_SIZE = 128
TOPK = 8
REMOTE_BLOCK_MAX = 2
QB_DEV = 24
CTX_SHARDS = 4
SEQUENCE_TOKENS = 12288


def pair_draw(key):
    pair_key = jax.random.fold_in(key, 7)
    key_seed_first, key_two = jax.random.split(pair_key, 2)
    key_pattern = jnp.clip(jax.random.normal(key_seed_first, (SEQUENCE_TOKENS, KEY_VALUE_HEADS, HEAD_SIZE), jnp.float32), -4.0, 4.0)
    query_field = jnp.clip(jax.random.normal(key_two, (SEQUENCE_TOKENS, QUERY_HEADS, HEAD_SIZE), jnp.float32), -4.0, 4.0)
    return (query_field, key_pattern)


def draw_queries(key, part):
    return pair_draw(key)[0].astype(jnp.bfloat16)


def draw_keys(key, part):
    return pair_draw(key)[1].astype(jnp.bfloat16)


def draw_chosen(key, part):
    shard_count = CTX_SHARDS
    blocks_per_shard = QB_DEV
    block_count = shard_count * blocks_per_shard
    leading_key, following_key = jax.random.split(jax.random.fold_in(key, 11))
    unscaled_scores = jax.random.randint(leading_key, (KEY_VALUE_HEADS, shard_count, shard_count, blocks_per_shard), 0, 1 << 20) * blocks_per_shard + jnp.arange(blocks_per_shard, dtype=jnp.int32)
    unused_score, selected_resident = lax.top_k(unscaled_scores, REMOTE_BLOCK_MAX)
    source_offset = (jnp.arange(shard_count, dtype=jnp.int32) * blocks_per_shard)[None, None, :, None]
    remote_blocks = (source_offset + selected_resident).reshape(KEY_VALUE_HEADS, shard_count, shard_count * REMOTE_BLOCK_MAX)
    block_numbers = jnp.arange(block_count, dtype=jnp.int32)
    device_of = block_numbers // blocks_per_shard
    within = block_numbers % blocks_per_shard
    remote_rows = jnp.repeat(remote_blocks, blocks_per_shard, axis=1)
    resident_rows = device_of[:, None] * blocks_per_shard + jnp.arange(blocks_per_shard, dtype=jnp.int32)[None, :]
    resident_rows = jnp.broadcast_to(resident_rows[None], (KEY_VALUE_HEADS, block_count, blocks_per_shard))
    candidates = jnp.concatenate([remote_rows, resident_rows], axis=-1)
    full_width = shard_count * REMOTE_BLOCK_MAX + blocks_per_shard
    slot_table = jnp.arange(full_width, dtype=jnp.int32)
    remote_valid = jnp.arange(shard_count * REMOTE_BLOCK_MAX, dtype=jnp.int32)[None, :] // REMOTE_BLOCK_MAX < device_of[:, None]
    local_valid = jnp.arange(blocks_per_shard, dtype=jnp.int32)[None, :] < within[:, None]
    valid = jnp.concatenate([remote_valid, local_valid], axis=-1)[None]
    full_scores = jax.random.randint(following_key, (KEY_VALUE_HEADS, block_count, full_width), 0, 1 << 20) * full_width + slot_table
    live_count = jnp.maximum(device_of * REMOTE_BLOCK_MAX, 1)[:, None]
    forced = jnp.zeros((block_count, full_width), dtype=bool)
    for turn in range(3):
        forced = forced | (slot_table[None, :] == (within[:, None] + turn * blocks_per_shard) % live_count)
    forced = forced & (device_of[:, None] >= 1)
    full_scores = jnp.where(forced[None], (1 << 20) * full_width + full_width + slot_table, full_scores)
    full_scores = jnp.where(valid, full_scores, -1 - slot_table)
    best_score, best_index = lax.top_k(full_scores, TOPK - 1)
    picked = jnp.take_along_axis(candidates, best_index, axis=-1)
    picked = jnp.where(best_score >= 0, picked, block_numbers[None, :, None])
    own_device = jnp.broadcast_to(block_numbers[None, :, None], (KEY_VALUE_HEADS, block_count, 1))
    return jnp.concatenate([own_device, picked], axis=-1).astype(jnp.int32)


def steps_of(own_key, extent, cuts, least, largest):
    gain = 1.0
    for position, parts in cuts:
        draws = jax.random.uniform(jax.random.fold_in(jax.random.fold_in(own_key, 6), position), (parts,), jnp.float32, least / len(cuts), largest / len(cuts))
        gain = gain * jnp.repeat(jnp.exp(draws), extent[position] // parts).reshape((-1,) + (1,) * (len(extent) - 1 - position))
    return gain


def centred(own_key, shape, deviation, reach, shards=(), kind=jnp.bfloat16):
    factor_of = steps_of(own_key, shape, shards, -0.22, 0.18) if shards else 1.0
    drawn = jax.random.normal(own_key, shape, jnp.float32) * deviation * factor_of
    return jnp.minimum(jnp.maximum(drawn, -reach), reach).astype(kind)


def setup_inputs(seed: int = 0, part: int = 0) -> dict:
    key_of = jax.random.split(jax.random.key(seed), 5)
    part_keys = jax.random.split(jax.random.fold_in(key_of[4], part), 5)
    return {
        "queries": draw_queries(jax.random.fold_in(jax.random.fold_in(key_of[4], part), 71), part),
        "keys": draw_keys(jax.random.fold_in(jax.random.fold_in(key_of[4], part), 71), part),
        "values": centred(part_keys[2], (SEQUENCE_TOKENS, KEY_VALUE_HEADS, HEAD_SIZE), 1.0, 6.0, ((0, 4), (1, 2))),
        "chosen": draw_chosen(jax.random.fold_in(jax.random.fold_in(key_of[4], part), 71), part),
    }


def attend(query_part, key_part, value_part, chosen_part):
    block_len = query_part.shape[1]
    head_dim = query_part.shape[-1]
    picks = chosen_part.shape[-1]
    scores = jnp.einsum("gqeah,egkh->egaqk", query_part.astype(jnp.float32), key_part.astype(jnp.float32)) * (head_dim ** -0.5)
    earlier = chosen_part[..., :, None] == chosen_part[..., None, :]
    before_slot = jnp.arange(picks)[:, None] > jnp.arange(picks)[None, :]
    repeated = jnp.any(earlier & before_slot[None, None], axis=-1)
    slot_open = jnp.repeat(jnp.logical_not(repeated), block_len, axis=-1)
    key_slot = jnp.arange(picks * block_len) // block_len
    key_place = jnp.arange(picks * block_len) % block_len
    query_place = jnp.arange(block_len)
    causal = (key_slot[None, :] > 0) | (key_place[None, :] <= query_place[:, None])
    visible = slot_open[:, :, None, None, :] & causal[None, None, None]
    highest = jnp.max(jnp.where(visible, scores, -jnp.inf), axis=-1, keepdims=True)
    weights = jnp.where(visible, jnp.exp(scores - highest), jnp.float32(0.0))
    totals = jnp.sum(weights, axis=-1)
    probabilities = lax.optimization_barrier(weights.astype(jnp.bfloat16)).astype(jnp.float32)
    attended = jnp.einsum("egaqk,egkh->gqeah", probabilities, value_part.astype(jnp.float32))
    scaled = attended / jnp.transpose(totals, (1, 3, 0, 2))[..., None]
    return scaled.astype(jnp.bfloat16)


def reference(queries, keys, values, chosen):
    tokens_all, query_heads, head_dim = queries.shape
    kv_heads = keys.shape[1]
    blocks = chosen.shape[1]
    picks = chosen.shape[2]
    block_len = tokens_all // blocks
    heads_per_group = query_heads // kv_heads
    group_size = 4

    def one_head(head_number):
        query_head = lax.dynamic_slice_in_dim(queries, head_number * heads_per_group, heads_per_group, 1)
        key_blocks = lax.dynamic_slice_in_dim(keys, head_number, 1, 1).reshape(blocks, block_len, head_dim)
        value_blocks = lax.dynamic_slice_in_dim(values, head_number, 1, 1).reshape(blocks, block_len, head_dim)
        chosen_head = lax.dynamic_index_in_dim(chosen, head_number, 0, keepdims=False)
        query_groups = query_head.reshape(blocks // group_size, group_size, block_len, 1, heads_per_group, head_dim)
        chosen_groups = chosen_head.reshape(blocks // group_size, group_size, picks)

        def block_group(operands):
            query_part, chosen_part = operands
            key_part = key_blocks[chosen_part].reshape(1, group_size, picks * block_len, head_dim)
            value_part = value_blocks[chosen_part].reshape(1, group_size, picks * block_len, head_dim)
            return attend(query_part, key_part, value_part, chosen_part[None])

        result = lax.map(block_group, (query_groups, chosen_groups))
        return result.reshape(tokens_all, heads_per_group, head_dim)

    stacked = lax.map(one_head, jnp.arange(kv_heads, dtype=jnp.int32))
    return jnp.transpose(stacked, (1, 0, 2, 3)).reshape(tokens_all, query_heads, head_dim)
```

```python
import functools

import jax
import jax.numpy as jnp
from jax import lax
from jax.experimental import pallas as pl
from jax.experimental.pallas import tpu as pltpu
from jax.sharding import PartitionSpec as P

QUERY_HEADS = 32
KEY_VALUE_HEADS = 8
REMOTE_BLOCK_MAX = 2
GROUP = QUERY_HEADS // KEY_VALUE_HEADS
LOG2E = 1.4426950408889634
MASKED = -1e30
CLOSED = 3e38
SAFE_TOTAL = 2.0**100


def block_rows(index, block_len):
    return pl.ds(pl.multiple_of(index * block_len, block_len), block_len)


def relayout_kernel(
    first_ref, keys_ref, values_ref, keys_out, values_out, keys_wide, values_wide,
    *, step_blocks, kv_heads, used, block_len,
):
    first = first_ref[0]
    keys_wide[...] = keys_ref[...].astype(jnp.float32)
    values_wide[...] = values_ref[...].astype(jnp.float32)
    for block in range(step_blocks):
        rows = slice(block * block_len, (block + 1) * block_len)
        for head in range(used):
            picked = pl.ds(block * block_len * kv_heads + first + head, block_len, stride=kv_heads)
            keys_out[head, rows, :] = keys_wide[picked, :].astype(jnp.bfloat16)
            values_out[head, rows, :] = values_wide[picked, :].T.astype(jnp.bfloat16)


def relayout(first, keys, values, used, block_len, step_blocks):
    tokens, kv_heads, head_dim = keys.shape
    rows = step_blocks * block_len
    taken = pl.BlockSpec((rows * kv_heads, head_dim), lambda g, *_: (g, 0))
    given = pl.BlockSpec((used, rows, head_dim), lambda g, *_: (0, g, 0))
    table = jax.ShapeDtypeStruct((used, tokens, head_dim), jnp.bfloat16)
    return pl.pallas_call(
        functools.partial(
            relayout_kernel, step_blocks=step_blocks, kv_heads=kv_heads, used=used,
            block_len=block_len,
        ),
        grid_spec=pltpu.PrefetchScalarGridSpec(
            num_scalar_prefetch=1,
            grid=(tokens // rows,),
            in_specs=[taken, taken],
            out_specs=[given, given],
            scratch_shapes=[pltpu.VMEM((rows * kv_heads, head_dim), jnp.float32)] * 2,
        ),
        out_shape=[table, table],
        compiler_params=pltpu.CompilerParams(vmem_limit_bytes=32 * 2**20),
        name="relayout",
    )(
        first,
        keys.reshape(tokens * kv_heads, head_dim),
        values.reshape(tokens * kv_heads, head_dim),
    )


def pack_kernel(request, keys_ref, values_ref, *rest, shifts, used, block_len):
    outs, (clear_ref, sems) = rest[:shifts], rest[shifts:]
    clear_ref[...] = jnp.zeros_like(clear_ref)
    copies = []
    for shift in range(shifts):
        for head in range(used):
            for turn in range(REMOTE_BLOCK_MAX):
                at = (shift * used + head) * REMOTE_BLOCK_MAX + turn
                source = block_rows(request[at], block_len)
                target = pl.ds(turn * block_len, block_len)
                for kind, table in enumerate((keys_ref, values_ref)):
                    copies.append(
                        pltpu.make_async_copy(
                            table.at[head, source],
                            outs[shift].at[kind, head, target],
                            sems.at[2 * at + kind],
                        )
                    )
    for copy in copies:
        copy.start()
    for copy in copies:
        copy.wait()


def pack(request, key_table, value_table, shifts, block_len, row_shape):
    used, _, head_dim = key_table.shape
    anywhere = pl.BlockSpec(memory_space=pl.ANY)
    parcel = jax.ShapeDtypeStruct(
        (2, used, REMOTE_BLOCK_MAX * block_len, head_dim), jnp.bfloat16
    )
    return pl.pallas_call(
        functools.partial(pack_kernel, shifts=shifts, used=used, block_len=block_len),
        grid_spec=pltpu.PrefetchScalarGridSpec(
            num_scalar_prefetch=1,
            grid=(1,),
            in_specs=[anywhere, anywhere],
            out_specs=[anywhere] * shifts + [pl.BlockSpec(row_shape, lambda g, *_: (0, 0))],
            scratch_shapes=[pltpu.SemaphoreType.DMA((2 * shifts * used * REMOTE_BLOCK_MAX,))],
        ),
        out_shape=[parcel] * shifts + [jax.ShapeDtypeStruct(row_shape, jnp.float32)],
        name="pack",
    )(request, key_table, value_table)


def split_heads(rows, used):
    count, head_dim = rows.shape
    if used == 1:
        return (rows,)
    wide = rows.astype(jnp.float32).reshape(count // 16, 2, 8, head_dim)
    even, odd = wide[:, 0], wide[:, 1]
    upper = lax.broadcasted_iota(jnp.int32, even.shape, 1) < GROUP
    first = jnp.where(upper, even, pltpu.roll(odd, GROUP, 1))
    second = jnp.where(upper, pltpu.roll(even, GROUP, 1), odd)
    return tuple(x.reshape(count // 2, head_dim).astype(jnp.bfloat16) for x in (first, second))


def join_heads(first, *others):
    count, head_dim = first.shape
    if not others:
        return first.astype(jnp.bfloat16)
    (second,) = others
    first = first.reshape(count // 8, 8, head_dim)
    second = second.reshape(count // 8, 8, head_dim)
    upper = lax.broadcasted_iota(jnp.int32, first.shape, 1) < GROUP
    even = jnp.where(upper, first, pltpu.roll(second, GROUP, 1))
    odd = jnp.where(upper, pltpu.roll(first, GROUP, 1), second)
    return jnp.stack([even, odd], axis=1).reshape(count * 2, head_dim).astype(jnp.bfloat16)


def score(key_rows, query):
    return lax.dot_general(
        key_rows, query, (((1,), (1,)), ((), ())), preferred_element_type=jnp.float32
    )


def causal(scores):
    key = lax.broadcasted_iota(jnp.int32, scores.shape, 0)
    per_head = scores.shape[1] // scores.shape[0]
    token = lax.broadcasted_iota(jnp.int32, scores.shape, 1) // per_head
    return jnp.where(key <= token, scores, MASKED)


def fold(weights):
    return jnp.sum(weights.reshape(weights.shape[0] // 8, 8, weights.shape[1]), axis=0)


def weigh(scores, highest, slots, scale, block_len):
    parts = []
    for turn, slot in enumerate(slots):
        shift = jnp.where(slot < 0, CLOSED, highest)
        parts.append(
            jnp.exp2(scores[turn * block_len : (turn + 1) * block_len] * scale - shift)
        )
    return jnp.concatenate(parts, axis=0)


def local_kernel(
    slots_ref, counts_ref, queries_ref, keys_ref, values_ref, clear_ref,
    sums_ref, totals_ref, highest_ref, bad_ref,
    *, step_blocks, used, picks, block_len, scale,
):
    step = pl.program_id(0)

    def gather(ref, head, slots, axis):
        return jnp.concatenate(
            [ref[head, block_rows(jnp.maximum(s, 0), block_len), :] for s in slots], axis=axis
        )

    def query_rows(block):
        rows = queries_ref.shape[0] // step_blocks
        return queries_ref[pl.ds(pl.multiple_of(block * rows, rows), rows), :]

    def attend(block, count):
        for head, query in enumerate(split_heads(query_rows(block), used)):
            item = block * used + head
            at = ((step * step_blocks + block) * used + head) * picks
            slots = [slots_ref[at + turn] for turn in range(count)]
            scores = score(gather(keys_ref, head, slots, 0), query)
            own = causal(scores[:block_len])
            highest = jnp.max(own, axis=0, keepdims=True) * scale
            scores = jnp.concatenate([own, scores[block_len:]], axis=0) if count > 1 else own
            weights = weigh(scores, highest, slots, scale, block_len)
            totals = fold(weights)
            highest_ref[item] = jnp.broadcast_to(highest, totals.shape)
            totals_ref[item] = totals
            bad_ref[...] = jnp.maximum(bad_ref[...], jnp.where(totals < SAFE_TOTAL, 0.0, 1.0))
            sums_ref[item] = jnp.dot(
                gather(values_ref, head, slots, 1),
                weights.astype(jnp.bfloat16),
                preferred_element_type=jnp.float32,
            )

    def one_block(block, carry):
        count = counts_ref[step * step_blocks + block]
        lax.switch(
            count - 1, [functools.partial(attend, block, n) for n in range(1, picks + 1)]
        )
        return carry

    def mend(block, carry):
        for head, query in enumerate(split_heads(query_rows(block), used)):
            item = block * used + head
            at = ((step * step_blocks + block) * used + head) * picks

            def slot_scores(turn, query=query, head=head, at=at):
                slot = slots_ref[at + turn]
                scores = score(gather(keys_ref, head, [slot], 0), query)
                return slot, jnp.where(turn == 0, causal(scores), scores)

            def raise_highest(turn, highest, slot_scores=slot_scores):
                slot, scores = slot_scores(turn)
                found = jnp.max(scores, axis=0, keepdims=True) * scale
                return jnp.where(slot < 0, highest, jnp.maximum(highest, found))

            highest = lax.fori_loop(
                0, picks, raise_highest, jnp.full((1, query.shape[0]), MASKED, jnp.float32)
            )
            highest_ref[item] = jnp.broadcast_to(highest, highest_ref.shape[1:])
            totals_ref[item] = jnp.zeros(totals_ref.shape[1:], jnp.float32)
            sums_ref[item] = jnp.zeros(sums_ref.shape[1:], jnp.float32)

            def add(turn, carry, slot_scores=slot_scores, item=item, head=head):
                slot, scores = slot_scores(turn)
                weights = weigh(scores, highest_ref[item][:1], [slot], scale, block_len)
                totals_ref[item] += fold(weights)
                sums_ref[item] += jnp.dot(
                    gather(values_ref, head, [slot], 1),
                    weights.astype(jnp.bfloat16),
                    preferred_element_type=jnp.float32,
                )
                return carry

            lax.fori_loop(0, picks, add, 0)
        return carry

    bad_ref[...] = clear_ref[...]
    lax.fori_loop(0, step_blocks, one_block, 0)

    @pl.when(jnp.max(bad_ref[...]) > 0.0)
    def _():
        lax.fori_loop(0, step_blocks, mend, 0)


def remote_kernel(
    slots_ref, counts_ref, queries_ref, sums_ref, totals_ref, highest_ref, *rest,
    shifts, step_blocks, used, picks, block_len, scale,
):
    parcels, (out_ref, keys_ref, values_ref, bad_ref, sems) = rest[:shifts], rest[shifts:]
    step = pl.program_id(0)
    parcel_rows = REMOTE_BLOCK_MAX * block_len

    @pl.when(step == 0)
    def _():
        copies = []
        for shift in range(shifts):
            place = pl.ds(shift * parcel_rows, parcel_rows)
            for head in range(used):
                for kind, table in enumerate((keys_ref, values_ref)):
                    copies.append(
                        pltpu.make_async_copy(
                            parcels[shift].at[kind, head],
                            table.at[head, place],
                            sems.at[(shift * used + head) * 2 + kind],
                        )
                    )
        for copy in copies:
            copy.start()
        for copy in copies:
            copy.wait()

    def gather(ref, head, slots, axis):
        return jnp.concatenate(
            [ref[head, block_rows(jnp.maximum(s, 0), block_len), :] for s in slots], axis=axis
        )

    def block_rows_of(block):
        rows = queries_ref.shape[0] // step_blocks
        return pl.ds(pl.multiple_of(block * rows, rows), rows)

    def finish(block, shares):
        parts = []
        for sums, totals in shares:
            parts.append((sums * (1.0 / jnp.sum(totals, axis=0, keepdims=True))).T)
        out_ref[block_rows_of(block), :] = join_heads(*parts)

    def attend(block, count):
        shares = []
        for head, query in enumerate(split_heads(queries_ref[block_rows_of(block), :], used)):
            item = block * used + head
            sums, totals = sums_ref[item], totals_ref[item]
            if count:
                at = ((step * step_blocks + block) * used + head) * picks
                slots = [slots_ref[at + turn] for turn in range(count)]
                scores = score(gather(keys_ref, head, slots, 0), query)
                weights = weigh(scores, highest_ref[item][:1], slots, scale, block_len)
                totals = totals + fold(weights)
                bad_ref[...] = jnp.maximum(
                    bad_ref[...], jnp.where(totals < 2 * SAFE_TOTAL, 0.0, 1.0)
                )
                sums = sums + jnp.dot(
                    gather(values_ref, head, slots, 1),
                    weights.astype(jnp.bfloat16),
                    preferred_element_type=jnp.float32,
                )
            shares.append((sums, totals))
        finish(block, shares)

    def one_block(block, carry):
        count = counts_ref[step * step_blocks + block]
        lax.switch(count, [functools.partial(attend, block, n) for n in range(picks)])
        return carry

    def mend(block, carry):
        shares = []
        for head, query in enumerate(split_heads(queries_ref[block_rows_of(block), :], used)):
            item = block * used + head
            at = ((step * step_blocks + block) * used + head) * picks
            before = highest_ref[item][:1]

            def slot_scores(turn, query=query, head=head, at=at):
                slot = slots_ref[at + turn]
                return slot, score(gather(keys_ref, head, [slot], 0), query)

            def raise_highest(turn, highest, slot_scores=slot_scores):
                slot, scores = slot_scores(turn)
                found = jnp.max(scores, axis=0, keepdims=True) * scale
                return jnp.where(slot < 0, highest, jnp.maximum(highest, found))

            highest = lax.fori_loop(0, picks - 1, raise_highest, before)
            shrink = jnp.exp2(before - highest)

            def add(turn, carry, slot_scores=slot_scores, head=head, highest=highest):
                sums, totals = carry
                slot, scores = slot_scores(turn)
                weights = weigh(scores, highest, [slot], scale, block_len)
                sums = sums + jnp.dot(
                    gather(values_ref, head, [slot], 1),
                    weights.astype(jnp.bfloat16),
                    preferred_element_type=jnp.float32,
                )
                return sums, totals + fold(weights)

            shares.append(
                lax.fori_loop(
                    0, picks - 1, add, (sums_ref[item] * shrink, totals_ref[item] * shrink)
                )
            )
        finish(block, shares)
        return carry

    bad_ref[...] = jnp.zeros_like(bad_ref)
    lax.fori_loop(0, step_blocks, one_block, 0)

    @pl.when(jnp.max(bad_ref[...]) > 0.0)
    def _():
        lax.fori_loop(0, step_blocks, mend, 0)


def compact(open_slot, index):
    picks = index.shape[-1]
    before = jnp.arange(picks)[:, None] < jnp.arange(picks)[None, :]
    place = jnp.sum(open_slot[..., :, None] & before, axis=-2)
    here = open_slot[..., :, None] & (place[..., :, None] == jnp.arange(picks))
    packed = jnp.sum(jnp.where(here, index[..., :, None] + 1, 0), axis=-2) - 1
    return packed, jnp.sum(open_slot, axis=-1)


def on_device(queries, keys, values, chosen):
    tokens, query_heads, head_dim = queries.shape
    blocks, picks = chosen.shape[1:]
    block_len = tokens // blocks
    used = max(1, query_heads // GROUP)
    per_head = query_heads // used
    shards = lax.axis_size("ctx")
    shifts = shards - 1
    position = lax.axis_index("ctx")
    base = position * blocks
    first = lax.axis_index("rep") * query_heads // GROUP
    scale = LOG2E * head_dim**-0.5
    step_blocks = next(n for n in (6, 4, 3, 2, 1) if blocks % n == 0)
    steps = blocks // step_blocks
    item_rows = per_head * block_len

    lists = lax.dynamic_slice_in_dim(chosen, first, used, 0)
    wanted = jnp.stack(
        [
            lax.ppermute(lists, "ctx", [(j, j - d) for j in range(d, shards)])
            for d in range(1, shards)
        ]
    )
    key_table, value_table = relayout(
        first.reshape(1), keys, values, used, block_len, step_blocks
    )
    within = wanted - base
    mine = (within >= 0) & (within < blocks)
    request = jnp.stack(
        [
            jnp.min(jnp.where(mine, within, blocks - 1), axis=(2, 3)),
            jnp.max(jnp.where(mine, within, 0), axis=(2, 3)),
        ],
        axis=-1,
    )
    *parcels, clear = pack(
        request.reshape(-1), key_table, value_table, shifts, block_len, (8, item_rows)
    )
    arrived = [
        lax.ppermute(parcel, "ctx", [(i, i + d) for i in range(shards - d)])
        for d, parcel in zip(range(1, shards), parcels)
    ]

    local = lists >= base
    repeated = (lists == (base + jnp.arange(blocks))[None, :, None]) & (jnp.arange(picks) > 0)
    local_slots, local_count = compact(local & ~repeated, lists - base)
    shard_of = lists // blocks
    from_shard = shard_of[..., None] == jnp.arange(shards)
    lowest = jnp.min(
        jnp.where(from_shard, lists[..., None], shards * blocks), axis=(1, 2), keepdims=True
    )
    is_lowest = jnp.any(from_shard & (lists[..., None] == lowest), axis=-1)
    remote_index = (position - 1 - shard_of) * REMOTE_BLOCK_MAX + jnp.where(is_lowest, 0, 1)
    remote_slots, remote_count = compact(~local, remote_index)

    def table(slots):
        return jnp.transpose(slots, (1, 0, 2)).reshape(-1)

    query_spec = pl.BlockSpec(
        (step_blocks * block_len * query_heads, head_dim), lambda g, *_: (g, 0)
    )
    table_spec = pl.BlockSpec(key_table.shape, lambda g, *_: (0, 0, 0))
    sums_spec = pl.BlockSpec((step_blocks * used, head_dim, item_rows), lambda g, *_: (g, 0, 0))
    row_spec = pl.BlockSpec((step_blocks * used, 8, item_rows), lambda g, *_: (g, 0, 0))
    sums_shape = jax.ShapeDtypeStruct((blocks * used, head_dim, item_rows), jnp.float32)
    row_shape = jax.ShapeDtypeStruct((blocks * used, 8, item_rows), jnp.float32)
    sizes = dict(
        step_blocks=step_blocks, used=used, picks=picks, block_len=block_len, scale=scale
    )
    query_rows = queries.reshape(tokens * query_heads, head_dim)
    sums, totals, highest = pl.pallas_call(
        functools.partial(local_kernel, **sizes),
        grid_spec=pltpu.PrefetchScalarGridSpec(
            num_scalar_prefetch=2,
            grid=(steps,),
            in_specs=[
                query_spec, table_spec, table_spec,
                pl.BlockSpec(clear.shape, lambda g, *_: (0, 0)),
            ],
            out_specs=[sums_spec, row_spec, row_spec],
            scratch_shapes=[pltpu.VMEM((8, item_rows), jnp.float32)],
        ),
        out_shape=[sums_shape, row_shape, row_shape],
        compiler_params=pltpu.CompilerParams(vmem_limit_bytes=40 * 2**20),
        cost_estimate=pl.CostEstimate(
            flops=3 * tokens * query_heads * picks * block_len * head_dim,
            bytes_accessed=32 * 2**20,
            transcendentals=tokens * query_heads * picks * block_len,
        ),
        name="local_part",
    )(
        table(local_slots), jnp.max(local_count, axis=0), query_rows, key_table, value_table,
        clear,
    )

    remote_rows = shifts * REMOTE_BLOCK_MAX * block_len
    out = pl.pallas_call(
        functools.partial(remote_kernel, shifts=shifts, **sizes),
        grid_spec=pltpu.PrefetchScalarGridSpec(
            num_scalar_prefetch=2,
            grid=(steps,),
            in_specs=[query_spec, sums_spec, row_spec, row_spec]
            + [pl.BlockSpec(memory_space=pl.ANY)] * shifts,
            out_specs=query_spec,
            scratch_shapes=[
                pltpu.VMEM((used, remote_rows, head_dim), jnp.bfloat16),
                pltpu.VMEM((used, remote_rows, head_dim), jnp.bfloat16),
                pltpu.VMEM((8, item_rows), jnp.float32),
                pltpu.SemaphoreType.DMA((2 * used * shifts,)),
            ],
        ),
        out_shape=jax.ShapeDtypeStruct(query_rows.shape, jnp.bfloat16),
        compiler_params=pltpu.CompilerParams(vmem_limit_bytes=40 * 2**20),
        name="remote_part",
    )(
        table(remote_slots), jnp.max(remote_count, axis=0), query_rows,
        sums, totals, highest, *arrived,
    )
    return out.reshape(tokens, query_heads, head_dim)


def solution(mesh):
    return jax.shard_map(
        on_device,
        mesh=mesh,
        in_specs=(
            P(("groups", "ctx"), ("heads", "rep"), None),
            P(("groups", "ctx"), "heads", None),
            P(("groups", "ctx"), "heads", None),
            P("heads", ("groups", "ctx"), None),
        ),
        out_specs=P(("groups", "ctx"), ("heads", "rep"), None),
        check_vma=False,
    )
```

```python
import functools

import jax
import jax.numpy as jnp
from jax import lax
from jax.experimental import pallas as pl
from jax.experimental.pallas import tpu as pltpu
from jax.sharding import PartitionSpec as P

QUERY_HEADS = 32
KEY_VALUE_HEADS = 8
REMOTE_BLOCK_MAX = 2
GROUP = QUERY_HEADS // KEY_VALUE_HEADS
LOG2E = 1.4426950408889634
MASKED = -1e30
CLOSED = 3e38
SAFE_TOTAL = 2.0**100
VMEM_BYTES = 60 * 2**20


def block_rows(index, block_len):
    return pl.ds(pl.multiple_of(index * block_len, block_len), block_len)


def relayout_kernel(
    first_ref, keys_ref, values_ref, keys_out, values_out, keys_wide, values_wide,
    *, step_blocks, kv_heads, used, block_len,
):
    first = first_ref[0]
    keys_wide[...] = keys_ref[...].astype(jnp.float32)
    values_wide[...] = values_ref[...].astype(jnp.float32)
    for block in range(step_blocks):
        rows = slice(block * block_len, (block + 1) * block_len)
        for head in range(used):
            picked = pl.ds(block * block_len * kv_heads + first + head, block_len, stride=kv_heads)
            keys_out[head, rows, :] = keys_wide[picked, :].astype(jnp.bfloat16)
            values_out[head, rows, :] = values_wide[picked, :].T.astype(jnp.bfloat16)


def relayout(first, keys, values, used, block_len, step_blocks):
    tokens, kv_heads, head_dim = keys.shape
    rows = step_blocks * block_len
    taken = pl.BlockSpec((rows * kv_heads, head_dim), lambda g, *_: (g, 0))
    given = pl.BlockSpec((used, rows, head_dim), lambda g, *_: (0, g, 0))
    table = jax.ShapeDtypeStruct((used, tokens, head_dim), jnp.bfloat16)
    return pl.pallas_call(
        functools.partial(
            relayout_kernel, step_blocks=step_blocks, kv_heads=kv_heads, used=used,
            block_len=block_len,
        ),
        grid_spec=pltpu.PrefetchScalarGridSpec(
            num_scalar_prefetch=1,
            grid=(tokens // rows,),
            in_specs=[taken, taken],
            out_specs=[given, given],
            scratch_shapes=[pltpu.VMEM((rows * kv_heads, head_dim), jnp.float32)] * 2,
        ),
        out_shape=[table, table],
        compiler_params=pltpu.CompilerParams(vmem_limit_bytes=VMEM_BYTES),
        name="relayout",
    )(
        first,
        keys.reshape(tokens * kv_heads, head_dim),
        values.reshape(tokens * kv_heads, head_dim),
    )


def pack_kernel(request, keys_ref, values_ref, *outs, used, block_len):
    *outs, clear_ref = outs
    clear_ref[...] = jnp.zeros_like(clear_ref)
    for shift, out in enumerate(outs):
        for head in range(used):
            for turn in range(REMOTE_BLOCK_MAX):
                at = (shift * used + head) * REMOTE_BLOCK_MAX + turn
                source = block_rows(request[at], block_len)
                target = slice(turn * block_len, (turn + 1) * block_len)
                out[0, head, target, :] = keys_ref[head, source, :]
                out[1, head, target, :] = values_ref[head, source, :]


def pack(request, key_table, value_table, shifts, block_len, row_shape):
    used, _, head_dim = key_table.shape
    parcel = (2, used, REMOTE_BLOCK_MAX * block_len, head_dim)
    whole = pl.BlockSpec(key_table.shape, lambda g, *_: (0, 0, 0))
    return pl.pallas_call(
        functools.partial(pack_kernel, used=used, block_len=block_len),
        grid_spec=pltpu.PrefetchScalarGridSpec(
            num_scalar_prefetch=1,
            grid=(1,),
            in_specs=[whole, whole],
            out_specs=[pl.BlockSpec(parcel, lambda g, *_: (0, 0, 0, 0))] * shifts
            + [pl.BlockSpec(row_shape, lambda g, *_: (0, 0))],
        ),
        out_shape=[jax.ShapeDtypeStruct(parcel, jnp.bfloat16)] * shifts
        + [jax.ShapeDtypeStruct(row_shape, jnp.float32)],
        compiler_params=pltpu.CompilerParams(vmem_limit_bytes=VMEM_BYTES),
        name="pack",
    )(request, key_table, value_table)


def split_heads(rows, used):
    count, head_dim = rows.shape
    if used == 1:
        return (rows,)
    wide = rows.astype(jnp.float32).reshape(count // 16, 2, 8, head_dim)
    even, odd = wide[:, 0], wide[:, 1]
    upper = lax.broadcasted_iota(jnp.int32, even.shape, 1) < GROUP
    first = jnp.where(upper, even, pltpu.roll(odd, GROUP, 1))
    second = jnp.where(upper, pltpu.roll(even, GROUP, 1), odd)
    return tuple(x.reshape(count // 2, head_dim).astype(jnp.bfloat16) for x in (first, second))


def join_heads(first, *others):
    count, head_dim = first.shape
    if not others:
        return first.astype(jnp.bfloat16)
    (second,) = others
    first = first.reshape(count // 8, 8, head_dim)
    second = second.reshape(count // 8, 8, head_dim)
    upper = lax.broadcasted_iota(jnp.int32, first.shape, 1) < GROUP
    even = jnp.where(upper, first, pltpu.roll(second, GROUP, 1))
    odd = jnp.where(upper, pltpu.roll(first, GROUP, 1), second)
    return jnp.stack([even, odd], axis=1).reshape(count * 2, head_dim).astype(jnp.bfloat16)


def score(key_rows, query):
    return lax.dot_general(
        key_rows, query, (((1,), (1,)), ((), ())), preferred_element_type=jnp.float32
    )


def causal(scores):
    key = lax.broadcasted_iota(jnp.int32, scores.shape, 0)
    per_head = scores.shape[1] // scores.shape[0]
    token = lax.broadcasted_iota(jnp.int32, scores.shape, 1) // per_head
    return jnp.where(key <= token, scores, MASKED)


def fold(weights):
    return jnp.sum(weights.reshape(weights.shape[0] // 8, 8, weights.shape[1]), axis=0)


def weigh(scores, highest, slots, scale, block_len):
    parts = []
    for turn, slot in enumerate(slots):
        shift = jnp.where(slot < 0, CLOSED, highest)
        parts.append(
            jnp.exp2(scores[turn * block_len : (turn + 1) * block_len] * scale - shift)
        )
    return jnp.concatenate(parts, axis=0)


def local_kernel(
    slots_ref, counts_ref, queries_ref, keys_ref, values_ref, clear_ref,
    sums_ref, totals_ref, highest_ref, bad_ref,
    *, step_blocks, used, picks, block_len, scale,
):
    step = pl.program_id(0)

    def gather(ref, head, slots, axis):
        return jnp.concatenate(
            [ref[head, block_rows(jnp.maximum(s, 0), block_len), :] for s in slots], axis=axis
        )

    def query_rows(block):
        rows = queries_ref.shape[0] // step_blocks
        return queries_ref[pl.ds(pl.multiple_of(block * rows, rows), rows), :]

    def attend(block, count):
        for head, query in enumerate(split_heads(query_rows(block), used)):
            item = block * used + head
            at = ((step * step_blocks + block) * used + head) * picks
            slots = [slots_ref[at + turn] for turn in range(count)]
            scores = score(gather(keys_ref, head, slots, 0), query)
            own = causal(scores[:block_len])
            highest = jnp.max(own, axis=0, keepdims=True) * scale
            scores = jnp.concatenate([own, scores[block_len:]], axis=0) if count > 1 else own
            weights = weigh(scores, highest, slots, scale, block_len)
            totals = fold(weights)
            highest_ref[item] = jnp.broadcast_to(highest, totals.shape)
            totals_ref[item] = totals
            bad_ref[...] = jnp.maximum(bad_ref[...], jnp.where(totals < SAFE_TOTAL, 0.0, 1.0))
            sums_ref[item] = jnp.dot(
                gather(values_ref, head, slots, 1),
                weights.astype(jnp.bfloat16),
                preferred_element_type=jnp.float32,
            )

    def one_block(block, carry):
        count = counts_ref[step * step_blocks + block]
        lax.switch(
            count - 1, [functools.partial(attend, block, n) for n in range(1, picks + 1)]
        )
        return carry

    def mend(block, carry):
        for head, query in enumerate(split_heads(query_rows(block), used)):
            item = block * used + head
            at = ((step * step_blocks + block) * used + head) * picks

            def slot_scores(turn, query=query, head=head, at=at):
                slot = slots_ref[at + turn]
                scores = score(gather(keys_ref, head, [slot], 0), query)
                return slot, jnp.where(turn == 0, causal(scores), scores)

            def raise_highest(turn, highest, slot_scores=slot_scores):
                slot, scores = slot_scores(turn)
                found = jnp.max(scores, axis=0, keepdims=True) * scale
                return jnp.where(slot < 0, highest, jnp.maximum(highest, found))

            highest = lax.fori_loop(
                0, picks, raise_highest, jnp.full((1, query.shape[0]), MASKED, jnp.float32)
            )
            highest_ref[item] = jnp.broadcast_to(highest, highest_ref.shape[1:])
            totals_ref[item] = jnp.zeros(totals_ref.shape[1:], jnp.float32)
            sums_ref[item] = jnp.zeros(sums_ref.shape[1:], jnp.float32)

            def add(turn, carry, slot_scores=slot_scores, item=item, head=head):
                slot, scores = slot_scores(turn)
                weights = weigh(scores, highest_ref[item][:1], [slot], scale, block_len)
                totals_ref[item] += fold(weights)
                sums_ref[item] += jnp.dot(
                    gather(values_ref, head, [slot], 1),
                    weights.astype(jnp.bfloat16),
                    preferred_element_type=jnp.float32,
                )
                return carry

            lax.fori_loop(0, picks, add, 0)
        return carry

    bad_ref[...] = clear_ref[...]
    lax.fori_loop(0, step_blocks, one_block, 0)

    @pl.when(jnp.max(bad_ref[...]) > 0.0)
    def _():
        lax.fori_loop(0, step_blocks, mend, 0)


def remote_kernel(
    slots_ref, counts_ref, queries_ref, sums_ref, totals_ref, highest_ref, *rest,
    shifts, step_blocks, used, picks, block_len, scale,
):
    parcels, (out_ref, keys_ref, values_ref, bad_ref) = rest[:shifts], rest[shifts:]
    step = pl.program_id(0)
    parcel_rows = REMOTE_BLOCK_MAX * block_len

    @pl.when(step == 0)
    def _():
        for shift, parcel in enumerate(parcels):
            place = pl.ds(shift * parcel_rows, parcel_rows)
            keys_ref[:, place, :] = parcel[0]
            values_ref[:, place, :] = parcel[1]

    def gather(ref, head, slots, axis):
        return jnp.concatenate(
            [ref[head, block_rows(jnp.maximum(s, 0), block_len), :] for s in slots], axis=axis
        )

    def block_rows_of(block):
        rows = queries_ref.shape[0] // step_blocks
        return pl.ds(pl.multiple_of(block * rows, rows), rows)

    def finish(block, shares):
        parts = []
        for sums, totals in shares:
            parts.append((sums * (1.0 / jnp.sum(totals, axis=0, keepdims=True))).T)
        out_ref[block_rows_of(block), :] = join_heads(*parts)

    def attend(block, count):
        shares = []
        for head, query in enumerate(split_heads(queries_ref[block_rows_of(block), :], used)):
            item = block * used + head
            sums, totals = sums_ref[item], totals_ref[item]
            if count:
                at = ((step * step_blocks + block) * used + head) * picks
                slots = [slots_ref[at + turn] for turn in range(count)]
                scores = score(gather(keys_ref, head, slots, 0), query)
                weights = weigh(scores, highest_ref[item][:1], slots, scale, block_len)
                totals = totals + fold(weights)
                bad_ref[...] = jnp.maximum(
                    bad_ref[...], jnp.where(totals < 2 * SAFE_TOTAL, 0.0, 1.0)
                )
                sums = sums + jnp.dot(
                    gather(values_ref, head, slots, 1),
                    weights.astype(jnp.bfloat16),
                    preferred_element_type=jnp.float32,
                )
            shares.append((sums, totals))
        finish(block, shares)

    def one_block(block, carry):
        count = counts_ref[step * step_blocks + block]
        lax.switch(count, [functools.partial(attend, block, n) for n in range(picks)])
        return carry

    def mend(block, carry):
        shares = []
        for head, query in enumerate(split_heads(queries_ref[block_rows_of(block), :], used)):
            item = block * used + head
            at = ((step * step_blocks + block) * used + head) * picks
            before = highest_ref[item][:1]

            def slot_scores(turn, query=query, head=head, at=at):
                slot = slots_ref[at + turn]
                return slot, score(gather(keys_ref, head, [slot], 0), query)

            def raise_highest(turn, highest, slot_scores=slot_scores):
                slot, scores = slot_scores(turn)
                found = jnp.max(scores, axis=0, keepdims=True) * scale
                return jnp.where(slot < 0, highest, jnp.maximum(highest, found))

            highest = lax.fori_loop(0, picks - 1, raise_highest, before)
            shrink = jnp.exp2(before - highest)

            def add(turn, carry, slot_scores=slot_scores, head=head, highest=highest):
                sums, totals = carry
                slot, scores = slot_scores(turn)
                weights = weigh(scores, highest, [slot], scale, block_len)
                sums = sums + jnp.dot(
                    gather(values_ref, head, [slot], 1),
                    weights.astype(jnp.bfloat16),
                    preferred_element_type=jnp.float32,
                )
                return sums, totals + fold(weights)

            shares.append(
                lax.fori_loop(
                    0, picks - 1, add, (sums_ref[item] * shrink, totals_ref[item] * shrink)
                )
            )
        finish(block, shares)
        return carry

    bad_ref[...] = jnp.zeros_like(bad_ref)
    lax.fori_loop(0, step_blocks, one_block, 0)

    @pl.when(jnp.max(bad_ref[...]) > 0.0)
    def _():
        lax.fori_loop(0, step_blocks, mend, 0)


def compact(open_slot, index):
    picks = index.shape[-1]
    before = jnp.arange(picks)[:, None] < jnp.arange(picks)[None, :]
    place = jnp.sum(open_slot[..., :, None] & before, axis=-2)
    here = open_slot[..., :, None] & (place[..., :, None] == jnp.arange(picks))
    packed = jnp.sum(jnp.where(here, index[..., :, None] + 1, 0), axis=-2) - 1
    return packed, jnp.sum(open_slot, axis=-1)


def on_device(queries, keys, values, chosen):
    tokens, query_heads, head_dim = queries.shape
    blocks, picks = chosen.shape[1:]
    block_len = tokens // blocks
    used = max(1, query_heads // GROUP)
    per_head = query_heads // used
    shards = lax.axis_size("ctx")
    shifts = shards - 1
    position = lax.axis_index("ctx")
    base = position * blocks
    first = lax.axis_index("rep") * query_heads // GROUP
    scale = LOG2E * head_dim**-0.5
    step_blocks = next(n for n in (6, 4, 3, 2, 1) if blocks % n == 0)
    steps = blocks // step_blocks
    item_rows = per_head * block_len

    lists = lax.dynamic_slice_in_dim(chosen, first, used, 0)
    wanted = jnp.stack(
        [
            lax.ppermute(lists, "ctx", [(j, j - d) for j in range(d, shards)])
            for d in range(1, shards)
        ]
    )
    key_table, value_table = relayout(
        first.reshape(1), keys, values, used, block_len, step_blocks
    )
    within = wanted - base
    mine = (within >= 0) & (within < blocks)
    request = jnp.stack(
        [
            jnp.min(jnp.where(mine, within, blocks - 1), axis=(2, 3)),
            jnp.max(jnp.where(mine, within, 0), axis=(2, 3)),
        ],
        axis=-1,
    )
    *parcels, clear = pack(
        request.reshape(-1), key_table, value_table, shifts, block_len, (8, item_rows)
    )
    arrived = [
        lax.ppermute(parcel, "ctx", [(i, i + d) for i in range(shards - d)])
        for d, parcel in zip(range(1, shards), parcels)
    ]

    local = lists >= base
    repeated = (lists == (base + jnp.arange(blocks))[None, :, None]) & (jnp.arange(picks) > 0)
    local_slots, local_count = compact(local & ~repeated, lists - base)
    shard_of = lists // blocks
    from_shard = shard_of[..., None] == jnp.arange(shards)
    lowest = jnp.min(
        jnp.where(from_shard, lists[..., None], shards * blocks), axis=(1, 2), keepdims=True
    )
    is_lowest = jnp.any(from_shard & (lists[..., None] == lowest), axis=-1)
    remote_index = (position - 1 - shard_of) * REMOTE_BLOCK_MAX + jnp.where(is_lowest, 0, 1)
    remote_slots, remote_count = compact(~local, remote_index)

    def table(slots):
        return jnp.transpose(slots, (1, 0, 2)).reshape(-1)

    query_spec = pl.BlockSpec(
        (step_blocks * block_len * query_heads, head_dim), lambda g, *_: (g, 0)
    )
    table_spec = pl.BlockSpec(key_table.shape, lambda g, *_: (0, 0, 0))
    sums_spec = pl.BlockSpec((step_blocks * used, head_dim, item_rows), lambda g, *_: (g, 0, 0))
    row_spec = pl.BlockSpec((step_blocks * used, 8, item_rows), lambda g, *_: (g, 0, 0))
    sums_shape = jax.ShapeDtypeStruct((blocks * used, head_dim, item_rows), jnp.float32)
    row_shape = jax.ShapeDtypeStruct((blocks * used, 8, item_rows), jnp.float32)
    sizes = dict(
        step_blocks=step_blocks, used=used, picks=picks, block_len=block_len, scale=scale
    )
    query_rows = queries.reshape(tokens * query_heads, head_dim)
    sums, totals, highest = pl.pallas_call(
        functools.partial(local_kernel, **sizes),
        grid_spec=pltpu.PrefetchScalarGridSpec(
            num_scalar_prefetch=2,
            grid=(steps,),
            in_specs=[
                query_spec, table_spec, table_spec,
                pl.BlockSpec(clear.shape, lambda g, *_: (0, 0)),
            ],
            out_specs=[sums_spec, row_spec, row_spec],
            scratch_shapes=[pltpu.VMEM((8, item_rows), jnp.float32)],
        ),
        out_shape=[sums_shape, row_shape, row_shape],
        compiler_params=pltpu.CompilerParams(vmem_limit_bytes=VMEM_BYTES),
        cost_estimate=pl.CostEstimate(
            flops=3 * tokens * query_heads * picks * block_len * head_dim,
            bytes_accessed=32 * 2**20,
            transcendentals=tokens * query_heads * picks * block_len,
        ),
        name="local_part",
    )(
        table(local_slots), jnp.max(local_count, axis=0), query_rows, key_table, value_table,
        clear,
    )

    remote_rows = shifts * REMOTE_BLOCK_MAX * block_len
    out = pl.pallas_call(
        functools.partial(remote_kernel, shifts=shifts, **sizes),
        grid_spec=pltpu.PrefetchScalarGridSpec(
            num_scalar_prefetch=2,
            grid=(steps,),
            in_specs=[query_spec, sums_spec, row_spec, row_spec]
            + [pl.BlockSpec(arrived[0].shape, lambda g, *_: (0, 0, 0, 0))] * shifts,
            out_specs=query_spec,
            scratch_shapes=[
                pltpu.VMEM((used, remote_rows, head_dim), jnp.bfloat16),
                pltpu.VMEM((used, remote_rows, head_dim), jnp.bfloat16),
                pltpu.VMEM((8, item_rows), jnp.float32),
            ],
        ),
        out_shape=jax.ShapeDtypeStruct(query_rows.shape, jnp.bfloat16),
        compiler_params=pltpu.CompilerParams(vmem_limit_bytes=VMEM_BYTES),
        name="remote_part",
    )(
        table(remote_slots), jnp.max(remote_count, axis=0), query_rows,
        sums, totals, highest, *arrived,
    )
    return out.reshape(tokens, query_heads, head_dim)


def solution(mesh):
    return jax.shard_map(
        on_device,
        mesh=mesh,
        in_specs=(
            P(("groups", "ctx"), ("heads", "rep"), None),
            P(("groups", "ctx"), "heads", None),
            P(("groups", "ctx"), "heads", None),
            P("heads", ("groups", "ctx"), None),
        ),
        out_specs=P(("groups", "ctx"), ("heads", "rep"), None),
        check_vma=False,
    )
```

```python
import functools

import jax
import jax.numpy as jnp
from jax import lax
from jax.experimental import pallas as pl
from jax.experimental.pallas import tpu as pltpu
from jax.sharding import PartitionSpec as P

QUERY_HEADS = 32
KEY_VALUE_HEADS = 8
REMOTE_BLOCK_MAX = 2
GROUP = QUERY_HEADS // KEY_VALUE_HEADS
LOG2E = 1.4426950408889634
MASKED = -1e30
CLOSED = 3e38
SAFE_TOTAL = 2.0**100
VMEM_BYTES = 60 * 2**20
UNITS_AT_ONCE = 8
FIELD = 10


def block_rows(index, block_len):
    return pl.ds(pl.multiple_of(index * block_len, block_len), block_len)


def pack_kernel(
    request, keys_ref, values_ref, *rest, shifts, used, kv_heads, block_len
):
    first_ref, outs = rest[0], rest[1 : shifts + 1]
    clear_ref, blocks_ref, wide_ref, sems = rest[shifts + 1 :]
    rows = block_len * kv_heads
    clear_ref[...] = jnp.zeros_like(clear_ref)
    wanted = [
        (shift, head, turn)
        for shift in range(shifts)
        for head in range(used)
        for turn in range(REMOTE_BLOCK_MAX)
    ]
    copies = []
    for at in range(len(wanted)):
        for kind, table in enumerate((keys_ref, values_ref)):
            copies.append(
                pltpu.make_async_copy(
                    table.at[block_rows(request[at], rows)],
                    blocks_ref.at[2 * at + kind],
                    sems.at[2 * at + kind],
                )
            )
    for copy in copies:
        copy.start()
    for at, (shift, head, turn) in enumerate(wanted):
        target = slice(turn * block_len, (turn + 1) * block_len)
        picked = pl.ds(first_ref[0] + head, block_len, stride=kv_heads)
        for kind in range(2):
            place = 2 * at + kind
            copies[place].wait()
            wide_ref[place] = blocks_ref[place].astype(jnp.float32)
            block = wide_ref[place, picked, :]
            outs[shift][kind, head, target, :] = (block.T if kind else block).astype(jnp.bfloat16)


def pack(request, first, keys, values, kv_heads, shifts, used, block_len, row_shape):
    head_dim = keys.shape[-1]
    parcel = (2, used, REMOTE_BLOCK_MAX * block_len, head_dim)
    anywhere = pl.BlockSpec(memory_space=pl.ANY)
    count = 2 * shifts * used * REMOTE_BLOCK_MAX
    rows = block_len * kv_heads
    return pl.pallas_call(
        functools.partial(
            pack_kernel, shifts=shifts, used=used, kv_heads=kv_heads, block_len=block_len
        ),
        grid_spec=pltpu.PrefetchScalarGridSpec(
            num_scalar_prefetch=1,
            grid=(1,),
            in_specs=[anywhere, anywhere, pl.BlockSpec(memory_space=pltpu.SMEM)],
            out_specs=[pl.BlockSpec(parcel, lambda g, *_: (0, 0, 0, 0))] * shifts
            + [pl.BlockSpec(row_shape, lambda g, *_: (0, 0))],
            scratch_shapes=[
                pltpu.VMEM((count, rows, head_dim), jnp.bfloat16),
                pltpu.VMEM((count, rows, head_dim), jnp.float32),
                pltpu.SemaphoreType.DMA((count,)),
            ],
        ),
        out_shape=[jax.ShapeDtypeStruct(parcel, jnp.bfloat16)] * shifts
        + [jax.ShapeDtypeStruct(row_shape, jnp.float32)],
        compiler_params=pltpu.CompilerParams(vmem_limit_bytes=VMEM_BYTES),
        name="pack",
    )(request, keys, values, first)


def split_heads(rows, used):
    count, head_dim = rows.shape
    if used == 1:
        return (rows,)
    wide = rows.astype(jnp.float32).reshape(count // 16, 2, 8, head_dim)
    even, odd = wide[:, 0], wide[:, 1]
    upper = lax.broadcasted_iota(jnp.int32, even.shape, 1) < GROUP
    first = jnp.where(upper, even, pltpu.roll(odd, GROUP, 1))
    second = jnp.where(upper, pltpu.roll(even, GROUP, 1), odd)
    return tuple(x.reshape(count // 2, head_dim).astype(jnp.bfloat16) for x in (first, second))


def join_heads(first, *others):
    count, head_dim = first.shape
    if not others:
        return first.astype(jnp.bfloat16)
    (second,) = others
    first = first.reshape(count // 8, 8, head_dim)
    second = second.reshape(count // 8, 8, head_dim)
    upper = lax.broadcasted_iota(jnp.int32, first.shape, 1) < GROUP
    even = jnp.where(upper, first, pltpu.roll(second, GROUP, 1))
    odd = jnp.where(upper, pltpu.roll(first, GROUP, 1), second)
    return jnp.stack([even, odd], axis=1).reshape(count * 2, head_dim).astype(jnp.bfloat16)


def score(key_rows, query):
    return lax.dot_general(
        key_rows, query, (((1,), (1,)), ((), ())), preferred_element_type=jnp.float32
    )


def causal(scores):
    key = lax.broadcasted_iota(jnp.int32, scores.shape, 0)
    per_head = scores.shape[1] // scores.shape[0]
    token = lax.broadcasted_iota(jnp.int32, scores.shape, 1) // per_head
    return jnp.where(key <= token, scores, MASKED)


def fold(weights):
    return jnp.sum(weights.reshape(weights.shape[0] // 8, 8, weights.shape[1]), axis=0)


def attend_units(
    units_ref, base, queries_ref, keys_ref, values_ref, highest_ref, sums_ref, totals_ref,
    *, used, block_len, scale, units_max,
):
    def read(unit):
        code = units_ref[base + unit]
        mask = (1 << FIELD) - 1
        return code >> (2 * FIELD), ((code >> FIELD) & mask) - 1, (code & mask) - 1

    def block(ref, item, slot):
        head = lax.rem(item, used)
        return ref[head, block_rows(jnp.maximum(slot, 0), block_len), :]

    def scores_of(unit):
        item, *slots = unit
        rows = jnp.concatenate([block(keys_ref, item, slot) for slot in slots], axis=0)
        return score(rows, queries_ref[item])

    def weigh(unit, scores, highest):
        item, *slots = unit
        parts = []
        for turn, slot in enumerate(slots):
            shift = jnp.where(slot < 0, CLOSED, highest)
            part = scores[turn * block_len : (turn + 1) * block_len]
            parts.append(jnp.exp2(part * scale - shift))
        weights = jnp.concatenate(parts, axis=0)
        columns = jnp.concatenate([block(values_ref, item, slot) for slot in slots], axis=1)
        summed = jnp.dot(
            columns, weights.astype(jnp.bfloat16), preferred_element_type=jnp.float32
        )
        return fold(weights), summed

    count = units_ref[base + units_max]

    def some(turn, carry):
        units = [read(turn * UNITS_AT_ONCE + n) for n in range(UNITS_AT_ONCE)]
        scores = [scores_of(unit) for unit in units]
        shares = [weigh(u, s, highest_ref[u[0], :1, :]) for u, s in zip(units, scores)]
        for unit, (total, summed) in zip(units, shares):
            totals_ref[unit[0]] += total
            sums_ref[unit[0]] += summed
        return carry

    lax.fori_loop(0, (count + UNITS_AT_ONCE - 1) // UNITS_AT_ONCE, some, 0)

    def only(unit, item):
        its, first, second = read(unit)
        return item, jnp.where(its == item, first, -1), jnp.where(its == item, second, -1)

    def raise_highest(item, highest):
        def look(turn, highest):
            unit = only(turn, item)
            scores = scores_of(unit)
            for place, slot in enumerate(unit[1:]):
                part = scores[place * block_len : (place + 1) * block_len]
                found = jnp.max(part, axis=0, keepdims=True) * scale
                highest = jnp.where(slot < 0, highest, jnp.maximum(highest, found))
            return highest

        return lax.fori_loop(0, count, look, highest)

    def add_again(item, highest, sums, totals):
        def add(turn, carry):
            unit = only(turn, item)
            total, summed = weigh(unit, scores_of(unit), highest)
            return carry[0] + summed, carry[1] + total

        return lax.fori_loop(0, count, add, (sums, totals))

    return raise_highest, add_again


def unsafe(totals):
    return jnp.max(jnp.where(totals < SAFE_TOTAL, 0.0, 1.0)) > 0.0


def local_kernel(
    units_ref, first_ref, queries_ref, keys_ref, values_ref, clear_ref,
    sums_ref, totals_ref, highest_ref, split_ref,
    key_table, value_table, keys_wide, values_wide,
    *, blocks, step_blocks, used, kv_heads, block_len, scale, units_max, at_once,
):
    step = pl.program_id(0)
    rows = block_len * kv_heads

    @pl.when(step == 0)
    def _():
        def take_apart(turn, carry):
            for n in range(at_once):
                block = turn * at_once + n
                source = block_rows(block, rows)
                keys_wide[n] = keys_ref[source, :].astype(jnp.float32)
                values_wide[n] = values_ref[source, :].astype(jnp.float32)
                for head in range(used):
                    picked = pl.ds(first_ref[0] + head, block_len, stride=kv_heads)
                    target = block_rows(block, block_len)
                    key_table[head, target, :] = keys_wide[n, picked, :].astype(jnp.bfloat16)
                    value_table[head, target, :] = values_wide[n, picked, :].T.astype(
                        jnp.bfloat16
                    )
            return carry

        lax.fori_loop(0, blocks // at_once, take_apart, 0)

    query_rows = queries_ref.shape[0] // step_blocks

    def own_part(item, block, highest=None):
        head = lax.rem(item, used)
        here = block_rows(step * step_blocks + block, block_len)
        scores = causal(score(key_table[head, here, :], split_ref[item]))
        if highest is None:
            highest = jnp.max(scores, axis=0, keepdims=True) * scale
        weights = jnp.exp2(scores * scale - highest)
        summed = jnp.dot(
            value_table[head, here, :], weights.astype(jnp.bfloat16),
            preferred_element_type=jnp.float32,
        )
        return highest, fold(weights), summed

    def own_blocks(turn, carry):
        todo = []
        for n in range(at_once):
            block = turn * at_once + n
            raw = queries_ref[pl.ds(pl.multiple_of(block * query_rows, query_rows), query_rows), :]
            for head, query in enumerate(split_heads(raw, used)):
                split_ref[block * used + head] = query
                todo.append((block * used + head, block))
        for item, (highest, total, summed) in [(item, own_part(item, b)) for item, b in todo]:
            highest_ref[item] = jnp.broadcast_to(highest, total.shape) + clear_ref[...]
            totals_ref[item] = total
            sums_ref[item] = summed
        return carry

    lax.fori_loop(0, step_blocks // at_once, own_blocks, 0)
    raise_highest, add_again = attend_units(
        units_ref, step * (units_max + 1), split_ref, key_table, value_table, highest_ref,
        sums_ref, totals_ref, used=used, block_len=block_len, scale=scale, units_max=units_max,
    )

    @pl.when(unsafe(totals_ref[...]))
    def _():
        def mend(item, carry):
            highest = raise_highest(item, highest_ref[item][:1])
            _, total, summed = own_part(item, item // used, highest)
            sums, totals = add_again(item, highest, summed, total)
            highest_ref[item] = jnp.broadcast_to(highest, totals.shape)
            totals_ref[item] = totals
            sums_ref[item] = sums
            return carry

        lax.fori_loop(0, step_blocks * used, mend, 0)


def remote_kernel(
    units_ref, split_ref, sums_in, totals_in, highest_ref, *rest,
    shifts, step_blocks, used, block_len, scale, units_max, at_once,
):
    parcels, (out_ref, key_table, value_table, sums_ref, totals_ref) = (
        rest[:shifts], rest[shifts:]
    )
    step = pl.program_id(0)
    parcel_rows = REMOTE_BLOCK_MAX * block_len

    @pl.when(step == 0)
    def _():
        for shift, parcel in enumerate(parcels):
            place = pl.ds(shift * parcel_rows, parcel_rows)
            key_table[:, place, :] = parcel[0]
            value_table[:, place, :] = parcel[1]

    sums_ref[...] = sums_in[...]
    totals_ref[...] = totals_in[...]
    raise_highest, add_again = attend_units(
        units_ref, step * (units_max + 1), split_ref, key_table, value_table, highest_ref,
        sums_ref, totals_ref, used=used, block_len=block_len, scale=scale, units_max=units_max,
    )

    @pl.when(unsafe(totals_ref[...] * 0.5))
    def _():
        def mend(item, carry):
            before = highest_ref[item][:1]
            highest = raise_highest(item, before)
            shrink = jnp.exp2(before - highest)
            sums, totals = add_again(
                item, highest, sums_in[item] * shrink, totals_in[item] * shrink
            )
            totals_ref[item] = totals
            sums_ref[item] = sums
            return carry

        lax.fori_loop(0, step_blocks * used, mend, 0)

    query_rows = out_ref.shape[0] // step_blocks

    def finish(turn, carry):
        for n in range(at_once):
            block = turn * at_once + n
            parts = []
            for head in range(used):
                item = block * used + head
                total = jnp.sum(totals_ref[item], axis=0, keepdims=True)
                parts.append((sums_ref[item] * (1.0 / total)).T)
            place = pl.ds(pl.multiple_of(block * query_rows, query_rows), query_rows)
            out_ref[place, :] = join_heads(*parts)
        return carry

    lax.fori_loop(0, step_blocks // at_once, finish, 0)


def list_units(open_slot, index, steps, units_max):
    used, blocks, picks = index.shape
    ahead = jnp.arange(picks)[:, None] < jnp.arange(picks)[None, :]
    place = jnp.sum(open_slot[..., :, None] & ahead, axis=-2)
    here = open_slot[..., :, None] & (place[..., :, None] == jnp.arange(picks))
    packed = jnp.sum(jnp.where(here, index[..., :, None] + 1, 0), axis=-2)
    pairs = jnp.transpose(packed, (1, 0, 2)).reshape(steps, -1, picks // 2, 2)
    item = jnp.arange(pairs.shape[1], dtype=jnp.int32)[None, :, None]
    codes = (item << (2 * FIELD)) + (pairs[..., 0] << FIELD) + pairs[..., 1]
    filled = (pairs[..., 0] > 0).reshape(steps, -1)
    codes = codes.reshape(steps, -1)
    ahead = jnp.arange(codes.shape[1])[:, None] < jnp.arange(codes.shape[1])[None, :]
    place = jnp.sum(filled[:, :, None] & ahead, axis=1)
    here = filled[:, :, None] & (place[:, :, None] == jnp.arange(units_max))
    listed = jnp.sum(jnp.where(here, codes[:, :, None], 0), axis=1)
    count = jnp.sum(filled, axis=1, keepdims=True, dtype=jnp.int32)
    return jnp.concatenate([listed, count], axis=1).reshape(-1).astype(jnp.int32)


def on_device(queries, keys, values, chosen):
    tokens, query_heads, head_dim = queries.shape
    kv_heads = keys.shape[1]
    blocks, picks = chosen.shape[1:]
    block_len = tokens // blocks
    used = max(1, query_heads // GROUP)
    per_head = query_heads // used
    shards = lax.axis_size("ctx")
    shifts = shards - 1
    position = lax.axis_index("ctx")
    base = position * blocks
    first = lax.axis_index("rep") * query_heads // GROUP
    scale = LOG2E * head_dim**-0.5
    step_blocks = next(n for n in (6, 4, 3, 2, 1) if blocks % n == 0)
    at_once = next(n for n in (3, 2, 1) if step_blocks % n == 0)
    steps = blocks // step_blocks
    item_rows = per_head * block_len
    units_max = step_blocks * used * (picks // 2)
    units_max = -(-units_max // UNITS_AT_ONCE) * UNITS_AT_ONCE

    lists = lax.dynamic_slice_in_dim(chosen, first, used, 0)
    wanted = jnp.stack(
        [
            lax.ppermute(lists, "ctx", [(j, j - d) for j in range(d, shards)])
            for d in range(1, shards)
        ]
    )
    within = wanted - base
    mine = (within >= 0) & (within < blocks)
    request = jnp.stack(
        [
            jnp.min(jnp.where(mine, within, blocks - 1), axis=(2, 3)),
            jnp.max(jnp.where(mine, within, 0), axis=(2, 3)),
        ],
        axis=-1,
    )
    first = first.reshape(1)
    query_rows = queries.reshape(tokens * query_heads, head_dim)
    key_rows = keys.reshape(tokens * kv_heads, head_dim)
    value_rows = values.reshape(tokens * kv_heads, head_dim)
    *parcels, clear = pack(
        request.reshape(-1), first, key_rows, value_rows, kv_heads, shifts, used, block_len,
        (8, item_rows),
    )
    arrived = [
        lax.ppermute(parcel, "ctx", [(i, i + d) for i in range(shards - d)])
        for d, parcel in zip(range(1, shards), parcels)
    ]

    local = lists >= base
    own = base + jnp.arange(blocks)
    local_units = list_units(local & (lists != own[None, :, None]), lists - base, steps, units_max)
    shard_of = lists // blocks
    from_shard = shard_of[..., None] == jnp.arange(shards)
    lowest = jnp.min(
        jnp.where(from_shard, lists[..., None], shards * blocks), axis=(1, 2), keepdims=True
    )
    is_lowest = jnp.any(from_shard & (lists[..., None] == lowest), axis=-1)
    remote_index = (position - 1 - shard_of) * REMOTE_BLOCK_MAX + jnp.where(is_lowest, 0, 1)
    remote_units = list_units(~local, remote_index, steps, units_max)

    def stepped(*shape):
        return pl.BlockSpec(shape, lambda g, *_: (g,) + (0,) * (len(shape) - 1))

    def whole(shape):
        return pl.BlockSpec(shape, lambda g, *_: (0,) * len(shape))

    items = step_blocks * used
    query_spec = stepped(step_blocks * block_len * query_heads, head_dim)
    sums_spec = stepped(items, head_dim, item_rows)
    row_spec = stepped(items, 8, item_rows)
    split_spec = stepped(items, item_rows, head_dim)
    sums_shape = jax.ShapeDtypeStruct((blocks * used, head_dim, item_rows), jnp.float32)
    row_shape = jax.ShapeDtypeStruct((blocks * used, 8, item_rows), jnp.float32)
    split_shape = jax.ShapeDtypeStruct((blocks * used, item_rows, head_dim), jnp.bfloat16)
    sizes = dict(
        step_blocks=step_blocks, used=used, block_len=block_len, scale=scale,
        units_max=units_max, at_once=at_once,
    )
    wide = pltpu.VMEM((at_once, block_len * kv_heads, head_dim), jnp.float32)
    table = pltpu.VMEM((used, tokens, head_dim), jnp.bfloat16)
    sums, totals, highest, split = pl.pallas_call(
        functools.partial(local_kernel, blocks=blocks, kv_heads=kv_heads, **sizes),
        grid_spec=pltpu.PrefetchScalarGridSpec(
            num_scalar_prefetch=2,
            grid=(steps,),
            in_specs=[
                query_spec, whole(key_rows.shape), whole(value_rows.shape), whole(clear.shape)
            ],
            out_specs=[sums_spec, row_spec, row_spec, split_spec],
            scratch_shapes=[table, table, wide, wide],
        ),
        out_shape=[sums_shape, row_shape, row_shape, split_shape],
        compiler_params=pltpu.CompilerParams(vmem_limit_bytes=VMEM_BYTES),
        cost_estimate=pl.CostEstimate(
            flops=3 * tokens * query_heads * picks * block_len * head_dim,
            bytes_accessed=32 * 2**20,
            transcendentals=tokens * query_heads * picks * block_len,
        ),
        name="local_part",
    )(local_units, first, query_rows, key_rows, value_rows, clear)

    table = pltpu.VMEM((used, shifts * REMOTE_BLOCK_MAX * block_len, head_dim), jnp.bfloat16)
    out = pl.pallas_call(
        functools.partial(remote_kernel, shifts=shifts, **sizes),
        grid_spec=pltpu.PrefetchScalarGridSpec(
            num_scalar_prefetch=1,
            grid=(steps,),
            in_specs=[split_spec, sums_spec, row_spec, row_spec]
            + [whole(arrived[0].shape)] * shifts,
            out_specs=query_spec,
            scratch_shapes=[
                table,
                table,
                pltpu.VMEM((items, head_dim, item_rows), jnp.float32),
                pltpu.VMEM((items, 8, item_rows), jnp.float32),
            ],
        ),
        out_shape=jax.ShapeDtypeStruct(query_rows.shape, jnp.bfloat16),
        compiler_params=pltpu.CompilerParams(vmem_limit_bytes=VMEM_BYTES),
        name="remote_part",
    )(remote_units, split, sums, totals, highest, *arrived)
    return out.reshape(tokens, query_heads, head_dim)


def solution(mesh):
    return jax.shard_map(
        on_device,
        mesh=mesh,
        in_specs=(
            P(("groups", "ctx"), ("heads", "rep"), None),
            P(("groups", "ctx"), "heads", None),
            P(("groups", "ctx"), "heads", None),
            P("heads", ("groups", "ctx"), None),
        ),
        out_specs=P(("groups", "ctx"), ("heads", "rep"), None),
        check_vma=False,
    )
```

```python
import functools

import jax
import jax.numpy as jnp
from jax import lax
from jax.experimental import pallas as pl
from jax.experimental.pallas import tpu as pltpu
from jax.sharding import PartitionSpec as P

QUERY_HEADS = 32
KEY_VALUE_HEADS = 8
REMOTE_BLOCK_MAX = 2
GROUP = QUERY_HEADS // KEY_VALUE_HEADS
LOG2E = 1.4426950408889634
MASKED = -1e30
CLOSED = 3e38
SAFE_TOTAL = 2.0**100
VMEM_BYTES = 60 * 2**20
LOCAL_VMEM_BYTES = 20 * 2**20
REMOTE_VMEM_BYTES = 12 * 2**20
UNITS_AT_ONCE = 8
FIELD = 10


def block_rows(index, block_len):
    return pl.ds(pl.multiple_of(index * block_len, block_len), block_len)


def pack_kernel(
    request, keys_ref, values_ref, *rest, shifts, used, kv_heads, block_len
):
    first_ref, outs = rest[0], rest[1 : shifts + 1]
    clear_ref, blocks_ref, wide_ref, sems = rest[shifts + 1 :]
    rows = block_len * kv_heads
    clear_ref[...] = jnp.zeros_like(clear_ref)
    wanted = [
        (shift, head, turn)
        for shift in range(shifts)
        for head in range(used)
        for turn in range(REMOTE_BLOCK_MAX)
    ]
    copies = []
    for at in range(len(wanted)):
        for kind, table in enumerate((keys_ref, values_ref)):
            copies.append(
                pltpu.make_async_copy(
                    table.at[block_rows(request[at], rows)],
                    blocks_ref.at[2 * at + kind],
                    sems.at[2 * at + kind],
                )
            )
    for copy in copies:
        copy.start()
    for at, (shift, head, turn) in enumerate(wanted):
        target = slice(turn * block_len, (turn + 1) * block_len)
        picked = pl.ds(first_ref[0] + head, block_len, stride=kv_heads)
        for kind in range(2):
            place = 2 * at + kind
            copies[place].wait()
            wide_ref[place] = blocks_ref[place].astype(jnp.float32)
            block = wide_ref[place, picked, :]
            outs[shift][kind, head, target, :] = (block.T if kind else block).astype(jnp.bfloat16)


def pack(request, first, keys, values, kv_heads, shifts, used, block_len, row_shape):
    head_dim = keys.shape[-1]
    parcel = (2, used, REMOTE_BLOCK_MAX * block_len, head_dim)
    anywhere = pl.BlockSpec(memory_space=pl.ANY)
    count = 2 * shifts * used * REMOTE_BLOCK_MAX
    rows = block_len * kv_heads
    return pl.pallas_call(
        functools.partial(
            pack_kernel, shifts=shifts, used=used, kv_heads=kv_heads, block_len=block_len
        ),
        grid_spec=pltpu.PrefetchScalarGridSpec(
            num_scalar_prefetch=1,
            grid=(1,),
            in_specs=[anywhere, anywhere, pl.BlockSpec(memory_space=pltpu.SMEM)],
            out_specs=[pl.BlockSpec(parcel, lambda g, *_: (0, 0, 0, 0))] * shifts
            + [pl.BlockSpec(row_shape, lambda g, *_: (0, 0))],
            scratch_shapes=[
                pltpu.VMEM((count, rows, head_dim), jnp.bfloat16),
                pltpu.VMEM((count, rows, head_dim), jnp.float32),
                pltpu.SemaphoreType.DMA((count,)),
            ],
        ),
        out_shape=[jax.ShapeDtypeStruct(parcel, jnp.bfloat16)] * shifts
        + [jax.ShapeDtypeStruct(row_shape, jnp.float32)],
        compiler_params=pltpu.CompilerParams(vmem_limit_bytes=VMEM_BYTES),
        name="pack",
    )(request, keys, values, first)


def split_heads(rows, used):
    count, head_dim = rows.shape
    if used == 1:
        return (rows,)
    wide = rows.astype(jnp.float32).reshape(count // 16, 2, 8, head_dim)
    even, odd = wide[:, 0], wide[:, 1]
    upper = lax.broadcasted_iota(jnp.int32, even.shape, 1) < GROUP
    first = jnp.where(upper, even, pltpu.roll(odd, GROUP, 1))
    second = jnp.where(upper, pltpu.roll(even, GROUP, 1), odd)
    return tuple(x.reshape(count // 2, head_dim).astype(jnp.bfloat16) for x in (first, second))


def join_heads(first, *others):
    count, head_dim = first.shape
    if not others:
        return first.astype(jnp.bfloat16)
    (second,) = others
    first = first.reshape(count // 8, 8, head_dim)
    second = second.reshape(count // 8, 8, head_dim)
    upper = lax.broadcasted_iota(jnp.int32, first.shape, 1) < GROUP
    even = jnp.where(upper, first, pltpu.roll(second, GROUP, 1))
    odd = jnp.where(upper, pltpu.roll(first, GROUP, 1), second)
    return jnp.stack([even, odd], axis=1).reshape(count * 2, head_dim).astype(jnp.bfloat16)


def score(key_rows, query):
    return lax.dot_general(
        key_rows, query, (((1,), (1,)), ((), ())), preferred_element_type=jnp.float32
    )


def causal_mask(shape):
    key = lax.broadcasted_iota(jnp.int32, shape, 0)
    token = lax.broadcasted_iota(jnp.int32, shape, 1) // (shape[1] // shape[0])
    return jnp.where(key <= token, 0.0, MASKED)


def fold(weights):
    return jnp.sum(weights.reshape(weights.shape[0] // 8, 8, weights.shape[1]), axis=0)


def attend_units(
    units_ref, base, queries_ref, keys_ref, values_ref, highest_ref, sums_ref, totals_ref,
    *, used, block_len, scale, units_max,
):
    def read(unit):
        code = units_ref[base + unit]
        mask = (1 << FIELD) - 1
        return code >> (2 * FIELD), ((code >> FIELD) & mask) - 1, (code & mask) - 1

    def block(ref, item, slot):
        head = lax.rem(item, used)
        return ref[head, block_rows(jnp.maximum(slot, 0), block_len), :]

    def scores_of(unit):
        item, *slots = unit
        rows = jnp.concatenate([block(keys_ref, item, slot) for slot in slots], axis=0)
        return score(rows, queries_ref[item])

    def weigh(unit, scores, highest):
        item, *slots = unit
        parts = []
        for turn, slot in enumerate(slots):
            shift = jnp.where(slot < 0, CLOSED, highest)
            part = scores[turn * block_len : (turn + 1) * block_len]
            parts.append(jnp.exp2(part * scale - shift))
        weights = jnp.concatenate(parts, axis=0)
        columns = jnp.concatenate([block(values_ref, item, slot) for slot in slots], axis=1)
        summed = jnp.dot(
            columns, weights.astype(jnp.bfloat16), preferred_element_type=jnp.float32
        )
        return fold(weights), summed

    count = units_ref[base + units_max]

    def some(turn, carry):
        units = [read(turn * UNITS_AT_ONCE + n) for n in range(UNITS_AT_ONCE)]
        scores = [scores_of(unit) for unit in units]
        shares = [weigh(u, s, highest_ref[u[0], :1, :]) for u, s in zip(units, scores)]
        for unit, (total, summed) in zip(units, shares):
            totals_ref[unit[0]] += total
            sums_ref[unit[0]] += summed
        return carry

    lax.fori_loop(0, (count + UNITS_AT_ONCE - 1) // UNITS_AT_ONCE, some, 0)

    def only(unit, item):
        its, first, second = read(unit)
        return item, jnp.where(its == item, first, -1), jnp.where(its == item, second, -1)

    def raise_highest(item, highest):
        def look(turn, highest):
            unit = only(turn, item)
            scores = scores_of(unit)
            for place, slot in enumerate(unit[1:]):
                part = scores[place * block_len : (place + 1) * block_len]
                found = jnp.max(part, axis=0, keepdims=True) * scale
                highest = jnp.where(slot < 0, highest, jnp.maximum(highest, found))
            return highest

        return lax.fori_loop(0, count, look, highest)

    def add_again(item, highest, sums, totals):
        def add(turn, carry):
            unit = only(turn, item)
            total, summed = weigh(unit, scores_of(unit), highest)
            return carry[0] + summed, carry[1] + total

        return lax.fori_loop(0, count, add, (sums, totals))

    return raise_highest, add_again


def step_items(ref, step, items):
    return ref.at[pl.ds(step * items, items)]


def unsafe(totals):
    return jnp.max(jnp.where(totals < SAFE_TOTAL, 0.0, 1.0)) > 0.0


def local_kernel(
    units_ref, first_ref, queries_ref, keys_ref, values_ref, clear_ref,
    all_sums, all_totals, all_highest, all_split,
    key_table, value_table, keys_raw, values_raw, keys_wide, values_wide, mask_ref, sems,
    *, blocks, step_blocks, used, kv_heads, block_len, scale, units_max, at_once,
):
    step = pl.program_id(0)
    rows = block_len * kv_heads
    sums_ref, totals_ref, highest_ref, split_ref = (
        step_items(ref, step, step_blocks * used)
        for ref in (all_sums, all_totals, all_highest, all_split)
    )

    @pl.when(step == 0)
    def _():
        mask_ref[...] = causal_mask(mask_ref.shape)
        chunk = rows * at_once

        def copies(turn):
            place = pl.ds(pl.multiple_of(turn * chunk, chunk), chunk)
            return [
                pltpu.make_async_copy(source.at[place], raw.at[place], sems.at[kind, turn])
                for kind, (source, raw) in enumerate(
                    ((keys_ref, keys_raw), (values_ref, values_raw))
                )
            ]

        for turn in range(blocks // at_once):
            for copy in copies(turn):
                copy.start()

        def take_apart(turn, carry):
            for copy in copies(turn):
                copy.wait()
            for n in range(at_once):
                block = turn * at_once + n
                source = block_rows(block, rows)
                keys_wide[n] = keys_raw[source, :].astype(jnp.float32)
                values_wide[n] = values_raw[source, :].astype(jnp.float32)
                for head in range(used):
                    picked = pl.ds(first_ref[0] + head, block_len, stride=kv_heads)
                    target = block_rows(block, block_len)
                    key_table[head, target, :] = keys_wide[n, picked, :].astype(jnp.bfloat16)
                    value_table[head, target, :] = values_wide[n, picked, :].T.astype(
                        jnp.bfloat16
                    )
            return carry

        lax.fori_loop(0, blocks // at_once, take_apart, 0)

    query_rows = queries_ref.shape[0] // step_blocks

    def own_scores(item, block, query):
        here = block_rows(step * step_blocks + block, block_len)
        scores = score(key_table[lax.rem(item, used), here, :], query)
        return scores + mask_ref[...]

    def own_share(item, block, scores, highest):
        here = block_rows(step * step_blocks + block, block_len)
        weights = jnp.exp2(scores * scale - highest)
        summed = jnp.dot(
            value_table[lax.rem(item, used), here, :], weights.astype(jnp.bfloat16),
            preferred_element_type=jnp.float32,
        )
        return fold(weights), summed

    def own_blocks(turn, carry):
        todo = []
        for n in range(at_once):
            block = turn * at_once + n
            raw = queries_ref[pl.ds(pl.multiple_of(block * query_rows, query_rows), query_rows), :]
            for head, query in enumerate(split_heads(raw, used)):
                todo.append((block * used + head, block, query))
        scores = [own_scores(*each) for each in todo]
        highest = [jnp.max(each, axis=0, keepdims=True) * scale for each in scores]
        shares = [
            own_share(item, block, s, m) for (item, block, _), s, m in zip(todo, scores, highest)
        ]
        for (item, _, query), m, (total, summed) in zip(todo, highest, shares):
            split_ref[item] = query
            highest_ref[item] = jnp.broadcast_to(m, total.shape) + clear_ref[...]
            totals_ref[item] = total
            sums_ref[item] = summed
        return carry

    lax.fori_loop(0, step_blocks // at_once, own_blocks, 0)
    raise_highest, add_again = attend_units(
        units_ref, step * (units_max + 1), split_ref, key_table, value_table, highest_ref,
        sums_ref, totals_ref, used=used, block_len=block_len, scale=scale, units_max=units_max,
    )

    @pl.when(unsafe(totals_ref[...]))
    def _():
        def mend(item, carry):
            highest = raise_highest(item, highest_ref[item][:1])
            block = item // used
            scores = own_scores(item, block, split_ref[item])
            total, summed = own_share(item, block, scores, highest)
            sums, totals = add_again(item, highest, summed, total)
            highest_ref[item] = jnp.broadcast_to(highest, totals.shape)
            totals_ref[item] = totals
            sums_ref[item] = sums
            return carry

        lax.fori_loop(0, step_blocks * used, mend, 0)


def remote_kernel(
    units_ref, all_split, all_sums, all_totals, all_highest, *rest,
    shifts, blocks, step_blocks, used, block_len, scale, units_max, at_once,
):
    parcels, (out_ref, key_table, value_table, sums_ref, totals_ref) = (
        rest[:shifts], rest[shifts:]
    )
    step = pl.program_id(0)
    parcel_rows = REMOTE_BLOCK_MAX * block_len
    split_ref, sums_in, totals_in, highest_ref = (
        step_items(ref, step, step_blocks * used)
        for ref in (all_split, all_sums, all_totals, all_highest)
    )

    @pl.when(step == 0)
    def _():
        for shift, parcel in enumerate(parcels):
            place = pl.ds(shift * parcel_rows, parcel_rows)
            key_table[:, place, :] = parcel[0]
            value_table[:, place, :] = parcel[1]

    sums_ref[...] = sums_in[...]
    totals_ref[...] = totals_in[...]
    raise_highest, add_again = attend_units(
        units_ref, step * (units_max + 1), split_ref, key_table, value_table, highest_ref,
        sums_ref, totals_ref, used=used, block_len=block_len, scale=scale, units_max=units_max,
    )

    @pl.when(unsafe(totals_ref[...] * 0.5))
    def _():
        def mend(item, carry):
            before = highest_ref[item][:1]
            highest = raise_highest(item, before)
            shrink = jnp.exp2(before - highest)
            sums, totals = add_again(
                item, highest, sums_in[item] * shrink, totals_in[item] * shrink
            )
            totals_ref[item] = totals
            sums_ref[item] = sums
            return carry

        lax.fori_loop(0, step_blocks * used, mend, 0)

    query_rows = out_ref.shape[0] // step_blocks

    def finish(turn, carry):
        for n in range(at_once):
            block = turn * at_once + n
            parts = []
            for head in range(used):
                item = block * used + head
                total = jnp.sum(totals_ref[item], axis=0, keepdims=True)
                parts.append((sums_ref[item] * (1.0 / total)).T)
            place = pl.ds(pl.multiple_of(block * query_rows, query_rows), query_rows)
            out_ref[place, :] = join_heads(*parts)
        return carry

    lax.fori_loop(0, step_blocks // at_once, finish, 0)


def stepped(*shape):
    return pl.BlockSpec(shape, lambda g, *_: (g,) + (0,) * (len(shape) - 1))


def whole(shape):
    return pl.BlockSpec(shape, lambda g, *_: (0,) * len(shape))


def local_part(units, first, query_rows, key_rows, value_rows, clear, **sizes):
    blocks, step_blocks, used = sizes["blocks"], sizes["step_blocks"], sizes["used"]
    head_dim = query_rows.shape[1]
    item_rows = clear.shape[1]
    steps = blocks // step_blocks
    tokens = blocks * sizes["block_len"]
    kv_heads = key_rows.shape[0] // tokens
    wide = pltpu.VMEM((sizes["at_once"], sizes["block_len"] * kv_heads, head_dim), jnp.float32)
    table = pltpu.VMEM((used, tokens, head_dim), jnp.bfloat16)
    raw = pltpu.VMEM(key_rows.shape, jnp.bfloat16)
    row_shape = pltpu.VMEM((blocks * used, 8, item_rows), jnp.float32)
    return pl.pallas_call(
        functools.partial(local_kernel, kv_heads=kv_heads, **sizes),
        grid_spec=pltpu.PrefetchScalarGridSpec(
            num_scalar_prefetch=2,
            grid=(steps,),
            in_specs=[
                stepped(query_rows.shape[0] // steps, head_dim),
                pl.BlockSpec(memory_space=pl.ANY), pl.BlockSpec(memory_space=pl.ANY),
                whole(clear.shape),
            ],
            out_specs=[pl.BlockSpec(memory_space=pltpu.VMEM)] * 4,
            scratch_shapes=[
                table, table, raw, raw, wide, wide,
                pltpu.VMEM((sizes["block_len"], item_rows), jnp.float32),
                pltpu.SemaphoreType.DMA((2, blocks // sizes["at_once"])),
            ],
        ),
        out_shape=[
            pltpu.VMEM((blocks * used, head_dim, item_rows), jnp.float32),
            row_shape,
            row_shape,
            pltpu.VMEM((blocks * used, item_rows, head_dim), jnp.bfloat16),
        ],
        compiler_params=pltpu.CompilerParams(vmem_limit_bytes=LOCAL_VMEM_BYTES),
        cost_estimate=pl.CostEstimate(
            flops=2**34, bytes_accessed=32 * 2**20, transcendentals=2**25
        ),
        name="local_part",
    )(units, first, query_rows, key_rows, value_rows, clear)


def remote_part(units, states, arrived, out_shape, **sizes):
    sums, totals, highest, split = (
        pltpu.with_memory_space_constraint(state, pltpu.VMEM) for state in states
    )
    shifts = len(arrived)
    items = sizes["step_blocks"] * sizes["used"]
    steps = sizes["blocks"] // sizes["step_blocks"]
    _, item_rows, head_dim = split.shape
    table = pltpu.VMEM(
        (sizes["used"], shifts * arrived[0].shape[2], head_dim), jnp.bfloat16
    )
    return pl.pallas_call(
        functools.partial(remote_kernel, shifts=shifts, **sizes),
        grid_spec=pltpu.PrefetchScalarGridSpec(
            num_scalar_prefetch=1,
            grid=(steps,),
            in_specs=[pl.BlockSpec(memory_space=pltpu.VMEM)] * (4 + shifts),
            out_specs=stepped(out_shape[0] // steps, head_dim),
            scratch_shapes=[
                table,
                table,
                pltpu.VMEM((items, head_dim, item_rows), jnp.float32),
                pltpu.VMEM((items, 8, item_rows), jnp.float32),
            ],
        ),
        out_shape=jax.ShapeDtypeStruct(out_shape, jnp.bfloat16),
        compiler_params=pltpu.CompilerParams(vmem_limit_bytes=REMOTE_VMEM_BYTES),
        name="remote_part",
    )(units, split, sums, totals, highest, *arrived)


def list_units(open_slot, index, steps, units_max):
    used, blocks, picks = index.shape
    ahead = jnp.arange(picks)[:, None] < jnp.arange(picks)[None, :]
    place = jnp.sum(open_slot[..., :, None] & ahead, axis=-2)
    here = open_slot[..., :, None] & (place[..., :, None] == jnp.arange(picks))
    packed = jnp.sum(jnp.where(here, index[..., :, None] + 1, 0), axis=-2)
    pairs = jnp.transpose(packed, (1, 0, 2)).reshape(steps, -1, picks // 2, 2)
    item = jnp.arange(pairs.shape[1], dtype=jnp.int32)[None, :, None]
    codes = (item << (2 * FIELD)) + (pairs[..., 0] << FIELD) + pairs[..., 1]
    filled = (pairs[..., 0] > 0).reshape(steps, -1)
    codes = codes.reshape(steps, -1)
    ahead = jnp.arange(codes.shape[1])[:, None] < jnp.arange(codes.shape[1])[None, :]
    place = jnp.sum(filled[:, :, None] & ahead, axis=1)
    here = filled[:, :, None] & (place[:, :, None] == jnp.arange(units_max))
    listed = jnp.sum(jnp.where(here, codes[:, :, None], 0), axis=1)
    count = jnp.sum(filled, axis=1, keepdims=True, dtype=jnp.int32)
    return jnp.concatenate([listed, count], axis=1).reshape(-1).astype(jnp.int32)


def on_device(queries, keys, values, chosen):
    tokens, query_heads, head_dim = queries.shape
    kv_heads = keys.shape[1]
    blocks, picks = chosen.shape[1:]
    block_len = tokens // blocks
    used = max(1, query_heads // GROUP)
    per_head = query_heads // used
    shards = lax.axis_size("ctx")
    shifts = shards - 1
    position = lax.axis_index("ctx")
    base = position * blocks
    first = lax.axis_index("rep") * query_heads // GROUP
    scale = LOG2E * head_dim**-0.5
    step_blocks = next(n for n in (6, 4, 3, 2, 1) if blocks % n == 0)
    at_once = next(n for n in (3, 2, 1) if step_blocks % n == 0)
    steps = blocks // step_blocks
    item_rows = per_head * block_len
    units_max = step_blocks * used * (picks // 2)
    units_max = -(-units_max // UNITS_AT_ONCE) * UNITS_AT_ONCE

    lists = lax.dynamic_slice_in_dim(chosen, first, used, 0)
    wanted = jnp.stack(
        [
            lax.ppermute(lists, "ctx", [(j, j - d) for j in range(d, shards)])
            for d in range(1, shards)
        ]
    )
    within = wanted - base
    mine = (within >= 0) & (within < blocks)
    request = jnp.stack(
        [
            jnp.min(jnp.where(mine, within, blocks - 1), axis=(2, 3)),
            jnp.max(jnp.where(mine, within, 0), axis=(2, 3)),
        ],
        axis=-1,
    )
    first = first.reshape(1)
    query_rows, key_rows, value_rows = (
        pltpu.with_memory_space_constraint(rows.reshape(-1, head_dim), pltpu.HBM)
        for rows in (queries, keys, values)
    )
    *parcels, clear = pack(
        request.reshape(-1), first, key_rows, value_rows, kv_heads, shifts, used, block_len,
        (8, item_rows),
    )
    arrived = [
        lax.ppermute(parcel, "ctx", [(i, i + d) for i in range(shards - d)])
        for d, parcel in zip(range(1, shards), parcels)
    ]

    local = lists >= base
    own = base + jnp.arange(blocks)
    local_units = list_units(local & (lists != own[None, :, None]), lists - base, steps, units_max)
    shard_of = lists // blocks
    from_shard = shard_of[..., None] == jnp.arange(shards)
    lowest = jnp.min(
        jnp.where(from_shard, lists[..., None], shards * blocks), axis=(1, 2), keepdims=True
    )
    is_lowest = jnp.any(from_shard & (lists[..., None] == lowest), axis=-1)
    remote_index = (position - 1 - shard_of) * REMOTE_BLOCK_MAX + jnp.where(is_lowest, 0, 1)
    remote_units = list_units(~local, remote_index, steps, units_max)

    sizes = dict(
        blocks=blocks, step_blocks=step_blocks, used=used, block_len=block_len, scale=scale,
        units_max=units_max, at_once=at_once,
    )
    states = local_part(local_units, first, query_rows, key_rows, value_rows, clear, **sizes)
    out = remote_part(remote_units, states, arrived, query_rows.shape, **sizes)
    return out.reshape(tokens, query_heads, head_dim)


def solution(mesh):
    return jax.shard_map(
        on_device,
        mesh=mesh,
        in_specs=(
            P(("groups", "ctx"), ("heads", "rep"), None),
            P(("groups", "ctx"), "heads", None),
            P(("groups", "ctx"), "heads", None),
            P("heads", ("groups", "ctx"), None),
        ),
        out_specs=P(("groups", "ctx"), ("heads", "rep"), None),
        check_vma=False,
    )
```

```python
import functools

import jax
import jax.numpy as jnp
from jax import lax
from jax.experimental import pallas as pl
from jax.experimental.pallas import tpu as pltpu
from jax.sharding import PartitionSpec as P

QUERY_HEADS = 32
KEY_VALUE_HEADS = 8
REMOTE_BLOCK_MAX = 2
GROUP = QUERY_HEADS // KEY_VALUE_HEADS
LOG2E = 1.4426950408889634
MASKED = -1e30
CLOSED = 3e38
SAFE_TOTAL = 2.0**100
VMEM_BYTES = 60 * 2**20
LOCAL_VMEM_BYTES = 22 * 2**20
REMOTE_VMEM_BYTES = 22 * 2**20
UNITS_AT_ONCE = 8
FIELD = 10
ONES_ROWS = 16


def block_rows(index, block_len):
    return pl.ds(pl.multiple_of(index * block_len, block_len), block_len)


def pack_kernel(
    request, keys_ref, values_ref, *rest, shifts, used, kv_heads, block_len
):
    first_ref, outs = rest[0], rest[1 : shifts + 1]
    clear_ref, blocks_ref, wide_ref, sems = rest[shifts + 1 :]
    rows = block_len * kv_heads
    clear_ref[...] = jnp.zeros_like(clear_ref)
    wanted = [
        (shift, head, turn)
        for shift in range(shifts)
        for head in range(used)
        for turn in range(REMOTE_BLOCK_MAX)
    ]
    copies = []
    for at in range(len(wanted)):
        for kind, table in enumerate((keys_ref, values_ref)):
            copies.append(
                pltpu.make_async_copy(
                    table.at[block_rows(request[at], rows)],
                    blocks_ref.at[2 * at + kind],
                    sems.at[2 * at + kind],
                )
            )
    for copy in copies:
        copy.start()
    for at, (shift, head, turn) in enumerate(wanted):
        target = slice(turn * block_len, (turn + 1) * block_len)
        picked = pl.ds(first_ref[0] + head, block_len, stride=kv_heads)
        for kind in range(2):
            place = 2 * at + kind
            copies[place].wait()
            wide_ref[place] = blocks_ref[place].astype(jnp.float32)
            block = wide_ref[place, picked, :]
            outs[shift][kind, head, target, :] = (block.T if kind else block).astype(jnp.bfloat16)


def pack(request, first, keys, values, kv_heads, shifts, used, block_len, row_shape):
    head_dim = keys.shape[-1]
    parcel = (2, used, REMOTE_BLOCK_MAX * block_len, head_dim)
    anywhere = pl.BlockSpec(memory_space=pl.ANY)
    count = 2 * shifts * used * REMOTE_BLOCK_MAX
    rows = block_len * kv_heads
    return pl.pallas_call(
        functools.partial(
            pack_kernel, shifts=shifts, used=used, kv_heads=kv_heads, block_len=block_len
        ),
        grid_spec=pltpu.PrefetchScalarGridSpec(
            num_scalar_prefetch=1,
            grid=(1,),
            in_specs=[anywhere, anywhere, pl.BlockSpec(memory_space=pltpu.SMEM)],
            out_specs=[pl.BlockSpec(parcel, lambda g, *_: (0, 0, 0, 0))] * shifts
            + [pl.BlockSpec(memory_space=pltpu.VMEM)],
            scratch_shapes=[
                pltpu.VMEM((count, rows, head_dim), jnp.bfloat16),
                pltpu.VMEM((count, rows, head_dim), jnp.float32),
                pltpu.SemaphoreType.DMA((count,)),
            ],
        ),
        out_shape=[jax.ShapeDtypeStruct(parcel, jnp.bfloat16)] * shifts
        + [pltpu.VMEM(row_shape, jnp.float32)],
        compiler_params=pltpu.CompilerParams(vmem_limit_bytes=VMEM_BYTES),
        name="pack",
    )(request, keys, values, first)


def split_heads(rows, used):
    count, head_dim = rows.shape
    wide = rows.astype(jnp.float32)
    if used == 1:
        return (wide,)
    wide = wide.reshape(count // 16, 2, 8, head_dim)
    even, odd = wide[:, 0], wide[:, 1]
    upper = lax.broadcasted_iota(jnp.int32, even.shape, 1) < GROUP
    first = jnp.where(upper, even, pltpu.roll(odd, GROUP, 1))
    second = jnp.where(upper, pltpu.roll(even, GROUP, 1), odd)
    return tuple(part.reshape(count // 2, head_dim) for part in (first, second))


def join_heads(first, *others):
    count, head_dim = first.shape
    if not others:
        return first.astype(jnp.bfloat16)
    (second,) = others
    first = first.reshape(count // 8, 8, head_dim)
    second = second.reshape(count // 8, 8, head_dim)
    upper = lax.broadcasted_iota(jnp.int32, first.shape, 1) < GROUP
    even = jnp.where(upper, first, pltpu.roll(second, GROUP, 1))
    odd = jnp.where(upper, pltpu.roll(first, GROUP, 1), second)
    return jnp.stack([even, odd], axis=1).reshape(count * 2, head_dim).astype(jnp.bfloat16)


def score(key_rows, query):
    return lax.dot_general(
        key_rows, query, (((1,), (1,)), ((), ())), preferred_element_type=jnp.float32
    )


def causal_mask(shape):
    key = lax.broadcasted_iota(jnp.int32, shape, 0)
    token = lax.broadcasted_iota(jnp.int32, shape, 1) // (shape[1] // shape[0])
    return jnp.where(key <= token, 0.0, MASKED)


def two_parts(values):
    high = values.astype(jnp.bfloat16)
    low = (values - high.astype(jnp.float32)).astype(jnp.bfloat16)
    return jnp.concatenate([high, low], axis=-1)


def doubled(key_rows):
    return jnp.concatenate([key_rows, key_rows], axis=-1)


def attend_units(
    units_ref, queries_ref, keys_ref, values_ref, highest_ref, sums_ref,
    *, used, block_len, units_max,
):
    def read(unit):
        code = units_ref[unit]
        mask = (1 << FIELD) - 1
        return code >> (2 * FIELD), ((code >> FIELD) & mask) - 1, (code & mask) - 1

    def rows_of(ref, item, slot):
        height = ref.shape[1] // (keys_ref.shape[1] // block_len)
        return ref[lax.rem(item, used), block_rows(jnp.maximum(slot, 0), height), :]

    def scores_of(unit):
        item, *slots = unit
        rows = jnp.concatenate([rows_of(keys_ref, item, slot) for slot in slots], axis=0)
        return score(doubled(rows), queries_ref[item])

    def weigh(unit, scores, highest):
        item, *slots = unit
        parts = []
        for turn, slot in enumerate(slots):
            shift = jnp.where(slot < 0, CLOSED, highest)
            parts.append(jnp.exp2(scores[turn * block_len : (turn + 1) * block_len] - shift))
        weights = jnp.concatenate(parts, axis=0).astype(jnp.bfloat16)
        columns = jnp.concatenate([rows_of(values_ref, item, slot) for slot in slots], axis=1)
        return jnp.dot(columns, weights, preferred_element_type=jnp.float32)

    count = units_ref[units_max]

    def some(turn, carry):
        units = [read(turn * UNITS_AT_ONCE + n) for n in range(UNITS_AT_ONCE)]
        scores = [scores_of(unit) for unit in units]
        for unit, its_scores in zip(units, scores):
            sums_ref[unit[0]] += weigh(unit, its_scores, highest_ref[unit[0], :1, :])
        return carry

    lax.fori_loop(0, (count + UNITS_AT_ONCE - 1) // UNITS_AT_ONCE, some, 0)

    def only(unit, item):
        its, first, second = read(unit)
        return item, jnp.where(its == item, first, -1), jnp.where(its == item, second, -1)

    def raise_highest(item, highest):
        def look(turn, highest):
            unit = only(turn, item)
            scores = scores_of(unit)
            for place, slot in enumerate(unit[1:]):
                part = scores[place * block_len : (place + 1) * block_len]
                found = jnp.max(part, axis=0, keepdims=True)
                highest = jnp.where(slot < 0, highest, jnp.maximum(highest, found))
            return highest

        return lax.fori_loop(0, count, look, highest)

    def add_again(item, highest):
        def add(turn, carry):
            unit = only(turn, item)
            sums_ref[item] += weigh(unit, scores_of(unit), highest)
            return carry

        lax.fori_loop(0, count, add, 0)

    return raise_highest, add_again


def unsafe(sums_ref, height):
    totals = sums_ref[:, height : height + 8, :]
    return jnp.max(jnp.where(totals < SAFE_TOTAL, 0.0, 1.0)) > 0.0


def local_kernel(
    units_ref, first_ref, queries_ref, keys_ref, values_ref, clear_ref,
    sums_ref, highest_ref, split_ref,
    key_table, value_table, queries_raw, keys_raw, values_raw, keys_wide, values_wide, mask_ref,
    sems,
    *, blocks, used, kv_heads, block_len, scale, units_max, at_once,
):
    rows = block_len * kv_heads
    query_rows = queries_ref.shape[0] // blocks
    height = value_table.shape[1] // blocks
    head_dim = keys_ref.shape[1]

    def copies(turn):
        found = []
        for kind, (source, raw) in enumerate(
            ((keys_ref, keys_raw), (values_ref, values_raw), (queries_ref, queries_raw))
        ):
            chunk = source.shape[0] // blocks * at_once
            place = pl.ds(pl.multiple_of(turn * chunk, chunk), chunk)
            found.append(pltpu.make_async_copy(source.at[place], raw.at[place], sems.at[kind, turn]))
        return found

    for turn in range(blocks // at_once):
        for copy in copies(turn):
            copy.start()
    mask_ref[...] = causal_mask(mask_ref.shape) + clear_ref[:1, :1]
    ones = jnp.ones((height - head_dim, block_len), jnp.bfloat16)

    def own_scores(item, block, query):
        here = key_table[lax.rem(item, used), block_rows(block, block_len), :]
        return score(doubled(here), query) + mask_ref[...]

    def own_sum(item, block, scores, highest):
        weights = jnp.exp2(scores - highest).astype(jnp.bfloat16)
        columns = value_table[lax.rem(item, used), block_rows(block, height), :]
        return jnp.dot(columns, weights, preferred_element_type=jnp.float32)

    def chunk(turn, carry):
        for copy in copies(turn):
            copy.wait()
        todo = []
        for n in range(at_once):
            block = turn * at_once + n
            source = block_rows(block, rows)
            keys_wide[n] = keys_raw[source, :].astype(jnp.float32)
            values_wide[n] = values_raw[source, :].astype(jnp.float32)
            raw = queries_raw[block_rows(block, query_rows), :]
            for head, query in enumerate(split_heads(raw, used)):
                picked = pl.ds(first_ref[0] + head, block_len, stride=kv_heads)
                key_rows = keys_wide[n, picked, :].astype(jnp.bfloat16)
                columns = jnp.concatenate(
                    [values_wide[n, picked, :].T.astype(jnp.bfloat16), ones], axis=0
                )
                key_table[head, block_rows(block, block_len), :] = key_rows
                value_table[head, block_rows(block, height), :] = columns
                query = two_parts(query * scale)
                split_ref[block * used + head] = query
                todo.append((block * used + head, query, key_rows, columns))
        scores = [score(doubled(k), query) + mask_ref[...] for _, query, k, _ in todo]
        for (item, _, _, columns), its_scores in zip(todo, scores):
            highest = jnp.max(its_scores, axis=0, keepdims=True)
            weights = jnp.exp2(its_scores - highest).astype(jnp.bfloat16)
            highest_ref[item] = jnp.broadcast_to(highest, highest_ref.shape[1:])
            sums_ref[item] = jnp.dot(columns, weights, preferred_element_type=jnp.float32)
        return carry

    lax.fori_loop(0, blocks // at_once, chunk, 0)
    raise_highest, add_again = attend_units(
        units_ref, split_ref, key_table, value_table, highest_ref, sums_ref,
        used=used, block_len=block_len, units_max=units_max,
    )

    @pl.when(unsafe(sums_ref, head_dim))
    def _():
        def mend(item, carry):
            highest = raise_highest(item, highest_ref[item][:1])
            block = item // used
            scores = own_scores(item, block, split_ref[item])
            highest_ref[item] = jnp.broadcast_to(highest, highest_ref.shape[1:])
            sums_ref[item] = own_sum(item, block, scores, highest)
            add_again(item, highest)
            return carry

        lax.fori_loop(0, blocks * used, mend, 0)


def remote_kernel(
    units_ref, split_ref, sums_in, highest_ref, *rest,
    shifts, blocks, used, block_len, units_max, at_once,
):
    parcels, (out_ref, key_table, value_table, sums_ref, staged, sems) = (
        rest[:shifts], rest[shifts:]
    )
    head_dim = out_ref.shape[1]
    height = sums_in.shape[1]
    query_rows = out_ref.shape[0] // blocks
    ones = jnp.ones((height - head_dim, block_len), jnp.bfloat16)

    for shift, parcel in enumerate(parcels):
        for turn in range(REMOTE_BLOCK_MAX):
            at = shift * REMOTE_BLOCK_MAX + turn
            source = slice(turn * block_len, (turn + 1) * block_len)
            for head in range(used):
                key_table[head, at * block_len : (at + 1) * block_len, :] = parcel[0, head, source, :]
                value_table[head, at * height : at * height + head_dim, :] = parcel[
                    1, head, source, :
                ]
                value_table[head, at * height + head_dim : (at + 1) * height, :] = ones

    def take(item, carry):
        sums_ref[item] = sums_in[item]
        return carry

    lax.fori_loop(0, blocks * used, take, 0)
    raise_highest, add_again = attend_units(
        units_ref, split_ref, key_table, value_table, highest_ref, sums_ref,
        used=used, block_len=block_len, units_max=units_max,
    )

    @pl.when(unsafe(sums_ref, head_dim))
    def _():
        def mend(item, carry):
            before = highest_ref[item][:1]
            highest = raise_highest(item, before)
            sums_ref[item] = sums_in[item] * jnp.exp2(before - highest)
            add_again(item, highest)
            return carry

        lax.fori_loop(0, blocks * used, mend, 0)

    rows = at_once * query_rows

    def give(turn):
        slot = lax.rem(turn, 2)
        place = pl.ds(pl.multiple_of(turn * rows, rows), rows)
        return pltpu.make_async_copy(staged.at[slot], out_ref.at[place], sems.at[slot])

    def finish(turn, carry):
        slot = lax.rem(turn, 2)

        @pl.when(turn >= 2)
        def _():
            give(turn - 2).wait()

        for n in range(at_once):
            parts = []
            for head in range(used):
                item = (turn * at_once + n) * used + head
                total = sums_ref[item, head_dim : head_dim + 1, :]
                parts.append((sums_ref[item, :head_dim, :] * (1.0 / total)).T)
            staged[slot, n * query_rows : (n + 1) * query_rows, :] = join_heads(*parts)
        give(turn).start()
        return carry

    turns = blocks // at_once
    lax.fori_loop(0, turns, finish, 0)
    for turn in range(max(0, turns - 2), turns):
        give(turn).wait()


def local_part(units, first, query_rows, key_rows, value_rows, clear, **sizes):
    blocks, used, block_len = sizes["blocks"], sizes["used"], sizes["block_len"]
    at_once = sizes["at_once"]
    head_dim = query_rows.shape[1]
    item_rows = query_rows.shape[0] // (blocks * used)
    kv_heads = key_rows.shape[0] // (blocks * block_len)
    anywhere = pl.BlockSpec(memory_space=pl.ANY)
    in_vmem = pl.BlockSpec(memory_space=pltpu.VMEM)
    wide = pltpu.VMEM((at_once, block_len * kv_heads, head_dim), jnp.float32)
    height = head_dim + ONES_ROWS
    return pl.pallas_call(
        functools.partial(local_kernel, kv_heads=kv_heads, **sizes),
        grid_spec=pltpu.PrefetchScalarGridSpec(
            num_scalar_prefetch=2,
            grid=(1,),
            in_specs=[anywhere, anywhere, anywhere, in_vmem],
            out_specs=[in_vmem] * 3,
            scratch_shapes=[
                pltpu.VMEM((used, blocks * block_len, head_dim), jnp.bfloat16),
                pltpu.VMEM((used, blocks * height, block_len), jnp.bfloat16),
                pltpu.VMEM(query_rows.shape, jnp.bfloat16),
                pltpu.VMEM(key_rows.shape, jnp.bfloat16),
                pltpu.VMEM(key_rows.shape, jnp.bfloat16),
                wide,
                wide,
                pltpu.VMEM((block_len, item_rows), jnp.float32),
                pltpu.SemaphoreType.DMA((3, blocks // at_once)),
            ],
        ),
        out_shape=[
            pltpu.VMEM((blocks * used, height, item_rows), jnp.float32),
            pltpu.VMEM((blocks * used, 8, item_rows), jnp.float32),
            pltpu.VMEM((blocks * used, item_rows, 2 * head_dim), jnp.bfloat16),
        ],
        compiler_params=pltpu.CompilerParams(vmem_limit_bytes=LOCAL_VMEM_BYTES),
        cost_estimate=pl.CostEstimate(
            flops=2**34, bytes_accessed=32 * 2**20, transcendentals=2**25
        ),
        name="local_part",
    )(units, first, query_rows, key_rows, value_rows, in_place(clear))


def in_place(array):
    return pltpu.with_memory_space_constraint(array, pltpu.VMEM)


def remote_part(units, states, arrived, out_shape, **sizes):
    sums, highest, split = (in_place(state) for state in states)
    shifts = len(arrived)
    blocks, used, block_len = sizes["blocks"], sizes["used"], sizes["block_len"]
    height = sums.shape[1]
    head_dim = out_shape[1]
    slots = shifts * REMOTE_BLOCK_MAX
    sizes.pop("scale")
    return pl.pallas_call(
        functools.partial(remote_kernel, shifts=shifts, **sizes),
        grid_spec=pltpu.PrefetchScalarGridSpec(
            num_scalar_prefetch=1,
            grid=(1,),
            in_specs=[pl.BlockSpec(memory_space=pltpu.VMEM)] * (3 + shifts),
            out_specs=pl.BlockSpec(memory_space=pl.ANY),
            scratch_shapes=[
                pltpu.VMEM((used, slots * block_len, head_dim), jnp.bfloat16),
                pltpu.VMEM((used, slots * height, block_len), jnp.bfloat16),
                pltpu.VMEM(sums.shape, jnp.float32),
                pltpu.VMEM(
                    (2, sizes["at_once"] * out_shape[0] // blocks, head_dim), jnp.bfloat16
                ),
                pltpu.SemaphoreType.DMA((2,)),
            ],
        ),
        out_shape=jax.ShapeDtypeStruct(out_shape, jnp.bfloat16),
        compiler_params=pltpu.CompilerParams(vmem_limit_bytes=REMOTE_VMEM_BYTES),
        name="remote_part",
    )(units, split, sums, highest, *arrived)


def list_units(open_slots, index, units_max):
    lists, items, picks = index.shape
    ahead = jnp.arange(picks)[:, None] < jnp.arange(picks)[None, :]
    place = jnp.sum(open_slots[..., :, None] & ahead, axis=-2)
    half = jnp.arange(0, picks, 2)
    hit = open_slots[..., :, None]
    even = jnp.sum(
        jnp.where(hit & (place[..., :, None] == half), index[..., :, None] + 1, 0), axis=-2
    )
    odd = jnp.sum(
        jnp.where(hit & (place[..., :, None] == half + 1), index[..., :, None] + 1, 0), axis=-2
    )
    item = jnp.arange(items, dtype=jnp.int32)[None, :, None]
    codes = ((item << (2 * FIELD)) + (even << FIELD) + odd).reshape(lists, -1)
    filled = (even > 0).reshape(lists, -1)
    ahead = jnp.arange(codes.shape[1])[:, None] < jnp.arange(codes.shape[1])[None, :]
    place = jnp.sum(filled[:, :, None] & ahead, axis=1)
    target = jnp.arange(units_max + 1)
    here = filled[:, :, None] & (place[:, :, None] == target)
    count = jnp.sum(filled, axis=1, keepdims=True, dtype=jnp.int32)
    listed = jnp.sum(jnp.where(here, codes[:, :, None], 0), axis=1)
    return jnp.where(target == units_max, count, listed).astype(jnp.int32)


def on_device(queries, keys, values, chosen):
    tokens, query_heads, head_dim = queries.shape
    kv_heads = keys.shape[1]
    blocks, picks = chosen.shape[1:]
    block_len = tokens // blocks
    used = max(1, query_heads // GROUP)
    shards = lax.axis_size("ctx")
    shifts = shards - 1
    position = lax.axis_index("ctx")
    base = position * blocks
    first = lax.axis_index("rep") * query_heads // GROUP
    scale = LOG2E * head_dim**-0.5
    at_once = next(n for n in (3, 2, 1) if blocks % n == 0)
    units_max = blocks * used * ((picks + 1) // 2)
    units_max = -(-units_max // UNITS_AT_ONCE) * UNITS_AT_ONCE

    lists = lax.dynamic_slice_in_dim(chosen, first, used, 0)
    wanted = jnp.stack(
        [
            lax.ppermute(lists, "ctx", [(j, j - d) for j in range(d, shards)])
            for d in range(1, shards)
        ]
    )
    within = wanted - base
    mine = (within >= 0) & (within < blocks)
    request = jnp.stack(
        [
            jnp.min(jnp.where(mine, within, blocks - 1), axis=(2, 3)),
            jnp.max(jnp.where(mine, within, 0), axis=(2, 3)),
        ],
        axis=-1,
    )
    first = first.reshape(1)
    query_rows, key_rows, value_rows = (
        pltpu.with_memory_space_constraint(rows.reshape(-1, head_dim), pltpu.HBM)
        for rows in (queries, keys, values)
    )
    *parcels, clear = pack(
        request.reshape(-1), first, key_rows, value_rows, kv_heads, shifts, used, block_len,
        (8, head_dim),
    )
    arrived = [
        lax.ppermute(parcel, "ctx", [(i, i + d) for i in range(shards - d)])
        for d, parcel in zip(range(1, shards), parcels)
    ]

    by_item = jnp.transpose(lists, (1, 0, 2)).reshape(blocks * used, picks)
    local = by_item >= base
    own = base + jnp.arange(blocks * used) // used
    shard_of = by_item // blocks
    from_shard = shard_of[..., None] == jnp.arange(shards)
    lowest = jnp.min(
        jnp.where(from_shard, by_item[..., None], shards * blocks)
        .reshape(blocks, used, picks, shards),
        axis=(0, 2),
    )
    lowest = jnp.tile(lowest, (blocks, 1))[:, None, :]
    is_lowest = jnp.any(from_shard & (by_item[..., None] == lowest), axis=-1)
    remote_index = (position - 1 - shard_of) * REMOTE_BLOCK_MAX + jnp.where(is_lowest, 0, 1)
    units = list_units(
        jnp.stack([local & (by_item != own[:, None]), ~local]),
        jnp.stack([by_item - base, remote_index]),
        units_max,
    )
    sizes = dict(
        blocks=blocks, used=used, block_len=block_len, scale=scale, units_max=units_max,
        at_once=at_once,
    )
    states = local_part(units[0], first, query_rows, key_rows, value_rows, clear, **sizes)
    out = remote_part(units[1], states, arrived, query_rows.shape, **sizes)
    return out.reshape(tokens, query_heads, head_dim)


def solution(mesh):
    return jax.shard_map(
        on_device,
        mesh=mesh,
        in_specs=(
            P(("groups", "ctx"), ("heads", "rep"), None),
            P(("groups", "ctx"), "heads", None),
            P(("groups", "ctx"), "heads", None),
            P("heads", ("groups", "ctx"), None),
        ),
        out_specs=P(("groups", "ctx"), ("heads", "rep"), None),
        check_vma=False,
    )
```

```python
import functools

import jax
import jax.numpy as jnp
from jax import lax
from jax.experimental import pallas as pl
from jax.experimental.pallas import tpu as pltpu
from jax.sharding import PartitionSpec as P

QUERY_HEADS = 32
KEY_VALUE_HEADS = 8
REMOTE_BLOCK_MAX = 2
GROUP = QUERY_HEADS // KEY_VALUE_HEADS
LOG2E = 1.4426950408889634
MASKED = -1e30
CLOSED = 3e38
SAFE_TOTAL = 2.0**100
VMEM_BYTES = 60 * 2**20
LOCAL_VMEM_BYTES = 22 * 2**20
REMOTE_VMEM_BYTES = 22 * 2**20
UNITS_AT_ONCE = 8
FIELD = 10
ONES_ROWS = 16


def block_rows(index, block_len):
    return pl.ds(pl.multiple_of(index * block_len, block_len), block_len)


def pack_kernel(
    request, keys_ref, values_ref, *rest, shifts, used, kv_heads, block_len
):
    first_ref, outs = rest[0], rest[1 : shifts + 1]
    clear_ref, blocks_ref, wide_ref, sems = rest[shifts + 1 :]
    rows = block_len * kv_heads
    clear_ref[...] = jnp.zeros_like(clear_ref)
    wanted = [
        (shift, head, turn)
        for shift in range(shifts)
        for head in range(used)
        for turn in range(REMOTE_BLOCK_MAX)
    ]
    copies = []
    for at in range(len(wanted)):
        for kind, table in enumerate((keys_ref, values_ref)):
            copies.append(
                pltpu.make_async_copy(
                    table.at[block_rows(request[at], rows)],
                    blocks_ref.at[2 * at + kind],
                    sems.at[2 * at + kind],
                )
            )
    for copy in copies:
        copy.start()
    for at, (shift, head, turn) in enumerate(wanted):
        target = slice(turn * block_len, (turn + 1) * block_len)
        picked = pl.ds(first_ref[0] + head, block_len, stride=kv_heads)
        for kind in range(2):
            place = 2 * at + kind
            copies[place].wait()
            wide_ref[place] = blocks_ref[place].astype(jnp.float32)
            block = wide_ref[place, picked, :]
            outs[shift][kind, head, target, :] = (block.T if kind else block).astype(jnp.bfloat16)


def pack(request, first, keys, values, kv_heads, shifts, used, block_len, row_shape):
    head_dim = keys.shape[-1]
    parcel = (2, used, REMOTE_BLOCK_MAX * block_len, head_dim)
    anywhere = pl.BlockSpec(memory_space=pl.ANY)
    count = 2 * shifts * used * REMOTE_BLOCK_MAX
    rows = block_len * kv_heads
    return pl.pallas_call(
        functools.partial(
            pack_kernel, shifts=shifts, used=used, kv_heads=kv_heads, block_len=block_len
        ),
        grid_spec=pltpu.PrefetchScalarGridSpec(
            num_scalar_prefetch=1,
            grid=(1,),
            in_specs=[anywhere, anywhere, pl.BlockSpec(memory_space=pltpu.SMEM)],
            out_specs=[pl.BlockSpec(parcel, lambda g, *_: (0, 0, 0, 0))] * shifts
            + [pl.BlockSpec(memory_space=pltpu.VMEM)],
            scratch_shapes=[
                pltpu.VMEM((count, rows, head_dim), jnp.bfloat16),
                pltpu.VMEM((count, rows, head_dim), jnp.float32),
                pltpu.SemaphoreType.DMA((count,)),
            ],
        ),
        out_shape=[jax.ShapeDtypeStruct(parcel, jnp.bfloat16)] * shifts
        + [pltpu.VMEM(row_shape, jnp.float32)],
        compiler_params=pltpu.CompilerParams(vmem_limit_bytes=VMEM_BYTES),
        name="pack",
    )(request, keys, values, first)


def split_heads(rows, used):
    count, head_dim = rows.shape
    wide = rows.astype(jnp.float32)
    if used == 1:
        return (wide,)
    wide = wide.reshape(count // 16, 2, 8, head_dim)
    even, odd = wide[:, 0], wide[:, 1]
    upper = lax.broadcasted_iota(jnp.int32, even.shape, 1) < GROUP
    first = jnp.where(upper, even, pltpu.roll(odd, GROUP, 1))
    second = jnp.where(upper, pltpu.roll(even, GROUP, 1), odd)
    return tuple(part.reshape(count // 2, head_dim) for part in (first, second))


def join_heads(first, *others):
    count, head_dim = first.shape
    if not others:
        return first.astype(jnp.bfloat16)
    (second,) = others
    first = first.reshape(count // 8, 8, head_dim)
    second = second.reshape(count // 8, 8, head_dim)
    upper = lax.broadcasted_iota(jnp.int32, first.shape, 1) < GROUP
    even = jnp.where(upper, first, pltpu.roll(second, GROUP, 1))
    odd = jnp.where(upper, pltpu.roll(first, GROUP, 1), second)
    return jnp.stack([even, odd], axis=1).reshape(count * 2, head_dim).astype(jnp.bfloat16)


def score(key_rows, query):
    return lax.dot_general(
        key_rows, query, (((1,), (1,)), ((), ())), preferred_element_type=jnp.float32
    )


def causal_mask(shape):
    key = lax.broadcasted_iota(jnp.int32, shape, 0)
    token = lax.broadcasted_iota(jnp.int32, shape, 1) // (shape[1] // shape[0])
    return jnp.where(key <= token, 0.0, MASKED)


def attend_units(
    units_ref, queries_ref, keys_ref, values_ref, highest_ref, sums_ref,
    *, used, block_len, scale, units_max,
):
    def read(unit):
        code = units_ref[unit]
        mask = (1 << FIELD) - 1
        return code >> (2 * FIELD), ((code >> FIELD) & mask) - 1, (code & mask) - 1

    def rows_of(ref, item, slot):
        height = ref.shape[1] // (keys_ref.shape[1] // block_len)
        return ref[lax.rem(item, used), block_rows(jnp.maximum(slot, 0), height), :]

    def scores_of(unit):
        item, *slots = unit
        rows = jnp.concatenate([rows_of(keys_ref, item, slot) for slot in slots], axis=0)
        return score(rows, queries_ref[item])

    def weigh(unit, scores, highest):
        item, *slots = unit
        parts = []
        for turn, slot in enumerate(slots):
            shift = jnp.where(slot < 0, CLOSED, highest)
            part = scores[turn * block_len : (turn + 1) * block_len]
            parts.append(jnp.exp2(part * scale - shift))
        weights = jnp.concatenate(parts, axis=0).astype(jnp.bfloat16)
        columns = jnp.concatenate([rows_of(values_ref, item, slot) for slot in slots], axis=1)
        return jnp.dot(columns, weights, preferred_element_type=jnp.float32)

    count = units_ref[units_max]

    def some(turn, carry):
        units = [read(turn * UNITS_AT_ONCE + n) for n in range(UNITS_AT_ONCE)]
        scores = [scores_of(unit) for unit in units]
        for unit, its_scores in zip(units, scores):
            sums_ref[unit[0]] += weigh(unit, its_scores, highest_ref[unit[0], :1, :])
        return carry

    lax.fori_loop(0, (count + UNITS_AT_ONCE - 1) // UNITS_AT_ONCE, some, 0)

    def only(unit, item):
        its, first, second = read(unit)
        return item, jnp.where(its == item, first, -1), jnp.where(its == item, second, -1)

    def raise_highest(item, highest):
        def look(turn, highest):
            unit = only(turn, item)
            scores = scores_of(unit)
            for place, slot in enumerate(unit[1:]):
                part = scores[place * block_len : (place + 1) * block_len]
                found = jnp.max(part, axis=0, keepdims=True) * scale
                highest = jnp.where(slot < 0, highest, jnp.maximum(highest, found))
            return highest

        return lax.fori_loop(0, count, look, highest)

    def add_again(item, highest):
        def add(turn, carry):
            unit = only(turn, item)
            sums_ref[item] += weigh(unit, scores_of(unit), highest)
            return carry

        lax.fori_loop(0, count, add, 0)

    return raise_highest, add_again


def unsafe(sums_ref, height):
    totals = sums_ref[:, height : height + 8, :]
    return jnp.max(jnp.where(totals < SAFE_TOTAL, 0.0, 1.0)) > 0.0


def local_kernel(
    units_ref, first_ref, queries_ref, keys_ref, values_ref, clear_ref,
    sums_ref, highest_ref, split_ref,
    key_table, value_table, queries_raw, keys_raw, values_raw, keys_wide, values_wide, mask_ref,
    sems,
    *, blocks, used, kv_heads, block_len, scale, units_max, at_once,
):
    rows = block_len * kv_heads
    query_rows = queries_ref.shape[0] // blocks
    height = value_table.shape[1] // blocks
    head_dim = keys_ref.shape[1]

    def copies(turn):
        found = []
        for kind, (source, raw) in enumerate(
            ((keys_ref, keys_raw), (values_ref, values_raw), (queries_ref, queries_raw))
        ):
            chunk = source.shape[0] // blocks * at_once
            place = pl.ds(pl.multiple_of(turn * chunk, chunk), chunk)
            found.append(pltpu.make_async_copy(source.at[place], raw.at[place], sems.at[kind, turn]))
        return found

    for turn in range(blocks // at_once):
        for copy in copies(turn):
            copy.start()
    mask_ref[...] = causal_mask(mask_ref.shape) + clear_ref[:1, :1]
    ones = jnp.ones((height - head_dim, block_len), jnp.bfloat16)

    def own_scores(item, block, query):
        here = key_table[lax.rem(item, used), block_rows(block, block_len), :]
        return score(here, query) + mask_ref[...]

    def own_sum(item, block, scores, highest):
        weights = jnp.exp2(scores * scale - highest).astype(jnp.bfloat16)
        columns = value_table[lax.rem(item, used), block_rows(block, height), :]
        return jnp.dot(columns, weights, preferred_element_type=jnp.float32)

    def chunk(turn, carry):
        for copy in copies(turn):
            copy.wait()
        todo = []
        for n in range(at_once):
            block = turn * at_once + n
            source = block_rows(block, rows)
            keys_wide[n] = keys_raw[source, :].astype(jnp.float32)
            values_wide[n] = values_raw[source, :].astype(jnp.float32)
            raw = queries_raw[block_rows(block, query_rows), :]
            for head, query in enumerate(split_heads(raw, used)):
                picked = pl.ds(first_ref[0] + head, block_len, stride=kv_heads)
                key_rows = keys_wide[n, picked, :].astype(jnp.bfloat16)
                columns = jnp.concatenate(
                    [values_wide[n, picked, :].T.astype(jnp.bfloat16), ones], axis=0
                )
                key_table[head, block_rows(block, block_len), :] = key_rows
                value_table[head, block_rows(block, height), :] = columns
                query = query.astype(jnp.bfloat16)
                split_ref[block * used + head] = query
                todo.append((block * used + head, query, key_rows, columns))
        scores = [score(k, query) + mask_ref[...] for _, query, k, _ in todo]
        for (item, _, _, columns), its_scores in zip(todo, scores):
            highest = jnp.max(its_scores, axis=0, keepdims=True) * scale
            weights = jnp.exp2(its_scores * scale - highest).astype(jnp.bfloat16)
            highest_ref[item] = jnp.broadcast_to(highest, highest_ref.shape[1:])
            sums_ref[item] = jnp.dot(columns, weights, preferred_element_type=jnp.float32)
        return carry

    lax.fori_loop(0, blocks // at_once, chunk, 0)
    raise_highest, add_again = attend_units(
        units_ref, split_ref, key_table, value_table, highest_ref, sums_ref,
        used=used, block_len=block_len, scale=scale, units_max=units_max,
    )

    @pl.when(unsafe(sums_ref, head_dim))
    def _():
        def mend(item, carry):
            highest = raise_highest(item, highest_ref[item][:1])
            block = item // used
            scores = own_scores(item, block, split_ref[item])
            highest_ref[item] = jnp.broadcast_to(highest, highest_ref.shape[1:])
            sums_ref[item] = own_sum(item, block, scores, highest)
            add_again(item, highest)
            return carry

        lax.fori_loop(0, blocks * used, mend, 0)


def remote_kernel(
    units_ref, split_ref, sums_in, highest_ref, *rest,
    shifts, blocks, used, block_len, scale, units_max, at_once,
):
    parcels, (out_ref, key_table, value_table, sums_ref, staged, sems) = (
        rest[:shifts], rest[shifts:]
    )
    head_dim = out_ref.shape[1]
    height = sums_in.shape[1]
    query_rows = out_ref.shape[0] // blocks
    ones = jnp.ones((height - head_dim, block_len), jnp.bfloat16)

    for shift, parcel in enumerate(parcels):
        for turn in range(REMOTE_BLOCK_MAX):
            at = shift * REMOTE_BLOCK_MAX + turn
            source = slice(turn * block_len, (turn + 1) * block_len)
            for head in range(used):
                key_table[head, at * block_len : (at + 1) * block_len, :] = parcel[0, head, source, :]
                value_table[head, at * height : at * height + head_dim, :] = parcel[
                    1, head, source, :
                ]
                value_table[head, at * height + head_dim : (at + 1) * height, :] = ones

    def take(item, carry):
        sums_ref[item] = sums_in[item]
        return carry

    lax.fori_loop(0, blocks * used, take, 0)
    raise_highest, add_again = attend_units(
        units_ref, split_ref, key_table, value_table, highest_ref, sums_ref,
        used=used, block_len=block_len, scale=scale, units_max=units_max,
    )

    @pl.when(unsafe(sums_ref, head_dim))
    def _():
        def mend(item, carry):
            before = highest_ref[item][:1]
            highest = raise_highest(item, before)
            sums_ref[item] = sums_in[item] * jnp.exp2(before - highest)
            add_again(item, highest)
            return carry

        lax.fori_loop(0, blocks * used, mend, 0)

    rows = at_once * query_rows

    def give(turn):
        slot = lax.rem(turn, 2)
        place = pl.ds(pl.multiple_of(turn * rows, rows), rows)
        return pltpu.make_async_copy(staged.at[slot], out_ref.at[place], sems.at[slot])

    def finish(turn, carry):
        slot = lax.rem(turn, 2)

        @pl.when(turn >= 2)
        def _():
            give(turn - 2).wait()

        for n in range(at_once):
            parts = []
            for head in range(used):
                item = (turn * at_once + n) * used + head
                total = sums_ref[item, head_dim : head_dim + 1, :]
                parts.append((sums_ref[item, :head_dim, :] * (1.0 / total)).T)
            staged[slot, n * query_rows : (n + 1) * query_rows, :] = join_heads(*parts)
        give(turn).start()
        return carry

    turns = blocks // at_once
    lax.fori_loop(0, turns, finish, 0)
    for turn in range(max(0, turns - 2), turns):
        give(turn).wait()


def local_part(units, first, query_rows, key_rows, value_rows, clear, **sizes):
    blocks, used, block_len = sizes["blocks"], sizes["used"], sizes["block_len"]
    at_once = sizes["at_once"]
    head_dim = query_rows.shape[1]
    item_rows = query_rows.shape[0] // (blocks * used)
    kv_heads = key_rows.shape[0] // (blocks * block_len)
    anywhere = pl.BlockSpec(memory_space=pl.ANY)
    in_vmem = pl.BlockSpec(memory_space=pltpu.VMEM)
    wide = pltpu.VMEM((at_once, block_len * kv_heads, head_dim), jnp.float32)
    height = head_dim + ONES_ROWS
    return pl.pallas_call(
        functools.partial(local_kernel, kv_heads=kv_heads, **sizes),
        grid_spec=pltpu.PrefetchScalarGridSpec(
            num_scalar_prefetch=2,
            grid=(1,),
            in_specs=[anywhere, anywhere, anywhere, in_vmem],
            out_specs=[in_vmem] * 3,
            scratch_shapes=[
                pltpu.VMEM((used, blocks * block_len, head_dim), jnp.bfloat16),
                pltpu.VMEM((used, blocks * height, block_len), jnp.bfloat16),
                pltpu.VMEM(query_rows.shape, jnp.bfloat16),
                pltpu.VMEM(key_rows.shape, jnp.bfloat16),
                pltpu.VMEM(key_rows.shape, jnp.bfloat16),
                wide,
                wide,
                pltpu.VMEM((block_len, item_rows), jnp.float32),
                pltpu.SemaphoreType.DMA((3, blocks // at_once)),
            ],
        ),
        out_shape=[
            pltpu.VMEM((blocks * used, height, item_rows), jnp.float32),
            pltpu.VMEM((blocks * used, 8, item_rows), jnp.float32),
            pltpu.VMEM((blocks * used, item_rows, head_dim), jnp.bfloat16),
        ],
        compiler_params=pltpu.CompilerParams(vmem_limit_bytes=LOCAL_VMEM_BYTES),
        cost_estimate=pl.CostEstimate(
            flops=2**34, bytes_accessed=32 * 2**20, transcendentals=2**25
        ),
        name="local_part",
    )(units, first, query_rows, key_rows, value_rows, in_place(clear))


def in_place(array):
    return pltpu.with_memory_space_constraint(array, pltpu.VMEM)


def remote_part(units, states, arrived, out_shape, **sizes):
    sums, highest, split = (in_place(state) for state in states)
    shifts = len(arrived)
    blocks, used, block_len = sizes["blocks"], sizes["used"], sizes["block_len"]
    height = sums.shape[1]
    head_dim = out_shape[1]
    slots = shifts * REMOTE_BLOCK_MAX
    return pl.pallas_call(
        functools.partial(remote_kernel, shifts=shifts, **sizes),
        grid_spec=pltpu.PrefetchScalarGridSpec(
            num_scalar_prefetch=1,
            grid=(1,),
            in_specs=[pl.BlockSpec(memory_space=pltpu.VMEM)] * (3 + shifts),
            out_specs=pl.BlockSpec(memory_space=pl.ANY),
            scratch_shapes=[
                pltpu.VMEM((used, slots * block_len, head_dim), jnp.bfloat16),
                pltpu.VMEM((used, slots * height, block_len), jnp.bfloat16),
                pltpu.VMEM(sums.shape, jnp.float32),
                pltpu.VMEM(
                    (2, sizes["at_once"] * out_shape[0] // blocks, head_dim), jnp.bfloat16
                ),
                pltpu.SemaphoreType.DMA((2,)),
            ],
        ),
        out_shape=jax.ShapeDtypeStruct(out_shape, jnp.bfloat16),
        compiler_params=pltpu.CompilerParams(vmem_limit_bytes=REMOTE_VMEM_BYTES),
        name="remote_part",
    )(units, split, sums, highest, *arrived)


def list_units(open_slots, index, units_max):
    lists, items, picks = index.shape
    ahead = jnp.arange(picks)[:, None] < jnp.arange(picks)[None, :]
    place = jnp.sum(open_slots[..., :, None] & ahead, axis=-2)
    half = jnp.arange(0, picks, 2)
    hit = open_slots[..., :, None]
    even = jnp.sum(
        jnp.where(hit & (place[..., :, None] == half), index[..., :, None] + 1, 0), axis=-2
    )
    odd = jnp.sum(
        jnp.where(hit & (place[..., :, None] == half + 1), index[..., :, None] + 1, 0), axis=-2
    )
    item = jnp.arange(items, dtype=jnp.int32)[None, :, None]
    codes = ((item << (2 * FIELD)) + (even << FIELD) + odd).reshape(lists, -1)
    filled = (even > 0).reshape(lists, -1)
    ahead = jnp.arange(codes.shape[1])[:, None] < jnp.arange(codes.shape[1])[None, :]
    place = jnp.sum(filled[:, :, None] & ahead, axis=1)
    target = jnp.arange(units_max + 1)
    here = filled[:, :, None] & (place[:, :, None] == target)
    count = jnp.sum(filled, axis=1, keepdims=True, dtype=jnp.int32)
    listed = jnp.sum(jnp.where(here, codes[:, :, None], 0), axis=1)
    return jnp.where(target == units_max, count, listed).astype(jnp.int32)


def on_device(queries, keys, values, chosen):
    tokens, query_heads, head_dim = queries.shape
    kv_heads = keys.shape[1]
    blocks, picks = chosen.shape[1:]
    block_len = tokens // blocks
    used = max(1, query_heads // GROUP)
    shards = lax.axis_size("ctx")
    shifts = shards - 1
    position = lax.axis_index("ctx")
    base = position * blocks
    first = lax.axis_index("rep") * query_heads // GROUP
    scale = LOG2E * head_dim**-0.5
    at_once = next(n for n in (3, 2, 1) if blocks % n == 0)
    given_at_once = next(n for n in (6, 4, 3, 2, 1) if blocks % n == 0)
    units_max = blocks * used * ((picks + 1) // 2)
    units_max = -(-units_max // UNITS_AT_ONCE) * UNITS_AT_ONCE

    lists = lax.dynamic_slice_in_dim(chosen, first, used, 0)
    wanted = jnp.stack(
        [
            lax.ppermute(chosen, "ctx", [(j, j - d) for j in range(d, shards)])
            for d in range(1, shards)
        ]
    )
    wanted = lax.dynamic_slice_in_dim(wanted, first, used, 1)
    within = wanted - base
    mine = (within >= 0) & (within < blocks)
    request = jnp.stack(
        [
            jnp.min(jnp.where(mine, within, blocks - 1), axis=(2, 3)),
            jnp.max(jnp.where(mine, within, 0), axis=(2, 3)),
        ],
        axis=-1,
    )
    first = first.reshape(1)
    query_rows, key_rows, value_rows = (
        pltpu.with_memory_space_constraint(rows.reshape(-1, head_dim), pltpu.HBM)
        for rows in (queries, keys, values)
    )
    *parcels, clear = pack(
        request.reshape(-1), first, key_rows, value_rows, kv_heads, shifts, used, block_len,
        (8, head_dim),
    )
    arrived = [
        lax.ppermute(parcel, "ctx", [(i, i + d) for i in range(shards - d)])
        for d, parcel in zip(range(1, shards), parcels)
    ]

    by_item = jnp.transpose(lists, (1, 0, 2)).reshape(blocks * used, picks)
    local = by_item >= base
    own = base + jnp.arange(blocks * used) // used
    shard_of = by_item // blocks
    from_shard = shard_of[..., None] == jnp.arange(shards)
    lowest = jnp.min(
        jnp.where(from_shard, by_item[..., None], shards * blocks)
        .reshape(blocks, used, picks, shards),
        axis=(0, 2),
    )
    lowest = jnp.tile(lowest, (blocks, 1))[:, None, :]
    is_lowest = jnp.any(from_shard & (by_item[..., None] == lowest), axis=-1)
    remote_index = (position - 1 - shard_of) * REMOTE_BLOCK_MAX + jnp.where(is_lowest, 0, 1)
    units = list_units(
        jnp.stack([local & (by_item != own[:, None]), ~local]),
        jnp.stack([by_item - base, remote_index]),
        units_max,
    )
    sizes = dict(
        blocks=blocks, used=used, block_len=block_len, scale=scale, units_max=units_max
    )
    states = local_part(units[0], first, query_rows, key_rows, value_rows, clear, at_once=at_once, **sizes)
    out = remote_part(units[1], states, arrived, query_rows.shape, at_once=given_at_once, **sizes)
    return out.reshape(tokens, query_heads, head_dim)


def solution(mesh):
    return jax.shard_map(
        on_device,
        mesh=mesh,
        in_specs=(
            P(("groups", "ctx"), ("heads", "rep"), None),
            P(("groups", "ctx"), "heads", None),
            P(("groups", "ctx"), "heads", None),
            P("heads", ("groups", "ctx"), None),
        ),
        out_specs=P(("groups", "ctx"), ("heads", "rep"), None),
        check_vma=False,
    )
```

```python
import functools

import jax
import jax.numpy as jnp
from jax import lax
from jax.experimental import pallas as pl
from jax.experimental.pallas import tpu as pltpu
from jax.sharding import PartitionSpec as P

QUERY_HEADS = 32
KEY_VALUE_HEADS = 8
REMOTE_BLOCK_MAX = 2
GROUP = QUERY_HEADS // KEY_VALUE_HEADS
LOG2E = 1.4426950408889634
MASKED = -1e30
CLOSED = 3e38
SAFE_TOTAL = 2.0**100
VMEM_BYTES = 60 * 2**20
LOCAL_VMEM_BYTES = 22 * 2**20
REMOTE_VMEM_BYTES = 22 * 2**20
UNIT_KINDS = ((4, 4), (2, 4))
WIDEST = 4
FIELD = 6
ONES_ROWS = 16


def block_rows(index, block_len):
    return pl.ds(pl.multiple_of(index * block_len, block_len), block_len)


def pack_kernel(
    request, keys_ref, values_ref, *rest, shifts, used, kv_heads, block_len
):
    first_ref, outs = rest[0], rest[1 : shifts + 1]
    clear_ref, blocks_ref, wide_ref, sems = rest[shifts + 1 :]
    rows = block_len * kv_heads
    clear_ref[...] = jnp.zeros_like(clear_ref)
    wanted = [
        (shift, head, turn)
        for shift in range(shifts)
        for head in range(used)
        for turn in range(REMOTE_BLOCK_MAX)
    ]
    copies = []
    for at in range(len(wanted)):
        for kind, table in enumerate((keys_ref, values_ref)):
            copies.append(
                pltpu.make_async_copy(
                    table.at[block_rows(request[at], rows)],
                    blocks_ref.at[2 * at + kind],
                    sems.at[2 * at + kind],
                )
            )
    for copy in copies:
        copy.start()
    for at, (shift, head, turn) in enumerate(wanted):
        target = slice(turn * block_len, (turn + 1) * block_len)
        picked = pl.ds(first_ref[0] + head, block_len, stride=kv_heads)
        for kind in range(2):
            place = 2 * at + kind
            copies[place].wait()
            wide_ref[place] = blocks_ref[place].astype(jnp.float32)
            block = wide_ref[place, picked, :]
            outs[shift][kind, head, target, :] = (block.T if kind else block).astype(jnp.bfloat16)


def pack(request, first, keys, values, kv_heads, shifts, used, block_len, row_shape):
    head_dim = keys.shape[-1]
    parcel = (2, used, REMOTE_BLOCK_MAX * block_len, head_dim)
    anywhere = pl.BlockSpec(memory_space=pl.ANY)
    count = 2 * shifts * used * REMOTE_BLOCK_MAX
    rows = block_len * kv_heads
    return pl.pallas_call(
        functools.partial(
            pack_kernel, shifts=shifts, used=used, kv_heads=kv_heads, block_len=block_len
        ),
        grid_spec=pltpu.PrefetchScalarGridSpec(
            num_scalar_prefetch=1,
            grid=(1,),
            in_specs=[anywhere, anywhere, pl.BlockSpec(memory_space=pltpu.SMEM)],
            out_specs=[pl.BlockSpec(memory_space=pltpu.VMEM)] * (shifts + 1),
            scratch_shapes=[
                pltpu.VMEM((count, rows, head_dim), jnp.bfloat16),
                pltpu.VMEM((count, rows, head_dim), jnp.float32),
                pltpu.SemaphoreType.DMA((count,)),
            ],
        ),
        out_shape=[pltpu.VMEM(parcel, jnp.bfloat16)] * shifts
        + [pltpu.VMEM(row_shape, jnp.float32)],
        compiler_params=pltpu.CompilerParams(vmem_limit_bytes=VMEM_BYTES),
        name="pack",
    )(request, keys, values, first)


def split_heads(rows, used):
    count, head_dim = rows.shape
    wide = rows.astype(jnp.float32)
    if used == 1:
        return (wide,)
    wide = wide.reshape(count // 16, 2, 8, head_dim)
    even, odd = wide[:, 0], wide[:, 1]
    upper = lax.broadcasted_iota(jnp.int32, even.shape, 1) < GROUP
    first = jnp.where(upper, even, pltpu.roll(odd, GROUP, 1))
    second = jnp.where(upper, pltpu.roll(even, GROUP, 1), odd)
    return tuple(part.reshape(count // 2, head_dim) for part in (first, second))


def join_heads(first, *others):
    count, head_dim = first.shape
    if not others:
        return first.astype(jnp.bfloat16)
    (second,) = others
    first = first.reshape(count // 8, 8, head_dim)
    second = second.reshape(count // 8, 8, head_dim)
    upper = lax.broadcasted_iota(jnp.int32, first.shape, 1) < GROUP
    even = jnp.where(upper, first, pltpu.roll(second, GROUP, 1))
    odd = jnp.where(upper, pltpu.roll(first, GROUP, 1), second)
    return jnp.stack([even, odd], axis=1).reshape(count * 2, head_dim).astype(jnp.bfloat16)


def score(key_rows, query):
    return lax.dot_general(
        key_rows, query, (((1,), (1,)), ((), ())), preferred_element_type=jnp.float32
    )


def causal_mask(shape):
    key = lax.broadcasted_iota(jnp.int32, shape, 0)
    token = lax.broadcasted_iota(jnp.int32, shape, 1) // (shape[1] // shape[0])
    return jnp.where(key <= token, 0.0, MASKED)


def attend_units(
    units_ref, queries_ref, keys_ref, values_ref, highest_ref, sums_ref,
    *, used, block_len, scale, units_max,
):
    def read(base, unit, width):
        code = units_ref[base + unit]
        mask = (1 << FIELD) - 1
        slots = [((code >> ((WIDEST - 1 - n) * FIELD)) & mask) - 1 for n in range(width)]
        return code >> (WIDEST * FIELD), *slots

    def rows_of(ref, item, slot):
        height = ref.shape[1] // (keys_ref.shape[1] // block_len)
        return ref[lax.rem(item, used), block_rows(jnp.maximum(slot, 0), height), :]

    def scores_of(unit):
        item, *slots = unit
        rows = jnp.concatenate([rows_of(keys_ref, item, slot) for slot in slots], axis=0)
        return score(rows, queries_ref[item])

    def weigh(unit, scores, highest):
        item, *slots = unit
        parts = []
        for turn, slot in enumerate(slots):
            shift = jnp.where(slot < 0, CLOSED, highest)
            part = scores[turn * block_len : (turn + 1) * block_len]
            parts.append(jnp.exp2(part * scale - shift))
        weights = jnp.concatenate(parts, axis=0).astype(jnp.bfloat16)
        columns = jnp.concatenate([rows_of(values_ref, item, slot) for slot in slots], axis=1)
        return jnp.dot(columns, weights, preferred_element_type=jnp.float32)

    lists = [(kind * (units_max + 1), *sizes) for kind, sizes in enumerate(UNIT_KINDS)]
    for base, width, at_once in lists:

        def some(turn, carry, base=base, width=width, at_once=at_once):
            units = [read(base, turn * at_once + n, width) for n in range(at_once)]
            scores = [scores_of(unit) for unit in units]
            for unit, its_scores in zip(units, scores):
                sums_ref[unit[0]] += weigh(unit, its_scores, highest_ref[unit[0], :1, :])
            return carry

        lax.fori_loop(0, (units_ref[base + units_max] + at_once - 1) // at_once, some, 0)

    def only(base, unit, width, item):
        its, *slots = read(base, unit, width)
        return item, *(jnp.where(its == item, slot, -1) for slot in slots)

    def raise_highest(item, highest):
        for base, width, _ in lists:

            def look(turn, highest, base=base, width=width):
                unit = only(base, turn, width, item)
                scores = scores_of(unit)
                for place, slot in enumerate(unit[1:]):
                    part = scores[place * block_len : (place + 1) * block_len]
                    found = jnp.max(part, axis=0, keepdims=True) * scale
                    highest = jnp.where(slot < 0, highest, jnp.maximum(highest, found))
                return highest

            highest = lax.fori_loop(0, units_ref[base + units_max], look, highest)
        return highest

    def add_again(item, highest):
        for base, width, _ in lists:

            def add(turn, carry, base=base, width=width):
                unit = only(base, turn, width, item)
                sums_ref[item] += weigh(unit, scores_of(unit), highest)
                return carry

            lax.fori_loop(0, units_ref[base + units_max], add, 0)

    return raise_highest, add_again


def unsafe(sums_ref, height):
    totals = sums_ref[:, height : height + 8, :]
    return jnp.max(jnp.where(totals < SAFE_TOTAL, 0.0, 1.0)) > 0.0


def local_kernel(
    units_ref, first_ref, queries_ref, keys_ref, values_ref, clear_ref,
    sums_ref, highest_ref, split_ref,
    key_table, value_table, queries_raw, keys_raw, values_raw, keys_wide, values_wide, mask_ref,
    sems,
    *, blocks, used, kv_heads, block_len, scale, units_max, at_once,
):
    rows = block_len * kv_heads
    query_rows = queries_ref.shape[0] // blocks
    height = value_table.shape[1] // blocks
    head_dim = keys_ref.shape[1]

    def copies(turn):
        found = []
        for kind, (source, raw) in enumerate(
            ((keys_ref, keys_raw), (values_ref, values_raw), (queries_ref, queries_raw))
        ):
            chunk = source.shape[0] // blocks * at_once
            place = pl.ds(pl.multiple_of(turn * chunk, chunk), chunk)
            found.append(pltpu.make_async_copy(source.at[place], raw.at[place], sems.at[kind, turn]))
        return found

    for turn in range(blocks // at_once):
        for copy in copies(turn):
            copy.start()
    mask_ref[...] = causal_mask(mask_ref.shape) + clear_ref[:1, :1]
    ones = jnp.ones((height - head_dim, block_len), jnp.bfloat16)

    def own_scores(item, block, query):
        here = key_table[lax.rem(item, used), block_rows(block, block_len), :]
        return score(here, query) + mask_ref[...]

    def own_sum(item, block, scores, highest):
        weights = jnp.exp2(scores * scale - highest).astype(jnp.bfloat16)
        columns = value_table[lax.rem(item, used), block_rows(block, height), :]
        return jnp.dot(columns, weights, preferred_element_type=jnp.float32)

    def chunk(turn, carry):
        for copy in copies(turn):
            copy.wait()
        todo = []
        for n in range(at_once):
            block = turn * at_once + n
            source = block_rows(block, rows)
            keys_wide[n] = keys_raw[source, :].astype(jnp.float32)
            values_wide[n] = values_raw[source, :].astype(jnp.float32)
            raw = queries_raw[block_rows(block, query_rows), :]
            for head, query in enumerate(split_heads(raw, used)):
                picked = pl.ds(first_ref[0] + head, block_len, stride=kv_heads)
                key_rows = keys_wide[n, picked, :].astype(jnp.bfloat16)
                columns = jnp.concatenate(
                    [values_wide[n, picked, :].T.astype(jnp.bfloat16), ones], axis=0
                )
                key_table[head, block_rows(block, block_len), :] = key_rows
                value_table[head, block_rows(block, height), :] = columns
                query = query.astype(jnp.bfloat16)
                split_ref[block * used + head] = query
                todo.append((block * used + head, query, key_rows, columns))
        scores = [score(k, query) + mask_ref[...] for _, query, k, _ in todo]
        for (item, _, _, columns), its_scores in zip(todo, scores):
            highest = jnp.max(its_scores, axis=0, keepdims=True) * scale
            weights = jnp.exp2(its_scores * scale - highest).astype(jnp.bfloat16)
            highest_ref[item] = jnp.broadcast_to(highest, highest_ref.shape[1:])
            sums_ref[item] = jnp.dot(columns, weights, preferred_element_type=jnp.float32)
        return carry

    lax.fori_loop(0, blocks // at_once, chunk, 0)
    raise_highest, add_again = attend_units(
        units_ref, split_ref, key_table, value_table, highest_ref, sums_ref,
        used=used, block_len=block_len, scale=scale, units_max=units_max,
    )

    @pl.when(unsafe(sums_ref, head_dim))
    def _():
        def mend(item, carry):
            highest = raise_highest(item, highest_ref[item][:1])
            block = item // used
            scores = own_scores(item, block, split_ref[item])
            highest_ref[item] = jnp.broadcast_to(highest, highest_ref.shape[1:])
            sums_ref[item] = own_sum(item, block, scores, highest)
            add_again(item, highest)
            return carry

        lax.fori_loop(0, blocks * used, mend, 0)


def remote_kernel(
    units_ref, split_ref, sums_in, highest_ref, *rest,
    shifts, blocks, used, block_len, scale, units_max, at_once,
):
    parcels, (out_ref, key_table, value_table, sums_ref, staged, sems) = (
        rest[:shifts], rest[shifts:]
    )
    head_dim = out_ref.shape[1]
    height = sums_in.shape[1]
    query_rows = out_ref.shape[0] // blocks
    ones = jnp.ones((height - head_dim, block_len), jnp.bfloat16)

    for shift, parcel in enumerate(parcels):
        for turn in range(REMOTE_BLOCK_MAX):
            at = shift * REMOTE_BLOCK_MAX + turn
            source = slice(turn * block_len, (turn + 1) * block_len)
            for head in range(used):
                key_table[head, at * block_len : (at + 1) * block_len, :] = parcel[0, head, source, :]
                value_table[head, at * height : at * height + head_dim, :] = parcel[
                    1, head, source, :
                ]
                value_table[head, at * height + head_dim : (at + 1) * height, :] = ones

    def take(item, carry):
        sums_ref[item] = sums_in[item]
        return carry

    lax.fori_loop(0, blocks * used, take, 0)
    raise_highest, add_again = attend_units(
        units_ref, split_ref, key_table, value_table, highest_ref, sums_ref,
        used=used, block_len=block_len, scale=scale, units_max=units_max,
    )

    @pl.when(unsafe(sums_ref, head_dim))
    def _():
        def mend(item, carry):
            before = highest_ref[item][:1]
            highest = raise_highest(item, before)
            sums_ref[item] = sums_in[item] * jnp.exp2(before - highest)
            add_again(item, highest)
            return carry

        lax.fori_loop(0, blocks * used, mend, 0)

    rows = at_once * query_rows

    def give(turn):
        slot = lax.rem(turn, 2)
        place = pl.ds(pl.multiple_of(turn * rows, rows), rows)
        return pltpu.make_async_copy(staged.at[slot], out_ref.at[place], sems.at[slot])

    def finish(turn, carry):
        slot = lax.rem(turn, 2)

        @pl.when(turn >= 2)
        def _():
            give(turn - 2).wait()

        for n in range(at_once):
            parts = []
            for head in range(used):
                item = (turn * at_once + n) * used + head
                total = sums_ref[item, head_dim : head_dim + 1, :]
                parts.append((sums_ref[item, :head_dim, :] * (1.0 / total)).T)
            staged[slot, n * query_rows : (n + 1) * query_rows, :] = join_heads(*parts)
        give(turn).start()
        return carry

    turns = blocks // at_once
    lax.fori_loop(0, turns, finish, 0)
    for turn in range(max(0, turns - 2), turns):
        give(turn).wait()


def local_part(units, first, query_rows, key_rows, value_rows, clear, **sizes):
    blocks, used, block_len = sizes["blocks"], sizes["used"], sizes["block_len"]
    at_once = sizes["at_once"]
    head_dim = query_rows.shape[1]
    item_rows = query_rows.shape[0] // (blocks * used)
    kv_heads = key_rows.shape[0] // (blocks * block_len)
    anywhere = pl.BlockSpec(memory_space=pl.ANY)
    in_vmem = pl.BlockSpec(memory_space=pltpu.VMEM)
    wide = pltpu.VMEM((at_once, block_len * kv_heads, head_dim), jnp.float32)
    height = head_dim + ONES_ROWS
    return pl.pallas_call(
        functools.partial(local_kernel, kv_heads=kv_heads, **sizes),
        grid_spec=pltpu.PrefetchScalarGridSpec(
            num_scalar_prefetch=2,
            grid=(1,),
            in_specs=[anywhere, anywhere, anywhere, in_vmem],
            out_specs=[in_vmem] * 3,
            scratch_shapes=[
                pltpu.VMEM((used, blocks * block_len, head_dim), jnp.bfloat16),
                pltpu.VMEM((used, blocks * height, block_len), jnp.bfloat16),
                pltpu.VMEM(query_rows.shape, jnp.bfloat16),
                pltpu.VMEM(key_rows.shape, jnp.bfloat16),
                pltpu.VMEM(key_rows.shape, jnp.bfloat16),
                wide,
                wide,
                pltpu.VMEM((block_len, item_rows), jnp.float32),
                pltpu.SemaphoreType.DMA((3, blocks // at_once)),
            ],
        ),
        out_shape=[
            pltpu.VMEM((blocks * used, height, item_rows), jnp.float32),
            pltpu.VMEM((blocks * used, 8, item_rows), jnp.float32),
            pltpu.VMEM((blocks * used, item_rows, head_dim), jnp.bfloat16),
        ],
        compiler_params=pltpu.CompilerParams(vmem_limit_bytes=LOCAL_VMEM_BYTES),
        cost_estimate=pl.CostEstimate(
            flops=2**34, bytes_accessed=32 * 2**20, transcendentals=2**25
        ),
        name="local_part",
    )(units, first, query_rows, key_rows, value_rows, in_place(clear))


def in_place(array):
    return pltpu.with_memory_space_constraint(array, pltpu.VMEM)


def remote_part(units, states, arrived, out_shape, **sizes):
    sums, highest, split = (in_place(state) for state in states)
    shifts = len(arrived)
    blocks, used, block_len = sizes["blocks"], sizes["used"], sizes["block_len"]
    height = sums.shape[1]
    head_dim = out_shape[1]
    slots = shifts * REMOTE_BLOCK_MAX
    return pl.pallas_call(
        functools.partial(remote_kernel, shifts=shifts, **sizes),
        grid_spec=pltpu.PrefetchScalarGridSpec(
            num_scalar_prefetch=1,
            grid=(1,),
            in_specs=[pl.BlockSpec(memory_space=pltpu.VMEM)] * (3 + shifts),
            out_specs=pl.BlockSpec(memory_space=pl.ANY),
            scratch_shapes=[
                pltpu.VMEM((used, slots * block_len, head_dim), jnp.bfloat16),
                pltpu.VMEM((used, slots * height, block_len), jnp.bfloat16),
                pltpu.VMEM(sums.shape, jnp.float32),
                pltpu.VMEM(
                    (2, sizes["at_once"] * out_shape[0] // blocks, head_dim), jnp.bfloat16
                ),
                pltpu.SemaphoreType.DMA((2,)),
            ],
        ),
        out_shape=jax.ShapeDtypeStruct(out_shape, jnp.bfloat16),
        compiler_params=pltpu.CompilerParams(vmem_limit_bytes=REMOTE_VMEM_BYTES),
        name="remote_part",
    )(units, split, sums, highest, *arrived)


def list_units(open_slots, index, units_max):
    parts, items, picks = index.shape
    ahead = jnp.arange(picks)[:, None] < jnp.arange(picks)[None, :]
    place = jnp.sum(open_slots[..., :, None] & ahead, axis=-2)
    width = -(-picks // WIDEST) * WIDEST
    here = open_slots[..., :, None] & (place[..., :, None] == jnp.arange(width))
    packed = jnp.sum(jnp.where(here, index[..., :, None] + 1, 0), axis=-2)
    groups = packed.reshape(parts, items * (width // WIDEST), WIDEST)
    shifts = jnp.arange(WIDEST - 1, -1, -1, dtype=jnp.int32) * FIELD
    item = jnp.arange(groups.shape[1], dtype=jnp.int32) // (width // WIDEST)
    codes = jnp.sum(groups << shifts, axis=-1) + (item << (WIDEST * FIELD))
    held = jnp.sum(groups > 0, axis=-1)
    narrow = UNIT_KINDS[1][0]
    filled = jnp.stack([held > narrow, (held > 0) & (held <= narrow)], axis=1)
    ahead = jnp.arange(codes.shape[1])[:, None] < jnp.arange(codes.shape[1])[None, :]
    place = jnp.sum(filled[..., :, None] & ahead, axis=-2)
    target = jnp.arange(units_max + 1)
    here = filled[..., :, None] & (place[..., :, None] == target)
    count = jnp.sum(filled, axis=-1, keepdims=True, dtype=jnp.int32)
    listed = jnp.sum(jnp.where(here, codes[:, None, :, None], 0), axis=-2)
    return jnp.where(target == units_max, count, listed).astype(jnp.int32).reshape(parts, -1)


def on_device(queries, keys, values, chosen):
    tokens, query_heads, head_dim = queries.shape
    kv_heads = keys.shape[1]
    blocks, picks = chosen.shape[1:]
    block_len = tokens // blocks
    used = max(1, query_heads // GROUP)
    shards = lax.axis_size("ctx")
    shifts = shards - 1
    position = lax.axis_index("ctx")
    base = position * blocks
    first = lax.axis_index("rep") * query_heads // GROUP
    scale = LOG2E * head_dim**-0.5
    at_once = next(n for n in (4, 3, 2, 1) if blocks % n == 0)
    given_at_once = next(n for n in (6, 4, 3, 2, 1) if blocks % n == 0)
    most = max(at_once for _, at_once in UNIT_KINDS)
    units_max = -(-blocks * used * -(-picks // WIDEST) // most) * most

    lists = lax.dynamic_slice_in_dim(chosen, first, used, 0)
    wanted = jnp.stack(
        [
            lax.ppermute(chosen, "ctx", [(j, j - d) for j in range(d, shards)])
            for d in range(1, shards)
        ]
    )
    wanted = lax.dynamic_slice_in_dim(wanted, first, used, 1)
    within = wanted - base
    mine = (within >= 0) & (within < blocks)
    request = jnp.stack(
        [
            jnp.min(jnp.where(mine, within, blocks - 1), axis=(2, 3)),
            jnp.max(jnp.where(mine, within, 0), axis=(2, 3)),
        ],
        axis=-1,
    )
    first = first.reshape(1)
    query_rows, key_rows, value_rows = (
        pltpu.with_memory_space_constraint(rows.reshape(-1, head_dim), pltpu.HBM)
        for rows in (queries, keys, values)
    )
    *parcels, clear = pack(
        request.reshape(-1), first, key_rows, value_rows, kv_heads, shifts, used, block_len,
        (8, head_dim),
    )
    arrived = [
        lax.ppermute(parcel, "ctx", [(i, i + d) for i in range(shards - d)])
        for d, parcel in zip(range(1, shards), parcels)
    ]

    by_item = jnp.transpose(lists, (1, 0, 2)).reshape(blocks * used, picks)
    local = by_item >= base
    own = base + jnp.arange(blocks * used) // used
    shard_of = by_item // blocks
    from_shard = shard_of[..., None] == jnp.arange(shards)
    lowest = jnp.min(
        jnp.where(from_shard, by_item[..., None], shards * blocks)
        .reshape(blocks, used, picks, shards),
        axis=(0, 2),
    )
    lowest = jnp.tile(lowest, (blocks, 1))[:, None, :]
    is_lowest = jnp.any(from_shard & (by_item[..., None] == lowest), axis=-1)
    remote_index = (position - 1 - shard_of) * REMOTE_BLOCK_MAX + jnp.where(is_lowest, 0, 1)
    units = list_units(
        jnp.stack([local & (by_item != own[:, None]), ~local]),
        jnp.stack([by_item - base, remote_index]),
        units_max,
    )
    sizes = dict(
        blocks=blocks, used=used, block_len=block_len, scale=scale, units_max=units_max
    )
    states = local_part(units[0], first, query_rows, key_rows, value_rows, clear, at_once=at_once, **sizes)
    out = remote_part(units[1], states, arrived, query_rows.shape, at_once=given_at_once, **sizes)
    return out.reshape(tokens, query_heads, head_dim)


def solution(mesh):
    return jax.shard_map(
        on_device,
        mesh=mesh,
        in_specs=(
            P(("groups", "ctx"), ("heads", "rep"), None),
            P(("groups", "ctx"), "heads", None),
            P(("groups", "ctx"), "heads", None),
            P("heads", ("groups", "ctx"), None),
        ),
        out_specs=P(("groups", "ctx"), ("heads", "rep"), None),
        check_vma=False,
    )
```

```python
import functools

import jax
import jax.numpy as jnp
from jax import lax
from jax.experimental import pallas as pl
from jax.experimental.pallas import tpu as pltpu
from jax.sharding import PartitionSpec as P

QUERY_HEADS = 32
KEY_VALUE_HEADS = 8
REMOTE_BLOCK_MAX = 2
GROUP = QUERY_HEADS // KEY_VALUE_HEADS
LOG2E = 1.4426950408889634
MASKED = -1e30
CLOSED = 3e38
SAFE_TOTAL = 2.0**100
PACK_VMEM_BYTES = 24 * 2**20
LOCAL_VMEM_BYTES = 26 * 2**20
REMOTE_VMEM_BYTES = 26 * 2**20
UNIT_KINDS = ((4, 6), (2, 6))
WIDEST = 4
FIELD = 6
ONES_ROWS = 16


def block_rows(index, block_len):
    return pl.ds(pl.multiple_of(index * block_len, block_len), block_len)


def pack_kernel(
    request, keys_ref, values_ref, *rest, shifts, used, kv_heads, block_len
):
    first_ref, outs = rest[0], rest[1 : shifts + 1]
    clear_ref, blocks_ref, wide_ref, sems = rest[shifts + 1 :]
    rows = block_len * kv_heads
    clear_ref[...] = jnp.zeros_like(clear_ref)
    wanted = [
        (shift, head, turn)
        for shift in range(shifts)
        for head in range(used)
        for turn in range(REMOTE_BLOCK_MAX)
    ]
    copies = []
    for at in range(len(wanted)):
        for kind, table in enumerate((keys_ref, values_ref)):
            copies.append(
                pltpu.make_async_copy(
                    table.at[block_rows(request[at], rows)],
                    blocks_ref.at[2 * at + kind],
                    sems.at[2 * at + kind],
                )
            )
    for copy in copies:
        copy.start()
    for at, (shift, head, turn) in enumerate(wanted):
        target = slice(turn * block_len, (turn + 1) * block_len)
        picked = pl.ds(first_ref[0] + head, block_len, stride=kv_heads)
        for kind in range(2):
            place = 2 * at + kind
            copies[place].wait()
            wide_ref[place] = blocks_ref[place].astype(jnp.float32)
            block = wide_ref[place, picked, :]
            outs[shift][kind, head, target, :] = (block.T if kind else block).astype(jnp.bfloat16)


def pack(request, first, keys, values, kv_heads, shifts, used, block_len, row_shape):
    head_dim = keys.shape[-1]
    parcel = (2, used, REMOTE_BLOCK_MAX * block_len, head_dim)
    anywhere = pl.BlockSpec(memory_space=pl.ANY)
    count = 2 * shifts * used * REMOTE_BLOCK_MAX
    rows = block_len * kv_heads
    return pl.pallas_call(
        functools.partial(
            pack_kernel, shifts=shifts, used=used, kv_heads=kv_heads, block_len=block_len
        ),
        grid_spec=pltpu.PrefetchScalarGridSpec(
            num_scalar_prefetch=1,
            grid=(1,),
            in_specs=[anywhere, anywhere, pl.BlockSpec(memory_space=pltpu.SMEM)],
            out_specs=[pl.BlockSpec(memory_space=pltpu.VMEM)] * (shifts + 1),
            scratch_shapes=[
                pltpu.VMEM((count, rows, head_dim), jnp.bfloat16),
                pltpu.VMEM((count, rows, head_dim), jnp.float32),
                pltpu.SemaphoreType.DMA((count,)),
            ],
        ),
        out_shape=[pltpu.VMEM(parcel, jnp.bfloat16)] * shifts
        + [pltpu.VMEM(row_shape, jnp.float32)],
        compiler_params=pltpu.CompilerParams(vmem_limit_bytes=PACK_VMEM_BYTES),
        name="pack",
    )(request, keys, values, first)


def split_heads(rows, used):
    count, head_dim = rows.shape
    wide = rows.astype(jnp.float32)
    if used == 1:
        return (wide,)
    wide = wide.reshape(count // 16, 2, 8, head_dim)
    even, odd = wide[:, 0], wide[:, 1]
    upper = lax.broadcasted_iota(jnp.int32, even.shape, 1) < GROUP
    first = jnp.where(upper, even, pltpu.roll(odd, GROUP, 1))
    second = jnp.where(upper, pltpu.roll(even, GROUP, 1), odd)
    return tuple(part.reshape(count // 2, head_dim) for part in (first, second))


def join_heads(first, *others):
    count, head_dim = first.shape
    if not others:
        return first.astype(jnp.bfloat16)
    (second,) = others
    first = first.reshape(count // 8, 8, head_dim)
    second = second.reshape(count // 8, 8, head_dim)
    upper = lax.broadcasted_iota(jnp.int32, first.shape, 1) < GROUP
    even = jnp.where(upper, first, pltpu.roll(second, GROUP, 1))
    odd = jnp.where(upper, pltpu.roll(first, GROUP, 1), second)
    return jnp.stack([even, odd], axis=1).reshape(count * 2, head_dim).astype(jnp.bfloat16)


def score(key_rows, query):
    return lax.dot_general(
        key_rows, query, (((1,), (1,)), ((), ())), preferred_element_type=jnp.float32
    )


def causal_mask(shape):
    key = lax.broadcasted_iota(jnp.int32, shape, 0)
    token = lax.broadcasted_iota(jnp.int32, shape, 1) // (shape[1] // shape[0])
    return jnp.where(key <= token, 0.0, MASKED)


def attend_units(
    units_ref, queries_ref, keys_ref, values_ref, highest_ref, sums_ref,
    *, used, block_len, scale, units_max,
):
    def read(base, unit, width):
        code = units_ref[base + unit]
        mask = (1 << FIELD) - 1
        slots = [((code >> ((WIDEST - 1 - n) * FIELD)) & mask) - 1 for n in range(width)]
        return code >> (WIDEST * FIELD), *slots

    def rows_of(ref, item, slot):
        height = ref.shape[1] // (keys_ref.shape[1] // block_len)
        return ref[lax.rem(item, used), block_rows(jnp.maximum(slot, 0), height), :]

    def scores_of(unit):
        item, *slots = unit
        rows = jnp.concatenate([rows_of(keys_ref, item, slot) for slot in slots], axis=0)
        return score(rows, queries_ref[item])

    def weigh(unit, scores, highest):
        item, *slots = unit
        parts = []
        for turn, slot in enumerate(slots):
            shift = jnp.where(slot < 0, CLOSED, highest)
            part = scores[turn * block_len : (turn + 1) * block_len]
            parts.append(jnp.exp2(part * scale - shift))
        weights = jnp.concatenate(parts, axis=0).astype(jnp.bfloat16)
        columns = jnp.concatenate([rows_of(values_ref, item, slot) for slot in slots], axis=1)
        return jnp.dot(columns, weights, preferred_element_type=jnp.float32)

    lists = [(kind * (units_max + 1), *sizes) for kind, sizes in enumerate(UNIT_KINDS)]
    for base, width, at_once in lists:

        def some(turn, carry, base=base, width=width, at_once=at_once):
            units = [read(base, turn * at_once + n, width) for n in range(at_once)]
            scores = [scores_of(unit) for unit in units]
            for unit, its_scores in zip(units, scores):
                sums_ref[unit[0]] += weigh(unit, its_scores, highest_ref[unit[0], :1, :])
            return carry

        lax.fori_loop(0, (units_ref[base + units_max] + at_once - 1) // at_once, some, 0)

    def only(base, unit, width, item):
        its, *slots = read(base, unit, width)
        return item, *(jnp.where(its == item, slot, -1) for slot in slots)

    def raise_highest(item, highest):
        for base, width, _ in lists:

            def look(turn, highest, base=base, width=width):
                unit = only(base, turn, width, item)
                scores = scores_of(unit)
                for place, slot in enumerate(unit[1:]):
                    part = scores[place * block_len : (place + 1) * block_len]
                    found = jnp.max(part, axis=0, keepdims=True) * scale
                    highest = jnp.where(slot < 0, highest, jnp.maximum(highest, found))
                return highest

            highest = lax.fori_loop(0, units_ref[base + units_max], look, highest)
        return highest

    def add_again(item, highest):
        for base, width, _ in lists:

            def add(turn, carry, base=base, width=width):
                unit = only(base, turn, width, item)
                sums_ref[item] += weigh(unit, scores_of(unit), highest)
                return carry

            lax.fori_loop(0, units_ref[base + units_max], add, 0)

    return raise_highest, add_again


def unsafe(sums_ref, height):
    totals = sums_ref[:, height : height + 8, :]
    return jnp.max(jnp.where(totals < SAFE_TOTAL, 0.0, 1.0)) > 0.0


def local_kernel(
    units_ref, first_ref, queries_ref, keys_ref, values_ref, clear_ref,
    sums_ref, highest_ref, split_ref,
    key_table, value_table, queries_raw, keys_raw, values_raw, keys_wide, values_wide, mask_ref,
    sems,
    *, blocks, used, kv_heads, block_len, scale, units_max, at_once,
):
    rows = block_len * kv_heads
    query_rows = queries_ref.shape[0] // blocks
    height = value_table.shape[1] // blocks
    head_dim = keys_ref.shape[1]

    def copies(turn):
        found = []
        for kind, (source, raw) in enumerate(
            ((keys_ref, keys_raw), (values_ref, values_raw), (queries_ref, queries_raw))
        ):
            chunk = source.shape[0] // blocks * at_once
            place = pl.ds(pl.multiple_of(turn * chunk, chunk), chunk)
            found.append(pltpu.make_async_copy(source.at[place], raw.at[place], sems.at[kind, turn]))
        return found

    for turn in range(blocks // at_once):
        for copy in copies(turn):
            copy.start()
    mask_ref[...] = causal_mask(mask_ref.shape) + clear_ref[:1, :1]
    ones = jnp.ones((height - head_dim, block_len), jnp.bfloat16)

    def own_scores(item, block, query):
        here = key_table[lax.rem(item, used), block_rows(block, block_len), :]
        return score(here, query) + mask_ref[...]

    def own_sum(item, block, scores, highest):
        weights = jnp.exp2(scores * scale - highest).astype(jnp.bfloat16)
        columns = value_table[lax.rem(item, used), block_rows(block, height), :]
        return jnp.dot(columns, weights, preferred_element_type=jnp.float32)

    def chunk(turn, carry):
        for copy in copies(turn):
            copy.wait()
        todo = []
        for n in range(at_once):
            block = turn * at_once + n
            source = block_rows(block, rows)
            keys_wide[n] = keys_raw[source, :].astype(jnp.float32)
            values_wide[n] = values_raw[source, :].astype(jnp.float32)
            raw = queries_raw[block_rows(block, query_rows), :]
            for head, query in enumerate(split_heads(raw, used)):
                picked = pl.ds(first_ref[0] + head, block_len, stride=kv_heads)
                key_rows = keys_wide[n, picked, :].astype(jnp.bfloat16)
                columns = jnp.concatenate(
                    [values_wide[n, picked, :].T.astype(jnp.bfloat16), ones], axis=0
                )
                key_table[head, block_rows(block, block_len), :] = key_rows
                value_table[head, block_rows(block, height), :] = columns
                query = query.astype(jnp.bfloat16)
                split_ref[block * used + head] = query
                todo.append((block * used + head, query, key_rows, columns))
        scores = [score(k, query) + mask_ref[...] for _, query, k, _ in todo]
        for (item, _, _, columns), its_scores in zip(todo, scores):
            highest = jnp.max(its_scores, axis=0, keepdims=True) * scale
            weights = jnp.exp2(its_scores * scale - highest).astype(jnp.bfloat16)
            highest_ref[item] = jnp.broadcast_to(highest, highest_ref.shape[1:])
            sums_ref[item] = jnp.dot(columns, weights, preferred_element_type=jnp.float32)
        return carry

    lax.fori_loop(0, blocks // at_once, chunk, 0)
    raise_highest, add_again = attend_units(
        units_ref, split_ref, key_table, value_table, highest_ref, sums_ref,
        used=used, block_len=block_len, scale=scale, units_max=units_max,
    )

    @pl.when(unsafe(sums_ref, head_dim))
    def _():
        def mend(item, carry):
            highest = raise_highest(item, highest_ref[item][:1])
            block = item // used
            scores = own_scores(item, block, split_ref[item])
            highest_ref[item] = jnp.broadcast_to(highest, highest_ref.shape[1:])
            sums_ref[item] = own_sum(item, block, scores, highest)
            add_again(item, highest)
            return carry

        lax.fori_loop(0, blocks * used, mend, 0)


def remote_kernel(
    units_ref, split_ref, sums_in, highest_ref, *rest,
    shifts, blocks, used, block_len, scale, units_max, at_once,
):
    parcels, (out_ref, key_table, value_table, sums_ref, staged, sems) = (
        rest[:shifts], rest[shifts:]
    )
    head_dim = out_ref.shape[1]
    height = sums_in.shape[1]
    query_rows = out_ref.shape[0] // blocks
    ones = jnp.ones((height - head_dim, block_len), jnp.bfloat16)

    for shift, parcel in enumerate(parcels):
        for turn in range(REMOTE_BLOCK_MAX):
            at = shift * REMOTE_BLOCK_MAX + turn
            source = slice(turn * block_len, (turn + 1) * block_len)
            for head in range(used):
                key_table[head, at * block_len : (at + 1) * block_len, :] = parcel[0, head, source, :]
                value_table[head, at * height : at * height + head_dim, :] = parcel[
                    1, head, source, :
                ]
                value_table[head, at * height + head_dim : (at + 1) * height, :] = ones

    def take(item, carry):
        sums_ref[item] = sums_in[item]
        return carry

    lax.fori_loop(0, blocks * used, take, 0)
    raise_highest, add_again = attend_units(
        units_ref, split_ref, key_table, value_table, highest_ref, sums_ref,
        used=used, block_len=block_len, scale=scale, units_max=units_max,
    )

    @pl.when(unsafe(sums_ref, head_dim))
    def _():
        def mend(item, carry):
            before = highest_ref[item][:1]
            highest = raise_highest(item, before)
            sums_ref[item] = sums_in[item] * jnp.exp2(before - highest)
            add_again(item, highest)
            return carry

        lax.fori_loop(0, blocks * used, mend, 0)

    rows = at_once * query_rows

    def give(turn):
        slot = lax.rem(turn, 2)
        place = pl.ds(pl.multiple_of(turn * rows, rows), rows)
        return pltpu.make_async_copy(staged.at[slot], out_ref.at[place], sems.at[slot])

    def finish(turn, carry):
        slot = lax.rem(turn, 2)

        @pl.when(turn >= 2)
        def _():
            give(turn - 2).wait()

        for n in range(at_once):
            parts = []
            for head in range(used):
                item = (turn * at_once + n) * used + head
                total = sums_ref[item, head_dim : head_dim + 1, :]
                parts.append((sums_ref[item, :head_dim, :] * (1.0 / total)).T)
            staged[slot, n * query_rows : (n + 1) * query_rows, :] = join_heads(*parts)
        give(turn).start()
        return carry

    turns = blocks // at_once
    lax.fori_loop(0, turns, finish, 0)
    for turn in range(max(0, turns - 2), turns):
        give(turn).wait()


def local_part(units, first, query_rows, key_rows, value_rows, clear, **sizes):
    blocks, used, block_len = sizes["blocks"], sizes["used"], sizes["block_len"]
    at_once = sizes["at_once"]
    head_dim = query_rows.shape[1]
    item_rows = query_rows.shape[0] // (blocks * used)
    kv_heads = key_rows.shape[0] // (blocks * block_len)
    anywhere = pl.BlockSpec(memory_space=pl.ANY)
    in_vmem = pl.BlockSpec(memory_space=pltpu.VMEM)
    wide = pltpu.VMEM((at_once, block_len * kv_heads, head_dim), jnp.float32)
    height = head_dim + ONES_ROWS
    return pl.pallas_call(
        functools.partial(local_kernel, kv_heads=kv_heads, **sizes),
        grid_spec=pltpu.PrefetchScalarGridSpec(
            num_scalar_prefetch=2,
            grid=(1,),
            in_specs=[anywhere, anywhere, anywhere, in_vmem],
            out_specs=[in_vmem] * 3,
            scratch_shapes=[
                pltpu.VMEM((used, blocks * block_len, head_dim), jnp.bfloat16),
                pltpu.VMEM((used, blocks * height, block_len), jnp.bfloat16),
                pltpu.VMEM(query_rows.shape, jnp.bfloat16),
                pltpu.VMEM(key_rows.shape, jnp.bfloat16),
                pltpu.VMEM(key_rows.shape, jnp.bfloat16),
                wide,
                wide,
                pltpu.VMEM((block_len, item_rows), jnp.float32),
                pltpu.SemaphoreType.DMA((3, blocks // at_once)),
            ],
        ),
        out_shape=[
            pltpu.VMEM((blocks * used, height, item_rows), jnp.float32),
            pltpu.VMEM((blocks * used, 8, item_rows), jnp.float32),
            pltpu.VMEM((blocks * used, item_rows, head_dim), jnp.bfloat16),
        ],
        compiler_params=pltpu.CompilerParams(vmem_limit_bytes=LOCAL_VMEM_BYTES),
        cost_estimate=pl.CostEstimate(
            flops=2**34, bytes_accessed=32 * 2**20, transcendentals=2**25
        ),
        name="local_part",
    )(units, first, query_rows, key_rows, value_rows, in_place(clear))


def in_place(array):
    return pltpu.with_memory_space_constraint(array, pltpu.VMEM)


def remote_part(units, states, arrived, out_shape, **sizes):
    sums, highest, split = (in_place(state) for state in states)
    shifts = len(arrived)
    blocks, used, block_len = sizes["blocks"], sizes["used"], sizes["block_len"]
    height = sums.shape[1]
    head_dim = out_shape[1]
    slots = shifts * REMOTE_BLOCK_MAX
    return pl.pallas_call(
        functools.partial(remote_kernel, shifts=shifts, **sizes),
        grid_spec=pltpu.PrefetchScalarGridSpec(
            num_scalar_prefetch=1,
            grid=(1,),
            in_specs=[pl.BlockSpec(memory_space=pltpu.VMEM)] * (3 + shifts),
            out_specs=pl.BlockSpec(memory_space=pl.ANY),
            scratch_shapes=[
                pltpu.VMEM((used, slots * block_len, head_dim), jnp.bfloat16),
                pltpu.VMEM((used, slots * height, block_len), jnp.bfloat16),
                pltpu.VMEM(sums.shape, jnp.float32),
                pltpu.VMEM(
                    (2, sizes["at_once"] * out_shape[0] // blocks, head_dim), jnp.bfloat16
                ),
                pltpu.SemaphoreType.DMA((2,)),
            ],
        ),
        out_shape=jax.ShapeDtypeStruct(out_shape, jnp.bfloat16),
        compiler_params=pltpu.CompilerParams(vmem_limit_bytes=REMOTE_VMEM_BYTES),
        name="remote_part",
    )(units, split, sums, highest, *arrived)


def list_units(open_slots, index, units_max):
    parts, items, picks = index.shape
    ahead = jnp.arange(picks)[:, None] < jnp.arange(picks)[None, :]
    place = jnp.sum(open_slots[..., :, None] & ahead, axis=-2)
    width = -(-picks // WIDEST) * WIDEST
    here = open_slots[..., :, None] & (place[..., :, None] == jnp.arange(width))
    packed = jnp.sum(jnp.where(here, index[..., :, None] + 1, 0), axis=-2)
    groups = packed.reshape(parts, items * (width // WIDEST), WIDEST)
    shifts = jnp.arange(WIDEST - 1, -1, -1, dtype=jnp.int32) * FIELD
    item = jnp.arange(groups.shape[1], dtype=jnp.int32) // (width // WIDEST)
    codes = jnp.sum(groups << shifts, axis=-1) + (item << (WIDEST * FIELD))
    held = jnp.sum(groups > 0, axis=-1)
    narrow = UNIT_KINDS[1][0]
    filled = jnp.stack([held > narrow, (held > 0) & (held <= narrow)], axis=1)
    ahead = jnp.arange(codes.shape[1])[:, None] < jnp.arange(codes.shape[1])[None, :]
    place = jnp.sum(filled[..., :, None] & ahead, axis=-2)
    target = jnp.arange(units_max + 1)
    here = filled[..., :, None] & (place[..., :, None] == target)
    count = jnp.sum(filled, axis=-1, keepdims=True, dtype=jnp.int32)
    listed = jnp.sum(jnp.where(here, codes[:, None, :, None], 0), axis=-2)
    return jnp.where(target == units_max, count, listed).astype(jnp.int32).reshape(parts, -1)


def on_device(queries, keys, values, chosen):
    tokens, query_heads, head_dim = queries.shape
    kv_heads = keys.shape[1]
    blocks, picks = chosen.shape[1:]
    block_len = tokens // blocks
    used = max(1, query_heads // GROUP)
    shards = lax.axis_size("ctx")
    shifts = shards - 1
    position = lax.axis_index("ctx")
    base = position * blocks
    first = lax.axis_index("rep") * query_heads // GROUP
    scale = LOG2E * head_dim**-0.5
    at_once = next(n for n in (4, 3, 2, 1) if blocks % n == 0)
    given_at_once = next(n for n in (6, 4, 3, 2, 1) if blocks % n == 0)
    most = max(at_once for _, at_once in UNIT_KINDS)
    units_max = -(-blocks * used * -(-picks // WIDEST) // most) * most

    lists = lax.dynamic_slice_in_dim(chosen, first, used, 0)
    wanted = jnp.stack(
        [
            lax.ppermute(chosen, "ctx", [(j, j - d) for j in range(d, shards)])
            for d in range(1, shards)
        ]
    )
    wanted = lax.dynamic_slice_in_dim(wanted, first, used, 1)
    within = wanted - base
    mine = (within >= 0) & (within < blocks)
    request = jnp.stack(
        [
            jnp.min(jnp.where(mine, within, blocks - 1), axis=(2, 3)),
            jnp.max(jnp.where(mine, within, 0), axis=(2, 3)),
        ],
        axis=-1,
    )
    first = first.reshape(1)
    query_rows, key_rows, value_rows = (
        pltpu.with_memory_space_constraint(rows.reshape(-1, head_dim), pltpu.HBM)
        for rows in (queries, keys, values)
    )
    *parcels, clear = pack(
        request.reshape(-1), first, key_rows, value_rows, kv_heads, shifts, used, block_len,
        (8, head_dim),
    )
    arrived = [
        lax.ppermute(parcel, "ctx", [(i, i + d) for i in range(shards - d)])
        for d, parcel in zip(range(1, shards), parcels)
    ]

    by_item = jnp.transpose(lists, (1, 0, 2)).reshape(blocks * used, picks)
    local = by_item >= base
    own = base + jnp.arange(blocks * used) // used
    shard_of = by_item // blocks
    from_shard = shard_of[..., None] == jnp.arange(shards)
    lowest = jnp.min(
        jnp.where(from_shard, by_item[..., None], shards * blocks)
        .reshape(blocks, used, picks, shards),
        axis=(0, 2),
    )
    lowest = jnp.tile(lowest, (blocks, 1))[:, None, :]
    is_lowest = jnp.any(from_shard & (by_item[..., None] == lowest), axis=-1)
    remote_index = (position - 1 - shard_of) * REMOTE_BLOCK_MAX + jnp.where(is_lowest, 0, 1)
    units = list_units(
        jnp.stack([local & (by_item != own[:, None]), ~local]),
        jnp.stack([by_item - base, remote_index]),
        units_max,
    )
    sizes = dict(
        blocks=blocks, used=used, block_len=block_len, scale=scale, units_max=units_max
    )
    states = local_part(units[0], first, query_rows, key_rows, value_rows, clear, at_once=at_once, **sizes)
    out = remote_part(units[1], states, arrived, query_rows.shape, at_once=given_at_once, **sizes)
    return out.reshape(tokens, query_heads, head_dim)


def solution(mesh):
    return jax.shard_map(
        on_device,
        mesh=mesh,
        in_specs=(
            P(("groups", "ctx"), ("heads", "rep"), None),
            P(("groups", "ctx"), "heads", None),
            P(("groups", "ctx"), "heads", None),
            P("heads", ("groups", "ctx"), None),
        ),
        out_specs=P(("groups", "ctx"), ("heads", "rep"), None),
        check_vma=False,
    )
```

```python
import functools

import jax
import jax.numpy as jnp
from jax import lax
from jax.experimental import pallas as pl
from jax.experimental.pallas import tpu as pltpu
from jax.sharding import PartitionSpec as P

QUERY_HEADS = 32
KEY_VALUE_HEADS = 8
REMOTE_BLOCK_MAX = 2
GROUP = QUERY_HEADS // KEY_VALUE_HEADS
LOG2E = 1.4426950408889634
MASKED = -1e30
CLOSED = 3e38
SAFE_TOTAL = 2.0**100
PACK_VMEM_BYTES = 24 * 2**20
LOCAL_VMEM_BYTES = 26 * 2**20
REMOTE_VMEM_BYTES = 26 * 2**20
UNIT_KINDS = ((4, 6), (2, 6))
WIDEST = 4
FIELD = 6
ONES_ROWS = 16


def block_rows(index, block_len):
    return pl.ds(pl.multiple_of(index * block_len, block_len), block_len)


def pack_kernel(
    request, keys_ref, values_ref, *rest, shifts, used, kv_heads, block_len
):
    first_ref, outs = rest[0], rest[1 : shifts + 1]
    clear_ref, blocks_ref, wide_ref, sems = rest[shifts + 1 :]
    rows = block_len * kv_heads
    clear_ref[...] = jnp.zeros_like(clear_ref)
    wanted = [
        (shift, head, turn)
        for shift in range(shifts)
        for head in range(used)
        for turn in range(REMOTE_BLOCK_MAX)
    ]
    copies = []
    for at in range(len(wanted)):
        for kind, table in enumerate((keys_ref, values_ref)):
            copies.append(
                pltpu.make_async_copy(
                    table.at[block_rows(request[at], rows)],
                    blocks_ref.at[2 * at + kind],
                    sems.at[2 * at + kind],
                )
            )
    for copy in copies:
        copy.start()
    for at, (shift, head, turn) in enumerate(wanted):
        target = slice(turn * block_len, (turn + 1) * block_len)
        picked = pl.ds(first_ref[0] + head, block_len, stride=kv_heads)
        for kind in range(2):
            place = 2 * at + kind
            copies[place].wait()
            wide_ref[place] = blocks_ref[place].astype(jnp.float32)
            block = wide_ref[place, picked, :]
            outs[shift][kind, head, target, :] = (block.T if kind else block).astype(jnp.bfloat16)


def pack(request, first, keys, values, kv_heads, shifts, used, block_len, row_shape):
    head_dim = keys.shape[-1]
    parcel = (2, used, REMOTE_BLOCK_MAX * block_len, head_dim)
    anywhere = pl.BlockSpec(memory_space=pl.ANY)
    count = 2 * shifts * used * REMOTE_BLOCK_MAX
    rows = block_len * kv_heads
    return pl.pallas_call(
        functools.partial(
            pack_kernel, shifts=shifts, used=used, kv_heads=kv_heads, block_len=block_len
        ),
        grid_spec=pltpu.PrefetchScalarGridSpec(
            num_scalar_prefetch=1,
            grid=(1,),
            in_specs=[anywhere, anywhere, pl.BlockSpec(memory_space=pltpu.SMEM)],
            out_specs=[pl.BlockSpec(memory_space=pltpu.VMEM)] * (shifts + 1),
            scratch_shapes=[
                pltpu.VMEM((count, rows, head_dim), jnp.bfloat16),
                pltpu.VMEM((count, rows, head_dim), jnp.float32),
                pltpu.SemaphoreType.DMA((count,)),
            ],
        ),
        out_shape=[pltpu.VMEM(parcel, jnp.bfloat16)] * shifts
        + [pltpu.VMEM(row_shape, jnp.float32)],
        compiler_params=pltpu.CompilerParams(vmem_limit_bytes=PACK_VMEM_BYTES),
        name="pack",
    )(request, keys, values, first)


def split_heads(rows, used):
    count, head_dim = rows.shape
    wide = rows.astype(jnp.float32)
    if used == 1:
        return (wide,)
    wide = wide.reshape(count // 16, 2, 8, head_dim)
    even, odd = wide[:, 0], wide[:, 1]
    upper = lax.broadcasted_iota(jnp.int32, even.shape, 1) < GROUP
    first = jnp.where(upper, even, pltpu.roll(odd, GROUP, 1))
    second = jnp.where(upper, pltpu.roll(even, GROUP, 1), odd)
    return tuple(part.reshape(count // 2, head_dim) for part in (first, second))


def join_heads(first, *others):
    count, head_dim = first.shape
    if not others:
        return first.astype(jnp.bfloat16)
    (second,) = others
    first = first.reshape(count // 8, 8, head_dim)
    second = second.reshape(count // 8, 8, head_dim)
    upper = lax.broadcasted_iota(jnp.int32, first.shape, 1) < GROUP
    even = jnp.where(upper, first, pltpu.roll(second, GROUP, 1))
    odd = jnp.where(upper, pltpu.roll(first, GROUP, 1), second)
    return jnp.stack([even, odd], axis=1).reshape(count * 2, head_dim).astype(jnp.bfloat16)


def score(key_rows, query):
    return lax.dot_general(
        key_rows, query, (((1,), (1,)), ((), ())), preferred_element_type=jnp.float32
    )


def causal_mask(shape):
    key = lax.broadcasted_iota(jnp.int32, shape, 0)
    token = lax.broadcasted_iota(jnp.int32, shape, 1) // (shape[1] // shape[0])
    return jnp.where(key <= token, 0.0, MASKED)


def attend_units(
    units_ref, queries_ref, keys_ref, values_ref, highest_ref, sums_ref,
    *, used, block_len, scale, units_max,
):
    def read(base, unit, width):
        code = units_ref[base + unit]
        mask = (1 << FIELD) - 1
        slots = [((code >> ((WIDEST - 1 - n) * FIELD)) & mask) - 1 for n in range(width)]
        return code >> (WIDEST * FIELD), *slots

    def rows_of(ref, item, slot):
        height = ref.shape[1] // (keys_ref.shape[1] // block_len)
        return ref[lax.rem(item, used), block_rows(jnp.maximum(slot, 0), height), :]

    def scores_of(unit):
        item, *slots = unit
        rows = jnp.concatenate([rows_of(keys_ref, item, slot) for slot in slots], axis=0)
        return score(rows, queries_ref[item])

    def weigh(unit, scores, highest):
        item, *slots = unit
        parts = []
        for turn, slot in enumerate(slots):
            shift = jnp.where(slot < 0, CLOSED, highest)
            part = scores[turn * block_len : (turn + 1) * block_len]
            parts.append(jnp.exp2(part * scale - shift))
        weights = jnp.concatenate(parts, axis=0).astype(jnp.bfloat16)
        columns = jnp.concatenate([rows_of(values_ref, item, slot) for slot in slots], axis=1)
        return jnp.dot(columns, weights, preferred_element_type=jnp.float32)

    lists = [(kind * (units_max + 1), *sizes) for kind, sizes in enumerate(UNIT_KINDS)]
    for base, width, at_once in lists:

        def some(turn, carry, base=base, width=width, at_once=at_once):
            units = [read(base, turn * at_once + n, width) for n in range(at_once)]
            scores = [scores_of(unit) for unit in units]
            for unit, its_scores in zip(units, scores):
                sums_ref[unit[0]] += weigh(unit, its_scores, highest_ref[unit[0], :1, :])
            return carry

        lax.fori_loop(0, (units_ref[base + units_max] + at_once - 1) // at_once, some, 0)

    def only(base, unit, width, item):
        its, *slots = read(base, unit, width)
        return item, *(jnp.where(its == item, slot, -1) for slot in slots)

    def raise_highest(item, highest):
        for base, width, _ in lists:

            def look(turn, highest, base=base, width=width):
                unit = only(base, turn, width, item)
                scores = scores_of(unit)
                for place, slot in enumerate(unit[1:]):
                    part = scores[place * block_len : (place + 1) * block_len]
                    found = jnp.max(part, axis=0, keepdims=True) * scale
                    highest = jnp.where(slot < 0, highest, jnp.maximum(highest, found))
                return highest

            highest = lax.fori_loop(0, units_ref[base + units_max], look, highest)
        return highest

    def add_again(item, highest):
        for base, width, _ in lists:

            def add(turn, carry, base=base, width=width):
                unit = only(base, turn, width, item)
                sums_ref[item] += weigh(unit, scores_of(unit), highest)
                return carry

            lax.fori_loop(0, units_ref[base + units_max], add, 0)

    return raise_highest, add_again


def unsafe(sums_ref, height):
    totals = sums_ref[:, height : height + 8, :]
    return jnp.max(jnp.where(totals < SAFE_TOTAL, 0.0, 1.0)) > 0.0


def local_kernel(
    units_ref, first_ref, queries_ref, keys_ref, values_ref, clear_ref,
    sums_ref, highest_ref, split_ref,
    key_table, value_table, queries_raw, keys_raw, values_raw, keys_wide, values_wide, mask_ref,
    sems,
    *, blocks, used, kv_heads, block_len, scale, units_max, at_once,
):
    rows = block_len * kv_heads
    query_rows = queries_ref.shape[0] // blocks
    height = value_table.shape[1] // blocks
    head_dim = keys_ref.shape[1]

    def copies(turn):
        found = []
        for kind, (source, raw) in enumerate(
            ((keys_ref, keys_raw), (values_ref, values_raw), (queries_ref, queries_raw))
        ):
            chunk = source.shape[0] // blocks * at_once
            place = pl.ds(pl.multiple_of(turn * chunk, chunk), chunk)
            found.append(pltpu.make_async_copy(source.at[place], raw.at[place], sems.at[kind, turn]))
        return found

    for turn in range(blocks // at_once):
        for copy in copies(turn):
            copy.start()
    mask_ref[...] = causal_mask(mask_ref.shape) + clear_ref[:1, :1]
    ones = jnp.ones((height - head_dim, block_len), jnp.bfloat16)

    def own_scores(item, block, query):
        here = key_table[lax.rem(item, used), block_rows(block, block_len), :]
        return score(here, query) + mask_ref[...]

    def own_sum(item, block, scores, highest):
        weights = jnp.exp2(scores * scale - highest).astype(jnp.bfloat16)
        columns = value_table[lax.rem(item, used), block_rows(block, height), :]
        return jnp.dot(columns, weights, preferred_element_type=jnp.float32)

    def chunk(turn, carry):
        for copy in copies(turn):
            copy.wait()
        todo = []
        for n in range(at_once):
            block = turn * at_once + n
            source = block_rows(block, rows)
            keys_wide[n] = keys_raw[source, :].astype(jnp.float32)
            values_wide[n] = values_raw[source, :].astype(jnp.float32)
            raw = queries_raw[block_rows(block, query_rows), :]
            for head, query in enumerate(split_heads(raw, used)):
                picked = pl.ds(first_ref[0] + head, block_len, stride=kv_heads)
                key_rows = keys_wide[n, picked, :].astype(jnp.bfloat16)
                columns = jnp.concatenate(
                    [values_wide[n, picked, :].T.astype(jnp.bfloat16), ones], axis=0
                )
                key_table[head, block_rows(block, block_len), :] = key_rows
                value_table[head, block_rows(block, height), :] = columns
                query = query.astype(jnp.bfloat16)
                split_ref[block * used + head] = query
                todo.append((block * used + head, query, key_rows, columns))
        scores = [score(k, query) + mask_ref[...] for _, query, k, _ in todo]
        for (item, _, _, columns), its_scores in zip(todo, scores):
            highest = jnp.max(its_scores, axis=0, keepdims=True) * scale
            weights = jnp.exp2(its_scores * scale - highest).astype(jnp.bfloat16)
            highest_ref[item] = jnp.broadcast_to(highest, highest_ref.shape[1:])
            sums_ref[item] = jnp.dot(columns, weights, preferred_element_type=jnp.float32)
        return carry

    lax.fori_loop(0, blocks // at_once, chunk, 0)
    raise_highest, add_again = attend_units(
        units_ref, split_ref, key_table, value_table, highest_ref, sums_ref,
        used=used, block_len=block_len, scale=scale, units_max=units_max,
    )

    @pl.when(unsafe(sums_ref, head_dim))
    def _():
        def mend(item, carry):
            highest = raise_highest(item, highest_ref[item][:1])
            block = item // used
            scores = own_scores(item, block, split_ref[item])
            highest_ref[item] = jnp.broadcast_to(highest, highest_ref.shape[1:])
            sums_ref[item] = own_sum(item, block, scores, highest)
            add_again(item, highest)
            return carry

        lax.fori_loop(0, blocks * used, mend, 0)


def remote_kernel(
    units_ref, split_ref, sums_in, highest_ref, *rest,
    shifts, blocks, used, block_len, scale, units_max, at_once,
):
    parcels, (out_ref, key_table, value_table, sums_ref, staged, sems) = (
        rest[:shifts], rest[shifts:]
    )
    head_dim = out_ref.shape[1]
    height = sums_in.shape[1]
    query_rows = out_ref.shape[0] // blocks
    ones = jnp.ones((height - head_dim, block_len), jnp.bfloat16)

    for shift, parcel in enumerate(parcels):
        for turn in range(REMOTE_BLOCK_MAX):
            at = shift * REMOTE_BLOCK_MAX + turn
            source = slice(turn * block_len, (turn + 1) * block_len)
            for head in range(used):
                key_table[head, at * block_len : (at + 1) * block_len, :] = parcel[0, head, source, :]
                value_table[head, at * height : at * height + head_dim, :] = parcel[
                    1, head, source, :
                ]
                value_table[head, at * height + head_dim : (at + 1) * height, :] = ones

    listed = units_ref[units_max] + units_ref[2 * units_max + 1] > 0
    together = next(n for n in (4, 2, 1) if blocks * used % n == 0)

    def take(turn, carry):
        for n in range(together):
            sums_ref[turn * together + n] = sums_in[turn * together + n]
        return carry

    lax.fori_loop(0, jnp.where(listed, blocks * used // together, 0), take, 0)
    raise_highest, add_again = attend_units(
        units_ref, split_ref, key_table, value_table, highest_ref, sums_ref,
        used=used, block_len=block_len, scale=scale, units_max=units_max,
    )

    @pl.when(listed & unsafe(sums_ref, head_dim))
    def _():
        def mend(item, carry):
            before = highest_ref[item][:1]
            highest = raise_highest(item, before)
            sums_ref[item] = sums_in[item] * jnp.exp2(before - highest)
            add_again(item, highest)
            return carry

        lax.fori_loop(0, blocks * used, mend, 0)

    rows = at_once * query_rows

    def give(turn):
        slot = lax.rem(turn, 2)
        place = pl.ds(pl.multiple_of(turn * rows, rows), rows)
        return pltpu.make_async_copy(staged.at[slot], out_ref.at[place], sems.at[slot])

    def finish(source, turn, carry):
        slot = lax.rem(turn, 2)

        @pl.when(turn >= 2)
        def _():
            give(turn - 2).wait()

        for n in range(at_once):
            parts = []
            for head in range(used):
                item = (turn * at_once + n) * used + head
                total = source[item, head_dim : head_dim + 1, :]
                parts.append((source[item, :head_dim, :] * (1.0 / total)).T)
            staged[slot, n * query_rows : (n + 1) * query_rows, :] = join_heads(*parts)
        give(turn).start()
        return carry

    turns = blocks // at_once
    for here, source in ((listed, sums_ref), (jnp.logical_not(listed), sums_in)):
        lax.fori_loop(
            0, jnp.where(here, turns, 0), functools.partial(finish, source), 0
        )
    for turn in range(max(0, turns - 2), turns):
        give(turn).wait()


def local_part(units, first, query_rows, key_rows, value_rows, clear, **sizes):
    blocks, used, block_len = sizes["blocks"], sizes["used"], sizes["block_len"]
    at_once = sizes["at_once"]
    head_dim = query_rows.shape[1]
    item_rows = query_rows.shape[0] // (blocks * used)
    kv_heads = key_rows.shape[0] // (blocks * block_len)
    anywhere = pl.BlockSpec(memory_space=pl.ANY)
    in_vmem = pl.BlockSpec(memory_space=pltpu.VMEM)
    wide = pltpu.VMEM((at_once, block_len * kv_heads, head_dim), jnp.float32)
    height = head_dim + ONES_ROWS
    return pl.pallas_call(
        functools.partial(local_kernel, kv_heads=kv_heads, **sizes),
        grid_spec=pltpu.PrefetchScalarGridSpec(
            num_scalar_prefetch=2,
            grid=(1,),
            in_specs=[anywhere, anywhere, anywhere, in_vmem],
            out_specs=[in_vmem] * 3,
            scratch_shapes=[
                pltpu.VMEM((used, blocks * block_len, head_dim), jnp.bfloat16),
                pltpu.VMEM((used, blocks * height, block_len), jnp.bfloat16),
                pltpu.VMEM(query_rows.shape, jnp.bfloat16),
                pltpu.VMEM(key_rows.shape, jnp.bfloat16),
                pltpu.VMEM(key_rows.shape, jnp.bfloat16),
                wide,
                wide,
                pltpu.VMEM((block_len, item_rows), jnp.float32),
                pltpu.SemaphoreType.DMA((3, blocks // at_once)),
            ],
        ),
        out_shape=[
            pltpu.VMEM((blocks * used, height, item_rows), jnp.float32),
            pltpu.VMEM((blocks * used, 8, item_rows), jnp.float32),
            pltpu.VMEM((blocks * used, item_rows, head_dim), jnp.bfloat16),
        ],
        compiler_params=pltpu.CompilerParams(vmem_limit_bytes=LOCAL_VMEM_BYTES),
        cost_estimate=pl.CostEstimate(
            flops=2**34, bytes_accessed=32 * 2**20, transcendentals=2**25
        ),
        name="local_part",
    )(units, first, query_rows, key_rows, value_rows, in_place(clear))


def in_place(array):
    return pltpu.with_memory_space_constraint(array, pltpu.VMEM)


def remote_part(units, states, arrived, out_shape, **sizes):
    sums, highest, split = (in_place(state) for state in states)
    shifts = len(arrived)
    blocks, used, block_len = sizes["blocks"], sizes["used"], sizes["block_len"]
    height = sums.shape[1]
    head_dim = out_shape[1]
    slots = shifts * REMOTE_BLOCK_MAX
    return pl.pallas_call(
        functools.partial(remote_kernel, shifts=shifts, **sizes),
        grid_spec=pltpu.PrefetchScalarGridSpec(
            num_scalar_prefetch=1,
            grid=(1,),
            in_specs=[pl.BlockSpec(memory_space=pltpu.VMEM)] * (3 + shifts),
            out_specs=pl.BlockSpec(memory_space=pl.ANY),
            scratch_shapes=[
                pltpu.VMEM((used, slots * block_len, head_dim), jnp.bfloat16),
                pltpu.VMEM((used, slots * height, block_len), jnp.bfloat16),
                pltpu.VMEM(sums.shape, jnp.float32),
                pltpu.VMEM(
                    (2, sizes["at_once"] * out_shape[0] // blocks, head_dim), jnp.bfloat16
                ),
                pltpu.SemaphoreType.DMA((2,)),
            ],
        ),
        out_shape=jax.ShapeDtypeStruct(out_shape, jnp.bfloat16),
        compiler_params=pltpu.CompilerParams(vmem_limit_bytes=REMOTE_VMEM_BYTES),
        name="remote_part",
    )(units, split, sums, highest, *arrived)


def list_units(open_slots, index, units_max):
    parts, items, picks = index.shape
    ahead = jnp.arange(picks)[:, None] < jnp.arange(picks)[None, :]
    place = jnp.sum(open_slots[..., :, None] & ahead, axis=-2)
    width = -(-picks // WIDEST) * WIDEST
    here = open_slots[..., :, None] & (place[..., :, None] == jnp.arange(width))
    packed = jnp.sum(jnp.where(here, index[..., :, None] + 1, 0), axis=-2)
    groups = packed.reshape(parts, items * (width // WIDEST), WIDEST)
    shifts = jnp.arange(WIDEST - 1, -1, -1, dtype=jnp.int32) * FIELD
    item = jnp.arange(groups.shape[1], dtype=jnp.int32) // (width // WIDEST)
    codes = jnp.sum(groups << shifts, axis=-1) + (item << (WIDEST * FIELD))
    held = jnp.sum(groups > 0, axis=-1)
    narrow = UNIT_KINDS[1][0]
    filled = jnp.stack([held > narrow, (held > 0) & (held <= narrow)], axis=1)
    ahead = jnp.arange(codes.shape[1])[:, None] < jnp.arange(codes.shape[1])[None, :]
    place = jnp.sum(filled[..., :, None] & ahead, axis=-2)
    target = jnp.arange(units_max + 1)
    here = filled[..., :, None] & (place[..., :, None] == target)
    count = jnp.sum(filled, axis=-1, keepdims=True, dtype=jnp.int32)
    listed = jnp.sum(jnp.where(here, codes[:, None, :, None], 0), axis=-2)
    return jnp.where(target == units_max, count, listed).astype(jnp.int32).reshape(parts, -1)


def on_device(queries, keys, values, chosen):
    tokens, query_heads, head_dim = queries.shape
    kv_heads = keys.shape[1]
    blocks, picks = chosen.shape[1:]
    block_len = tokens // blocks
    used = max(1, query_heads // GROUP)
    shards = lax.axis_size("ctx")
    shifts = shards - 1
    position = lax.axis_index("ctx")
    base = position * blocks
    first = lax.axis_index("rep") * query_heads // GROUP
    scale = LOG2E * head_dim**-0.5
    at_once = next(n for n in (4, 3, 2, 1) if blocks % n == 0)
    given_at_once = next(n for n in (6, 4, 3, 2, 1) if blocks % n == 0)
    most = max(at_once for _, at_once in UNIT_KINDS)
    units_max = -(-blocks * used * -(-picks // WIDEST) // most) * most

    lists = lax.dynamic_slice_in_dim(chosen, first, used, 0)
    wanted = jnp.stack(
        [
            lax.ppermute(chosen, "ctx", [(j, j - d) for j in range(d, shards)])
            for d in range(1, shards)
        ]
    )
    wanted = lax.dynamic_slice_in_dim(wanted, first, used, 1)
    within = wanted - base
    mine = (within >= 0) & (within < blocks)
    request = jnp.stack(
        [
            jnp.min(jnp.where(mine, within, blocks - 1), axis=(2, 3)),
            jnp.max(jnp.where(mine, within, 0), axis=(2, 3)),
        ],
        axis=-1,
    )
    first = first.reshape(1)
    query_rows, key_rows, value_rows = (
        pltpu.with_memory_space_constraint(rows.reshape(-1, head_dim), pltpu.HBM)
        for rows in (queries, keys, values)
    )
    *parcels, clear = pack(
        request.reshape(-1), first, key_rows, value_rows, kv_heads, shifts, used, block_len,
        (8, head_dim),
    )
    arrived = [
        lax.ppermute(parcel, "ctx", [(i, i + d) for i in range(shards - d)])
        for d, parcel in zip(range(1, shards), parcels)
    ]

    by_item = jnp.transpose(lists, (1, 0, 2)).reshape(blocks * used, picks)
    local = by_item >= base
    own = base + jnp.arange(blocks * used) // used
    shard_of = by_item // blocks
    from_shard = shard_of[..., None] == jnp.arange(shards)
    lowest = jnp.min(
        jnp.where(from_shard, by_item[..., None], shards * blocks)
        .reshape(blocks, used, picks, shards),
        axis=(0, 2),
    )
    lowest = jnp.tile(lowest, (blocks, 1))[:, None, :]
    is_lowest = jnp.any(from_shard & (by_item[..., None] == lowest), axis=-1)
    remote_index = (position - 1 - shard_of) * REMOTE_BLOCK_MAX + jnp.where(is_lowest, 0, 1)
    units = list_units(
        jnp.stack([local & (by_item != own[:, None]), ~local]),
        jnp.stack([by_item - base, remote_index]),
        units_max,
    )
    sizes = dict(
        blocks=blocks, used=used, block_len=block_len, scale=scale, units_max=units_max
    )
    states = local_part(units[0], first, query_rows, key_rows, value_rows, clear, at_once=at_once, **sizes)
    out = remote_part(units[1], states, arrived, query_rows.shape, at_once=given_at_once, **sizes)
    return out.reshape(tokens, query_heads, head_dim)


def solution(mesh):
    return jax.shard_map(
        on_device,
        mesh=mesh,
        in_specs=(
            P(("groups", "ctx"), ("heads", "rep"), None),
            P(("groups", "ctx"), "heads", None),
            P(("groups", "ctx"), "heads", None),
            P("heads", ("groups", "ctx"), None),
        ),
        out_specs=P(("groups", "ctx"), ("heads", "rep"), None),
        check_vma=False,
    )
```
